128 devices in a mesh: wide: 32 (over y, z, core), narrow: 4 (over x).
Axes of the slice: x: 4, y: 4, z: 4, core: 2. Of those that a mesh axis runs over, the one named last changes fastest.
Arguments:
- coefficients: float32 [16, 256, 32, 128], P('narrow', 'wide'), may hold values from -6 to 6
- observed: float32 [16, 256, 32, 128], P('narrow', 'wide'), may hold values from -6 to 6
- blocks: bfloat16 [4, 32, 128, 128, 128], P('narrow', 'wide'), may hold values from -0.3125 to 0.3125
- block_rows: int32 [4, 32, 128], P('narrow', 'wide'), may hold values from 0 to 31
- block_cols: int32 [4, 32, 128], P('narrow', 'wide'), may hold values from 0 to 59, as said below
- live_count: int32 [4, 32], P('narrow', 'wide'), may hold values from 1 to 128, as said below
Outputs:
- updated: float32 [16, 256, 32, 128], P('narrow', 'wide')
- residual: float32 [16, 256, 32, 128], P('narrow', 'wide')
The draws below stay inside these ranges and needn't reach their ends.
Inputs may be any that keep to these rules, and one draw needn't show every extreme that they name: block_cols of a slot lies in the 3 x 3 neighbourhood of its block_rows position: with r = block_rows, c // 10 - r // 8 and c % 10 - r % 8 are each 0, 1 or 2. `live_count`: at least one tile uses all 128 slots.
All inputs are finite; a program needn't handle non-finite values.
Results may differ from the reference program's by a relative error of at most 0.0065.
Values may be sent and summed in bfloat16 or wider, within the bound.
No kernel may reach another device: no remote copies, remote signals or barrier semaphores. Data moves between devices by JAX's collectives and lax.ppermute only.
A program may use at most 64 MiB of HBM per device.

```python
import jax
import jax.numpy as jnp
from jax import lax

P_SIZE = 128
FRAMES = 32
TBX = 4
TBY = 8
SLOTS = 128
ITERS = 5
NTX = 4
NTY = 32
GX = 16
GY = 256


def slot_plan(key):
    row_ids = jax.random.randint(jax.random.fold_in(key, 11), (NTX, NTY, SLOTS), 0, TBX * TBY, dtype=jnp.int32)
    offsets = jax.random.randint(jax.random.fold_in(key, 12), (NTX, NTY, SLOTS), 0, 9, dtype=jnp.int32)
    col_ids = (row_ids // TBY + offsets // 3) * (TBY + 2) + row_ids % TBY + offsets % 3
    return (row_ids, col_ids)


def draw_block_rows(key, part):
    row_ids, col_ids = slot_plan(key)
    return row_ids


def draw_block_cols(key, part):
    row_ids, col_ids = slot_plan(key)
    return col_ids


def draw_live_count(key, part):
    key = jax.random.fold_in(key, 3)
    lowest = max(SLOTS // 8, 1)
    counts = jax.random.randint(jax.random.fold_in(key, 1), (NTX * NTY,), lowest, SLOTS // 2 + 1, dtype=jnp.int32)
    chosen = jax.random.randint(jax.random.fold_in(key, 2), (), 0, NTX * NTY, dtype=jnp.int32)
    counts = counts.at[chosen].set(SLOTS)
    return counts.reshape(NTX, NTY)


def block_scale(rng, dims, shards, least, high):
    level = 1.0
    for position, blocks in shards:
        heights = jax.random.uniform(jax.random.fold_in(jax.random.fold_in(rng, 6), position), (blocks,), jnp.float32, least / len(shards), high / len(shards))
        level = level * jnp.repeat(jnp.exp(heights), dims[position] // blocks).reshape((-1,) + (1,) * (len(dims) - 1 - position))
    return level


def scatter_about(rng, extent, width, limit, cuts=(), kind=jnp.bfloat16):
    result = width * jax.random.normal(rng, extent, jnp.float32)
    if cuts:
        result = result * block_scale(rng, extent, cuts, -0.22, 0.18)
    return jnp.clip(result, -limit, limit).astype(kind)


def setup_inputs(seed: int = 0) -> dict:
    key_list = jax.random.split(jax.random.key(seed), 7)
    return {
        "coefficients": scatter_about(key_list[0], (GX, GY, FRAMES, P_SIZE), 1.0, 6.0, ((0, 4), (1, 32)), jnp.float32),
        "observed": scatter_about(key_list[1], (GX, GY, FRAMES, P_SIZE), 1.0, 6.0, ((0, 4), (1, 32)), jnp.float32),
        "blocks": scatter_about(key_list[2], (NTX, NTY, SLOTS, P_SIZE, P_SIZE), (3 * P_SIZE) ** -0.5, 0.3125, ((0, 4), (1, 32))),
        "block_rows": draw_block_rows(jax.random.fold_in(key_list[6], 71), 0),
        "block_cols": draw_block_cols(jax.random.fold_in(key_list[6], 71), 0),
        "live_count": draw_live_count(jax.random.fold_in(key_list[6], 71), 0),
    }


descent = 0.1


def tile_products(source, matrices, gather_ids, scatter_ids, live_slots, segments, pattern):
    taken = source[gather_ids].astype(jnp.float32)
    products = jnp.einsum(pattern, taken, matrices.astype(jnp.float32))
    live_mask = (jnp.arange(SLOTS, dtype=jnp.int32) < live_slots).astype(jnp.float32)[:, None, None]
    return jax.ops.segment_sum(products * live_mask, scatter_ids, num_segments=segments)


def reference(coefficients, observed, blocks, block_rows, block_cols, live_count):
    tile_total = NTX * NTY
    flat_blocks = blocks.reshape(tile_total, SLOTS, P_SIZE, P_SIZE)
    row_ids = block_rows.reshape(tile_total, SLOTS)
    col_ids = block_cols.reshape(tile_total, SLOTS)
    counts = live_count.reshape(tile_total)
    tile_order = jnp.arange(tile_total, dtype=jnp.int32)
    extended_total = (TBX + 2) * (TBY + 2)
    residual = jnp.zeros_like(observed)
    for iteration in range(ITERS):
        low = coefficients.astype(jnp.bfloat16)
        padded = jnp.pad(low, ((1, 1), (1, 1), (0, 0), (0, 0)))

        def forward(tile_index):
            tile_row = tile_index // NTY
            tile_col = tile_index % NTY
            zero_index = jnp.int32(0)
            extended = lax.dynamic_slice(padded, (tile_row * TBX, tile_col * TBY, zero_index, zero_index), (TBX + 2, TBY + 2, FRAMES, P_SIZE))
            extended = extended.reshape(extended_total, FRAMES, P_SIZE)
            return tile_products(extended, flat_blocks[tile_index], col_ids[tile_index], row_ids[tile_index], counts[tile_index], TBX * TBY, 'sfp,spq->sfq')

        predicted = lax.map(forward, tile_order)
        predicted = predicted.reshape(NTX, NTY, TBX, TBY, FRAMES, P_SIZE).transpose(0, 2, 1, 3, 4, 5).reshape(GX, GY, FRAMES, P_SIZE)
        residual = predicted - observed
        residual_low = residual.astype(jnp.bfloat16)
        residual_tiles = residual_low.reshape(NTX, TBX, NTY, TBY, FRAMES, P_SIZE).transpose(0, 2, 1, 3, 4, 5).reshape(tile_total, TBX * TBY, FRAMES, P_SIZE)

        def adjoint(accumulated, tile_index):
            tile_row = tile_index // NTY
            tile_col = tile_index % NTY
            zero_index = jnp.int32(0)
            contrib = tile_products(residual_tiles[tile_index], flat_blocks[tile_index], row_ids[tile_index], col_ids[tile_index], counts[tile_index], extended_total, 'sfq,spq->sfp')
            contrib = contrib.reshape(TBX + 2, TBY + 2, FRAMES, P_SIZE)
            corner = (tile_row * TBX, tile_col * TBY, zero_index, zero_index)
            current = lax.dynamic_slice(accumulated, corner, (TBX + 2, TBY + 2, FRAMES, P_SIZE))
            return lax.dynamic_update_slice(accumulated, current + contrib, corner), None

        accumulated, unused = lax.scan(adjoint, jnp.zeros((GX + 2, GY + 2, FRAMES, P_SIZE), jnp.float32), tile_order)
        gradient = accumulated[1:-1, 1:-1]
        coefficients = coefficients - descent * gradient
    return coefficients, residual
```

```python
import functools

import jax
import jax.numpy as jnp
from jax import lax
from jax.experimental import pallas as pl
from jax.experimental.pallas import tpu as pltpu
from jax.sharding import PartitionSpec as P

ITERS = 5
descent = 0.1
NN = (((1,), (0,)), ((), ()))
NT = (((1,), (1,)), ((), ()))

ROW_FIRST, ROW_LAST, COL_FIRST, COL_LAST, EVEN = range(5)


def cast_low(value):
    return value.astype(jnp.bfloat16)


def wide_value(value):
    return value.astype(jnp.float32)


def kept(value, drop):
    return jnp.where(drop, jnp.zeros_like(value), value)


def half_step(source_ref, blocks_ref, total_ref, source_ids, target_ids, slots, dims):
    for slot in range(slots):
        product = lax.dot_general(
            source_ref[source_ids[slot]],
            blocks_ref[slot],
            dims,
            preferred_element_type=jnp.float32,
        )
        target = target_ids[slot]
        total_ref[target] = total_ref[target] + product


def products(sizes, info_ref, rows_ref, cols_ref, observed_ref, blocks_ref, next_ref, grad_ref, residual_ref, low_ref, rlow_ref):
    tile_x, tile_y, slots = sizes
    own = tile_x * tile_y
    extended = (tile_x + 2) * (tile_y + 2)
    low_ref[extended] = jnp.zeros_like(low_ref[extended])
    for block in range(own):
        residual_ref[block] = -observed_ref[block]
    residual_ref[own] = jnp.zeros_like(residual_ref[own])
    half_step(low_ref, blocks_ref, residual_ref, cols_ref, rows_ref, slots, NN)
    for block in range(own + 1):
        rlow_ref[block] = cast_low(residual_ref[block])
    for block in range(extended + 1):
        grad_ref[block] = jnp.zeros_like(grad_ref[block])
    half_step(rlow_ref, blocks_ref, grad_ref, rows_ref, cols_ref, slots, NT)


def send_columns(sizes, last, info_ref, grad_ref, pair_ref, next_ref):
    tile_x, tile_y, _ = sizes
    span = tile_y + 2
    even = info_ref[EVEN] == 1
    for out_ref, right in ((pair_ref, even), (next_ref, jnp.logical_not(even))):
        if last:
            col = jnp.where(right, span - 1, 0)
            for row in range(tile_x + 2):
                out_ref[row] = cast_low(grad_ref[row * span + col])
        else:
            col = jnp.where(right, span - 2, 0)
            for row in range(tile_x + 2):
                for step in range(2):
                    out_ref[row * 2 + step] = cast_low(grad_ref[row * span + col + step])


def outside(sizes, info_ref, row, col):
    tile_x, tile_y, _ = sizes
    flag = None
    for hit, place in (
        (row == 0, ROW_FIRST),
        (row == tile_x + 1, ROW_LAST),
        (col == 0, COL_FIRST),
        (col == tile_y + 1, COL_LAST),
    ):
        if hit:
            here = info_ref[place] == 1
            flag = here if flag is None else jnp.logical_or(flag, here)
    return flag


def first_kernel(sizes, last, info_ref, rows_ref, cols_ref, coef_ref, above_ref, below_ref, pair_in, next_in, observed_ref, blocks_ref, x_ref, grad_ref, residual_ref, pair_ref, next_ref, low_ref, rlow_ref):
    tile_x, tile_y, _ = sizes
    span = tile_y + 2
    even = info_ref[EVEN] == 1
    for row in range(tile_x + 2):
        for col in range(span):
            if col == 0:
                value = jnp.where(even, wide_value(next_in[row]), wide_value(pair_in[row]))
            elif col == tile_y + 1:
                value = jnp.where(even, wide_value(pair_in[row]), wide_value(next_in[row]))
            elif row == 0:
                value = wide_value(above_ref[col - 1])
            elif row == tile_x + 1:
                value = wide_value(below_ref[col - 1])
            else:
                value = coef_ref[(row - 1) * tile_y + col - 1]
            drop = outside(sizes, info_ref, row, col)
            if drop is not None:
                value = kept(value, drop)
            x_ref[row * span + col] = value
            low_ref[row * span + col] = cast_low(value)
    products(sizes, info_ref, rows_ref, cols_ref, observed_ref, blocks_ref, None, grad_ref, residual_ref, low_ref, rlow_ref)
    send_columns(sizes, last, info_ref, grad_ref, pair_ref, next_ref)


def step_kernel(sizes, last, info_ref, rows_ref, cols_ref, x_in, grad_in, above_ref, below_ref, observed_ref, blocks_ref, x_ref, grad_ref, residual_ref, pair_ref, next_ref, low_ref, rlow_ref):
    tile_x, tile_y, _ = sizes
    span = tile_y + 2
    first = info_ref[ROW_FIRST] == 1
    final = info_ref[ROW_LAST] == 1
    for row in range(tile_x + 2):
        for col in range(span):
            at = row * span + col
            gradient = grad_in[at]
            if row < 2:
                gradient = gradient + kept(wide_value(above_ref[row * span + col]), first)
            elif row >= tile_x:
                gradient = gradient + kept(wide_value(below_ref[(row - tile_x) * span + col]), final)
            value = x_in[at] - descent * gradient
            drop = outside(sizes, info_ref, row, col)
            if drop is not None:
                value = kept(value, drop)
            x_ref[at] = value
            low_ref[at] = cast_low(value)
    products(sizes, info_ref, rows_ref, cols_ref, observed_ref, blocks_ref, None, grad_ref, residual_ref, low_ref, rlow_ref)
    send_columns(sizes, last, info_ref, grad_ref, pair_ref, next_ref)


def fold_kernel(sizes, last, info_ref, grad_in, pair_in, next_in, grad_ref, up_ref, down_ref):
    tile_x, tile_y, _ = sizes
    span = tile_y + 2
    even = info_ref[EVEN] == 1
    width = 1 if last else 2
    lefts = {1: 0} if last else {0: 0, 1: 1}
    rights = {tile_y: 0} if last else {tile_y: 0, tile_y + 1: 1}
    for row in range(tile_x + 2):
        for col in range(span):
            at = row * span + col
            value = grad_in[at]
            for places, from_pair, place in (
                (lefts, jnp.logical_not(even), COL_FIRST),
                (rights, even, COL_LAST),
            ):
                if col in places:
                    where = row * width + places[col]
                    came = jnp.where(from_pair, wide_value(pair_in[where]), wide_value(next_in[where]))
                    value = value + kept(came, info_ref[place] == 1)
            grad_ref[at] = value
            if last:
                if 1 <= col <= tile_y:
                    if row == 0:
                        up_ref[col - 1] = cast_low(value)
                    if row == tile_x + 1:
                        down_ref[col - 1] = cast_low(value)
            else:
                if row < 2:
                    up_ref[row * span + col] = cast_low(value)
                if row >= tile_x:
                    down_ref[(row - tile_x) * span + col] = cast_low(value)


def final_kernel(sizes, info_ref, x_in, grad_in, above_ref, below_ref, out_ref):
    tile_x, tile_y, _ = sizes
    span = tile_y + 2
    first = info_ref[ROW_FIRST] == 1
    final = info_ref[ROW_LAST] == 1
    for row in range(1, tile_x + 1):
        for col in range(1, tile_y + 1):
            at = row * span + col
            gradient = grad_in[at]
            if row == 1:
                gradient = gradient + kept(wide_value(above_ref[col - 1]), first)
            if row == tile_x:
                gradient = gradient + kept(wide_value(below_ref[col - 1]), final)
            out_ref[(row - 1) * tile_y + col - 1] = x_in[at] - descent * gradient


def local(coefficients, observed, blocks, block_rows, block_cols, live_count):
    tile_x, tile_y, frames, width = coefficients.shape
    slots = blocks.shape[2]
    own = tile_x * tile_y
    span = tile_y + 2
    extended = (tile_x + 2) * span
    sizes = (tile_x, tile_y, slots)
    narrow = lax.axis_size("narrow")
    wide = lax.axis_size("wide")
    a = lax.axis_index("narrow")
    b = lax.axis_index("wide")
    info = jnp.stack([a == 0, a == narrow - 1, b == 0, b == wide - 1, b % 2 == 0]).astype(jnp.int32)
    even = b % 2 == 0

    up_ring = [(i, (i - 1) % narrow) for i in range(narrow)]
    down_ring = [(i, (i + 1) % narrow) for i in range(narrow)]
    pairs = [(i, i ^ 1) for i in range(wide)]
    others = [(i, ((i - 1) ^ 1) + 1) for i in range(1, wide - 1)] + [(0, wide - 1), (wide - 1, 0)]

    def along_narrow(up, down):
        return lax.ppermute(down, "narrow", down_ring), lax.ppermute(up, "narrow", up_ring)

    def along_wide(pair, other):
        return lax.ppermute(pair, "wide", pairs), lax.ppermute(other, "wide", others)

    matrices = blocks.reshape(slots, width, width)
    live = jnp.arange(slots, dtype=jnp.int32) < live_count.reshape(())
    row_ids = jnp.where(live, block_rows.reshape(slots), own)
    col_ids = jnp.where(live, block_cols.reshape(slots), extended)
    seen = observed.reshape(own, frames, width)

    smem = pl.BlockSpec(memory_space=pltpu.SMEM)
    vmem = pl.BlockSpec(memory_space=pltpu.VMEM)

    def shape(count, kind):
        return jax.ShapeDtypeStruct((count, frames, width), kind)

    params = pltpu.CompilerParams(vmem_limit_bytes=24 << 20)
    scratch = [
        pltpu.VMEM((extended + 1, frames, width), jnp.bfloat16),
        pltpu.VMEM((own + 1, frames, width), jnp.bfloat16),
    ]

    def step_call(kernel, last, inputs, name):
        sent = tile_x + 2 if last else 2 * (tile_x + 2)
        return pl.pallas_call(
            functools.partial(kernel, sizes, last),
            out_shape=[
                shape(extended, jnp.float32),
                shape(extended + 1, jnp.float32),
                shape(own + 1, jnp.float32),
                shape(sent, jnp.bfloat16),
                shape(sent, jnp.bfloat16),
            ],
            in_specs=[smem] * 3 + [vmem] * (len(inputs) - 3),
            out_specs=[vmem] * 5,
            scratch_shapes=scratch,
            compiler_params=params,
            name=name,
        )(*inputs)

    start = cast_low(coefficients)
    above, below = along_narrow(start[0], start[tile_x - 1])
    sides = []
    for col in (0, tile_y - 1):
        sides.append(
            jnp.concatenate([above[col : col + 1], start[:, col], below[col : col + 1]], axis=0)
        )
    pair_in, next_in = along_wide(
        jnp.where(even, sides[1], sides[0]), jnp.where(even, sides[0], sides[1])
    )
    x, grad, residual, pair_out, next_out = step_call(
        first_kernel,
        False,
        [info, row_ids, col_ids, coefficients.reshape(own, frames, width), above, below, pair_in, next_in, seen, matrices],
        "first_step",
    )
    for iteration in range(ITERS):
        last = iteration == ITERS - 1
        pair_in, next_in = along_wide(pair_out, next_out)
        rows_sent = tile_y if last else 2 * span
        grad, up, down = pl.pallas_call(
            functools.partial(fold_kernel, sizes, last),
            out_shape=[
                shape(extended, jnp.float32),
                shape(rows_sent, jnp.bfloat16),
                shape(rows_sent, jnp.bfloat16),
            ],
            in_specs=[smem] + [vmem] * 3,
            out_specs=[vmem] * 3,
            compiler_params=params,
            name="fold_columns",
        )(info, grad, pair_in, next_in)
        above, below = along_narrow(up, down)
        if last:
            updated = pl.pallas_call(
                functools.partial(final_kernel, sizes),
                out_shape=shape(own, jnp.float32),
                in_specs=[smem] + [vmem] * 4,
                out_specs=vmem,
                compiler_params=params,
                name="final_update",
            )(info, x, grad, above, below)
        else:
            x, grad, residual, pair_out, next_out = step_call(
                step_kernel,
                iteration == ITERS - 2,
                [info, row_ids, col_ids, x, grad, above, below, seen, matrices],
                "one_step",
            )
    return (
        updated.reshape(coefficients.shape),
        residual[:own].reshape(coefficients.shape),
    )


def solution(mesh):
    placed = (
        P("narrow", "wide", None, None),
        P("narrow", "wide", None, None),
        P("narrow", "wide", None, None, None),
        P("narrow", "wide", None),
        P("narrow", "wide", None),
        P("narrow", "wide"),
    )
    return jax.shard_map(
        local,
        mesh=mesh,
        in_specs=placed,
        out_specs=(P("narrow", "wide", None, None), P("narrow", "wide", None, None)),
        check_vma=False,
    )
```

```python
import functools

import jax
import jax.numpy as jnp
from jax import lax
from jax.experimental import pallas as pl
from jax.experimental.pallas import tpu as pltpu
from jax.sharding import PartitionSpec as P

ITERS = 5
descent = 0.1

ROW_FIRST, ROW_LAST, COL_FIRST, COL_LAST, EVEN = range(5)


def cast_low(value):
    return value.astype(jnp.bfloat16)


def wide_value(value):
    return value.astype(jnp.float32)


def kept(value, drop):
    return jnp.where(drop, jnp.zeros_like(value), value)


def half_step(source_ref, blocks_ref, total_ref, source_ids, target_ids, slots):
    for slot in range(slots):
        product = jnp.dot(
            source_ref[source_ids[slot]], blocks_ref[slot], preferred_element_type=jnp.float32
        )
        target = target_ids[slot]
        total_ref[target] = total_ref[target] + product


def products(sizes, rows_ref, cols_ref, observed_ref, blocks_ref, turned_ref, grad_ref, residual_ref, low_ref, rlow_ref):
    tile_x, tile_y, slots = sizes
    own = tile_x * tile_y
    extended = (tile_x + 2) * (tile_y + 2)
    low_ref[extended] = jnp.zeros_like(low_ref[extended])
    for block in range(own):
        residual_ref[block] = -observed_ref[block]
    residual_ref[own] = jnp.zeros_like(residual_ref[own])
    half_step(low_ref, blocks_ref, residual_ref, cols_ref, rows_ref, slots)
    for block in range(own + 1):
        rlow_ref[block] = cast_low(residual_ref[block])
    for block in range(extended + 1):
        grad_ref[block] = jnp.zeros_like(grad_ref[block])
    half_step(rlow_ref, turned_ref, grad_ref, rows_ref, cols_ref, slots)


def send_columns(sizes, last, info_ref, grad_ref, pair_ref, next_ref):
    tile_x, tile_y, _ = sizes
    span = tile_y + 2
    even = info_ref[EVEN] == 1
    for out_ref, right in ((pair_ref, even), (next_ref, jnp.logical_not(even))):
        if last:
            col = jnp.where(right, span - 1, 0)
            for row in range(tile_x + 2):
                out_ref[row] = cast_low(grad_ref[row * span + col])
        else:
            col = jnp.where(right, span - 2, 0)
            for row in range(tile_x + 2):
                for step in range(2):
                    out_ref[row * 2 + step] = cast_low(grad_ref[row * span + col + step])


def outside(sizes, info_ref, row, col):
    tile_x, tile_y, _ = sizes
    flag = None
    for hit, place in (
        (row == 0, ROW_FIRST),
        (row == tile_x + 1, ROW_LAST),
        (col == 0, COL_FIRST),
        (col == tile_y + 1, COL_LAST),
    ):
        if hit:
            here = info_ref[place] == 1
            flag = here if flag is None else jnp.logical_or(flag, here)
    return flag


def came_along_wide(sizes, last, info_ref, pair_in, next_in, row, col):
    tile_x, tile_y, _ = sizes
    even = info_ref[EVEN] == 1
    width = 1 if last else 2
    lefts = {1: 0} if last else {0: 0, 1: 1}
    rights = {tile_y: 0} if last else {tile_y: 0, tile_y + 1: 1}
    for places, from_pair, place in (
        (lefts, jnp.logical_not(even), COL_FIRST),
        (rights, even, COL_LAST),
    ):
        if col in places:
            at = row * width + places[col]
            came = jnp.where(from_pair, pair_in[at], next_in[at])
            return kept(wide_value(came), info_ref[place] == 1)
    return None


def turn_kernel(group, blocks_ref, turned_ref):
    def turn(step, carry):
        for place in range(group):
            slot = step * group + place
            turned_ref[slot] = blocks_ref[slot].T
        return carry

    lax.fori_loop(0, blocks_ref.shape[0] // group, turn, 0)


def first_kernel(sizes, info_ref, rows_ref, cols_ref, coef_ref, above_ref, below_ref, pair_in, next_in, observed_ref, blocks_ref, turned_ref, x_ref, grad_ref, pair_ref, next_ref, low_ref, rlow_ref, residual_ref):
    tile_x, tile_y, _ = sizes
    span = tile_y + 2
    even = info_ref[EVEN] == 1
    for row in range(tile_x + 2):
        for col in range(span):
            if col == 0:
                value = wide_value(jnp.where(even, next_in[row], pair_in[row]))
            elif col == tile_y + 1:
                value = wide_value(jnp.where(even, pair_in[row], next_in[row]))
            elif row == 0:
                value = wide_value(above_ref[col - 1])
            elif row == tile_x + 1:
                value = wide_value(below_ref[col - 1])
            else:
                value = coef_ref[(row - 1) * tile_y + col - 1]
            drop = outside(sizes, info_ref, row, col)
            if drop is not None:
                value = kept(value, drop)
            x_ref[row * span + col] = value
            low_ref[row * span + col] = cast_low(value)
    products(sizes, rows_ref, cols_ref, observed_ref, blocks_ref, turned_ref, grad_ref, residual_ref, low_ref, rlow_ref)
    send_columns(sizes, False, info_ref, grad_ref, pair_ref, next_ref)


def step_kernel(sizes, last, info_ref, rows_ref, cols_ref, x_in, grad_in, pair_in, next_in, above_ref, below_ref, observed_ref, blocks_ref, turned_ref, x_ref, grad_ref, pair_ref, next_ref, *rest):
    tile_x, tile_y, _ = sizes
    span = tile_y + 2
    if last:
        residual_ref, low_ref, rlow_ref = rest
    else:
        low_ref, rlow_ref, residual_ref = rest
    first = info_ref[ROW_FIRST] == 1
    final = info_ref[ROW_LAST] == 1
    for row in range(tile_x + 2):
        for col in range(span):
            at = row * span + col
            gradient = grad_in[at]
            came = came_along_wide(sizes, False, info_ref, pair_in, next_in, row, col)
            if came is not None:
                gradient = gradient + came
            if row < 2:
                gradient = gradient + wide_value(kept(above_ref[row * span + col], first))
            elif row >= tile_x:
                gradient = gradient + wide_value(kept(below_ref[(row - tile_x) * span + col], final))
            value = x_in[at] - descent * gradient
            drop = outside(sizes, info_ref, row, col)
            if drop is not None:
                value = kept(value, drop)
            x_ref[at] = value
            low_ref[at] = cast_low(value)
    products(sizes, rows_ref, cols_ref, observed_ref, blocks_ref, turned_ref, grad_ref, residual_ref, low_ref, rlow_ref)
    send_columns(sizes, last, info_ref, grad_ref, pair_ref, next_ref)


def fold_kernel(sizes, last, info_ref, grad_in, pair_in, next_in, up_ref, down_ref):
    tile_x, tile_y, _ = sizes
    span = tile_y + 2

    def folded(row, col):
        value = grad_in[row * span + col]
        came = came_along_wide(sizes, last, info_ref, pair_in, next_in, row, col)
        return cast_low(value if came is None else value + came)

    if last:
        for col in range(1, tile_y + 1):
            up_ref[col - 1] = folded(0, col)
            down_ref[col - 1] = folded(tile_x + 1, col)
    else:
        for row in range(2):
            for col in range(span):
                up_ref[row * span + col] = folded(row, col)
                down_ref[row * span + col] = folded(tile_x + row, col)


def final_kernel(sizes, info_ref, x_in, grad_in, pair_in, next_in, above_ref, below_ref, out_ref):
    tile_x, tile_y, _ = sizes
    span = tile_y + 2
    first = info_ref[ROW_FIRST] == 1
    final = info_ref[ROW_LAST] == 1
    for row in range(1, tile_x + 1):
        for col in range(1, tile_y + 1):
            at = row * span + col
            gradient = grad_in[at]
            came = came_along_wide(sizes, True, info_ref, pair_in, next_in, row, col)
            if came is not None:
                gradient = gradient + came
            if row == 1:
                gradient = gradient + wide_value(kept(above_ref[col - 1], first))
            if row == tile_x:
                gradient = gradient + wide_value(kept(below_ref[col - 1], final))
            out_ref[(row - 1) * tile_y + col - 1] = x_in[at] - descent * gradient


def local(coefficients, observed, blocks, block_rows, block_cols, live_count):
    tile_x, tile_y, frames, width = coefficients.shape
    slots = blocks.shape[2]
    own = tile_x * tile_y
    span = tile_y + 2
    extended = (tile_x + 2) * span
    sizes = (tile_x, tile_y, slots)
    narrow = lax.axis_size("narrow")
    wide = lax.axis_size("wide")
    a = lax.axis_index("narrow")
    b = lax.axis_index("wide")
    info = jnp.stack([a == 0, a == narrow - 1, b == 0, b == wide - 1, b % 2 == 0]).astype(jnp.int32)
    even = b % 2 == 0

    up_ring = [(i, (i - 1) % narrow) for i in range(narrow)]
    down_ring = [(i, (i + 1) % narrow) for i in range(narrow)]
    pairs = [(i, i ^ 1) for i in range(wide)]
    others = [(i, ((i - 1) ^ 1) + 1) for i in range(1, wide - 1)] + [(0, 0), (wide - 1, wide - 1)]

    def along_narrow(up, down):
        return lax.ppermute(down, "narrow", down_ring), lax.ppermute(up, "narrow", up_ring)

    def along_wide(pair, other):
        return lax.ppermute(pair, "wide", pairs), lax.ppermute(other, "wide", others)

    matrices = blocks.reshape(slots, width, width)
    live = jnp.arange(slots, dtype=jnp.int32) < live_count.reshape(())
    row_ids = jnp.where(live, block_rows.reshape(slots), own)
    col_ids = jnp.where(live, block_cols.reshape(slots), extended)
    seen = observed.reshape(own, frames, width)

    smem = pl.BlockSpec(memory_space=pltpu.SMEM)
    vmem = pl.BlockSpec(memory_space=pltpu.VMEM)

    def shape(count, kind):
        return jax.ShapeDtypeStruct((count, frames, width), kind)

    def call(kernel, name, inputs, scalars, outputs, scratch=(), flops=0):
        return pl.pallas_call(
            kernel,
            out_shape=outputs,
            in_specs=[smem] * scalars + [vmem] * (len(inputs) - scalars),
            out_specs=jax.tree.map(lambda _: vmem, outputs),
            scratch_shapes=list(scratch),
            compiler_params=pltpu.CompilerParams(vmem_limit_bytes=24 << 20),
            cost_estimate=pl.CostEstimate(flops=flops, bytes_accessed=1 << 20, transcendentals=0),
            name=name,
        )(*inputs)

    low_scratch = pltpu.VMEM((extended + 1, frames, width), jnp.bfloat16)
    rlow_scratch = pltpu.VMEM((own + 1, frames, width), jnp.bfloat16)
    residual_scratch = pltpu.VMEM((own + 1, frames, width), jnp.float32)
    work = 4 * slots * frames * width * width

    def step_outputs(last):
        sent = tile_x + 2 if last else 2 * (tile_x + 2)
        outputs = [
            shape(extended, jnp.float32),
            shape(extended + 1, jnp.float32),
            shape(sent, jnp.bfloat16),
            shape(sent, jnp.bfloat16),
        ]
        return outputs + [shape(own + 1, jnp.float32)] if last else outputs

    above, below = along_narrow(cast_low(coefficients[0]), cast_low(coefficients[tile_x - 1]))
    turned = call(
        functools.partial(turn_kernel, 32),
        "turn_blocks",
        [matrices],
        0,
        jax.ShapeDtypeStruct(matrices.shape, matrices.dtype),
        flops=work,
    )
    sides = []
    for col in (0, tile_y - 1):
        sides.append(
            jnp.concatenate(
                [above[col : col + 1], cast_low(coefficients[:, col]), below[col : col + 1]], axis=0
            )
        )
    pair_in, next_in = along_wide(
        jnp.where(even, sides[1], sides[0]), jnp.where(even, sides[0], sides[1])
    )
    x, grad, pair_out, next_out = call(
        functools.partial(first_kernel, sizes),
        "first_step",
        [info, row_ids, col_ids, coefficients.reshape(own, frames, width), above, below, pair_in, next_in, seen, matrices, turned],
        3,
        step_outputs(False),
        [low_scratch, rlow_scratch, residual_scratch],
        work,
    )
    for iteration in range(ITERS):
        last = iteration == ITERS - 1
        pair_in, next_in = along_wide(pair_out, next_out)
        rows_sent = tile_y if last else 2 * span
        up, down = call(
            functools.partial(fold_kernel, sizes, last),
            "fold_columns",
            [info, grad, pair_in, next_in],
            1,
            [shape(rows_sent, jnp.bfloat16), shape(rows_sent, jnp.bfloat16)],
        )
        above, below = along_narrow(up, down)
        if last:
            updated = call(
                functools.partial(final_kernel, sizes),
                "final_update",
                [info, x, grad, pair_in, next_in, above, below],
                1,
                shape(own, jnp.float32),
            )
        else:
            ending = iteration == ITERS - 2
            x, grad, pair_out, next_out, *rest = call(
                functools.partial(step_kernel, sizes, ending),
                "one_step",
                [info, row_ids, col_ids, x, grad, pair_in, next_in, above, below, seen, matrices, turned],
                3,
                step_outputs(ending),
                [low_scratch, rlow_scratch] + ([] if ending else [residual_scratch]),
                work,
            )
    residual = rest[0]
    return (
        updated.reshape(coefficients.shape),
        residual[:own].reshape(coefficients.shape),
    )


def solution(mesh):
    placed = (
        P("narrow", "wide", None, None),
        P("narrow", "wide", None, None),
        P("narrow", "wide", None, None, None),
        P("narrow", "wide", None),
        P("narrow", "wide", None),
        P("narrow", "wide"),
    )
    return jax.shard_map(
        local,
        mesh=mesh,
        in_specs=placed,
        out_specs=(P("narrow", "wide", None, None), P("narrow", "wide", None, None)),
        check_vma=False,
    )
```

```python
import functools

import jax
import jax.numpy as jnp
from jax import lax
from jax.experimental import pallas as pl
from jax.experimental.pallas import tpu as pltpu
from jax.sharding import PartitionSpec as P

ITERS = 5
descent = 0.1

ROW_FIRST, ROW_LAST, COL_FIRST, COL_LAST, EVEN = range(5)


def cast_low(value):
    return value.astype(jnp.bfloat16)


def wide_value(value):
    return value.astype(jnp.float32)


def kept(value, drop):
    return jnp.where(drop, jnp.zeros_like(value), value)


def half_step(source_ref, blocks_ref, total_ref, source_ids, target_ids, slots):
    for slot in range(slots):
        product = jnp.dot(
            source_ref[source_ids[slot]], blocks_ref[slot], preferred_element_type=jnp.float32
        )
        target = target_ids[slot]
        total_ref[target] = total_ref[target] + product


def products(sizes, rows_ref, cols_ref, observed_ref, blocks_ref, turned_ref, grad_ref, residual_ref, low_ref, rlow_ref):
    tile_x, tile_y, slots = sizes
    own = tile_x * tile_y
    extended = (tile_x + 2) * (tile_y + 2)
    low_ref[extended] = jnp.zeros_like(low_ref[extended])
    for block in range(own):
        residual_ref[block] = -observed_ref[block]
    residual_ref[own] = jnp.zeros_like(residual_ref[own])
    half_step(low_ref, blocks_ref, residual_ref, cols_ref, rows_ref, slots)
    for block in range(own + 1):
        rlow_ref[block] = cast_low(residual_ref[block])
    for block in range(extended + 1):
        grad_ref[block] = jnp.zeros_like(grad_ref[block])
    half_step(rlow_ref, turned_ref, grad_ref, rows_ref, cols_ref, slots)


def send_columns(sizes, last, info_ref, grad_ref, pair_ref, next_ref):
    tile_x, tile_y, _ = sizes
    span = tile_y + 2
    even = info_ref[EVEN] == 1
    for out_ref, right in ((pair_ref, even), (next_ref, jnp.logical_not(even))):
        if last:
            col = jnp.where(right, span - 1, 0)
            for row in range(tile_x + 2):
                out_ref[row] = cast_low(grad_ref[row * span + col])
        else:
            col = jnp.where(right, span - 2, 0)
            for row in range(tile_x + 2):
                for step in range(2):
                    out_ref[row * 2 + step] = cast_low(grad_ref[row * span + col + step])


def outside(sizes, info_ref, row, col):
    tile_x, tile_y, _ = sizes
    flag = None
    for hit, place in (
        (row == 0, ROW_FIRST),
        (row == tile_x + 1, ROW_LAST),
        (col == 0, COL_FIRST),
        (col == tile_y + 1, COL_LAST),
    ):
        if hit:
            here = info_ref[place] == 1
            flag = here if flag is None else jnp.logical_or(flag, here)
    return flag


def came_along_wide(sizes, last, info_ref, pair_in, next_in, row, col):
    tile_x, tile_y, _ = sizes
    even = info_ref[EVEN] == 1
    width = 1 if last else 2
    lefts = {1: 0} if last else {0: 0, 1: 1}
    rights = {tile_y: 0} if last else {tile_y: 0, tile_y + 1: 1}
    for places, from_pair, place in (
        (lefts, jnp.logical_not(even), COL_FIRST),
        (rights, even, COL_LAST),
    ):
        if col in places:
            at = row * width + places[col]
            came = jnp.where(from_pair, pair_in[at], next_in[at])
            return kept(wide_value(came), info_ref[place] == 1)
    return None


def prepare_kernel(sizes, chunks, flags_ref, live_ref, rows_in, cols_in, blocks_in, info_ref, rows_ref, cols_ref, blocks_ref, turned_ref, arrived):
    tile_x, tile_y, slots = sizes
    size = slots // chunks

    def bring(chunk):
        part = pl.ds(chunk * size, size)
        return pltpu.make_async_copy(blocks_in.at[part], blocks_ref.at[part], arrived.at[chunk])

    for chunk in range(chunks):
        bring(chunk).start()
    for place in range(5):
        info_ref[place] = flags_ref[place]
    live = live_ref[0]

    def copy(slot, carry):
        used = slot < live
        rows_ref[slot] = jnp.where(used, rows_in[slot], tile_x * tile_y)
        cols_ref[slot] = jnp.where(used, cols_in[slot], (tile_x + 2) * (tile_y + 2))
        return carry

    lax.fori_loop(0, slots, copy, 0)
    for chunk in range(chunks):
        bring(chunk).wait()
        for place in range(size):
            slot = chunk * size + place
            turned_ref[slot] = blocks_ref[slot].T


def first_kernel(sizes, info_ref, rows_ref, cols_ref, coef_ref, above_ref, below_ref, pair_in, next_in, observed_ref, blocks_ref, turned_ref, x_ref, grad_ref, pair_ref, next_ref, low_ref, rlow_ref, residual_ref):
    tile_x, tile_y, _ = sizes
    span = tile_y + 2
    even = info_ref[EVEN] == 1
    for row in range(tile_x + 2):
        for col in range(span):
            if col == 0:
                value = wide_value(jnp.where(even, next_in[row], pair_in[row]))
            elif col == tile_y + 1:
                value = wide_value(jnp.where(even, pair_in[row], next_in[row]))
            elif row == 0:
                value = wide_value(above_ref[col - 1])
            elif row == tile_x + 1:
                value = wide_value(below_ref[col - 1])
            else:
                value = coef_ref[(row - 1) * tile_y + col - 1]
            drop = outside(sizes, info_ref, row, col)
            if drop is not None:
                value = kept(value, drop)
            x_ref[row * span + col] = value
            low_ref[row * span + col] = cast_low(value)
    products(sizes, rows_ref, cols_ref, observed_ref, blocks_ref, turned_ref, grad_ref, residual_ref, low_ref, rlow_ref)
    send_columns(sizes, False, info_ref, grad_ref, pair_ref, next_ref)


def step_kernel(sizes, last, info_ref, rows_ref, cols_ref, x_in, grad_in, pair_in, next_in, above_ref, below_ref, observed_ref, blocks_ref, turned_ref, x_ref, grad_ref, pair_ref, next_ref, *rest):
    tile_x, tile_y, _ = sizes
    span = tile_y + 2
    if last:
        residual_ref, low_ref, rlow_ref = rest
    else:
        low_ref, rlow_ref, residual_ref = rest
    first = info_ref[ROW_FIRST] == 1
    final = info_ref[ROW_LAST] == 1
    for row in range(tile_x + 2):
        for col in range(span):
            at = row * span + col
            gradient = grad_in[at]
            came = came_along_wide(sizes, False, info_ref, pair_in, next_in, row, col)
            if came is not None:
                gradient = gradient + came
            if row < 2:
                gradient = gradient + wide_value(kept(above_ref[row * span + col], first))
            elif row >= tile_x:
                gradient = gradient + wide_value(kept(below_ref[(row - tile_x) * span + col], final))
            value = x_in[at] - descent * gradient
            drop = outside(sizes, info_ref, row, col)
            if drop is not None:
                value = kept(value, drop)
            x_ref[at] = value
            low_ref[at] = cast_low(value)
    products(sizes, rows_ref, cols_ref, observed_ref, blocks_ref, turned_ref, grad_ref, residual_ref, low_ref, rlow_ref)
    send_columns(sizes, last, info_ref, grad_ref, pair_ref, next_ref)


def fold_kernel(sizes, last, info_ref, grad_in, pair_in, next_in, up_ref, down_ref):
    tile_x, tile_y, _ = sizes
    span = tile_y + 2

    def folded(row, col):
        value = grad_in[row * span + col]
        came = came_along_wide(sizes, last, info_ref, pair_in, next_in, row, col)
        return cast_low(value if came is None else value + came)

    if last:
        for col in range(1, tile_y + 1):
            up_ref[col - 1] = folded(0, col)
            down_ref[col - 1] = folded(tile_x + 1, col)
    else:
        for row in range(2):
            for col in range(span):
                up_ref[row * span + col] = folded(row, col)
                down_ref[row * span + col] = folded(tile_x + row, col)


def final_kernel(sizes, info_ref, x_in, grad_in, pair_in, next_in, above_ref, below_ref, out_ref):
    tile_x, tile_y, _ = sizes
    span = tile_y + 2
    first = info_ref[ROW_FIRST] == 1
    final = info_ref[ROW_LAST] == 1
    for row in range(1, tile_x + 1):
        for col in range(1, tile_y + 1):
            at = row * span + col
            gradient = grad_in[at]
            came = came_along_wide(sizes, True, info_ref, pair_in, next_in, row, col)
            if came is not None:
                gradient = gradient + came
            if row == 1:
                gradient = gradient + wide_value(kept(above_ref[col - 1], first))
            if row == tile_x:
                gradient = gradient + wide_value(kept(below_ref[col - 1], final))
            out_ref[(row - 1) * tile_y + col - 1] = x_in[at] - descent * gradient


def local(coefficients, observed, blocks, block_rows, block_cols, live_count):
    tile_x, tile_y, frames, width = coefficients.shape
    slots = blocks.shape[2]
    own = tile_x * tile_y
    span = tile_y + 2
    extended = (tile_x + 2) * span
    sizes = (tile_x, tile_y, slots)
    narrow = lax.axis_size("narrow")
    wide = lax.axis_size("wide")
    a = lax.axis_index("narrow")
    b = lax.axis_index("wide")
    flags = jnp.stack([a == 0, a == narrow - 1, b == 0, b == wide - 1, b % 2 == 0]).astype(jnp.int32)
    even = b % 2 == 0

    def everywhere(move):
        return [
            (i * narrow + j, to_i * narrow + to_j)
            for i in range(wide)
            for j in range(narrow)
            for to_i, to_j in [move(i, j)]
        ]

    def other(i, j):
        return (i, j ^ 1) if i in (0, wide - 1) else (((i - 1) ^ 1) + 1, j)

    up_ring = everywhere(lambda i, j: (i, (j - 1) % narrow))
    down_ring = everywhere(lambda i, j: (i, (j + 1) % narrow))
    pairs = everywhere(lambda i, j: (i ^ 1, j))
    others = everywhere(other)

    def send(value, ring):
        return lax.ppermute(value, ("wide", "narrow"), ring)

    def along_narrow(up, down):
        return send(down, down_ring), send(up, up_ring)

    def along_wide(pair, other):
        return send(pair, pairs), send(other, others)

    seen = observed.reshape(own, frames, width)

    smem = pl.BlockSpec(memory_space=pltpu.SMEM)
    vmem = pl.BlockSpec(memory_space=pltpu.VMEM)

    def shape(count, kind):
        return jax.ShapeDtypeStruct((count, frames, width), kind)

    def place(output):
        return vmem if len(output.shape) > 1 else smem

    def call(kernel, name, inputs, scalars, outputs, scratch=(), flops=0):
        return pl.pallas_call(
            kernel,
            out_shape=outputs,
            in_specs=[smem] * scalars + [vmem] * (len(inputs) - scalars),
            out_specs=jax.tree.map(place, outputs),
            scratch_shapes=list(scratch),
            compiler_params=pltpu.CompilerParams(vmem_limit_bytes=24 << 20),
            cost_estimate=pl.CostEstimate(flops=flops, bytes_accessed=1 << 20, transcendentals=0),
            name=name,
        )(*inputs)

    low_scratch = pltpu.VMEM((extended + 1, frames, width), jnp.bfloat16)
    rlow_scratch = pltpu.VMEM((own + 1, frames, width), jnp.bfloat16)
    residual_scratch = pltpu.VMEM((own + 1, frames, width), jnp.float32)
    work = 4 * slots * frames * width * width

    def step_outputs(last):
        sent = tile_x + 2 if last else 2 * (tile_x + 2)
        outputs = [
            shape(extended, jnp.float32),
            shape(extended + 1, jnp.float32),
            shape(sent, jnp.bfloat16),
            shape(sent, jnp.bfloat16),
        ]
        return outputs + [shape(own + 1, jnp.float32)] if last else outputs

    edges = lax.optimization_barrier(
        (coefficients[0], coefficients[tile_x - 1], coefficients[:, 0], coefficients[:, tile_y - 1])
    )
    top, bottom, left, right = [cast_low(edge) for edge in edges]
    above, below = along_narrow(top, bottom)
    chunks = 8
    info, row_ids, col_ids, matrices, turned = pl.pallas_call(
        functools.partial(prepare_kernel, sizes, chunks),
        out_shape=[
            pltpu.SMEM((5,), jnp.int32),
            pltpu.SMEM((slots,), jnp.int32),
            pltpu.SMEM((slots,), jnp.int32),
            pltpu.VMEM((slots, width, width), jnp.bfloat16),
            pltpu.VMEM((slots, width, width), jnp.bfloat16),
        ],
        in_specs=[smem] * 4 + [pl.BlockSpec(memory_space=pltpu.HBM)],
        out_specs=[smem] * 3 + [vmem] * 2,
        scratch_shapes=[pltpu.SemaphoreType.DMA((chunks,))],
        compiler_params=pltpu.CompilerParams(vmem_limit_bytes=24 << 20),
        cost_estimate=pl.CostEstimate(flops=work, bytes_accessed=12 << 20, transcendentals=0),
        name="prepare_slots",
    )(flags, live_count.reshape(1), block_rows.reshape(slots), block_cols.reshape(slots), pltpu.with_memory_space_constraint(blocks.reshape(slots, width, width), pltpu.HBM))
    above, below, turned = lax.optimization_barrier((above, below, turned))
    sides = []
    for col, edge in ((0, left), (tile_y - 1, right)):
        sides.append(jnp.concatenate([above[col : col + 1], edge, below[col : col + 1]], axis=0))
    pair_in, next_in = along_wide(
        jnp.where(even, sides[1], sides[0]), jnp.where(even, sides[0], sides[1])
    )
    x, grad, pair_out, next_out = call(
        functools.partial(first_kernel, sizes),
        "first_step",
        [info, row_ids, col_ids, coefficients.reshape(own, frames, width), above, below, pair_in, next_in, seen, matrices, turned],
        3,
        step_outputs(False),
        [low_scratch, rlow_scratch, residual_scratch],
        work,
    )
    for iteration in range(ITERS):
        last = iteration == ITERS - 1
        pair_in, next_in = along_wide(pair_out, next_out)
        rows_sent = tile_y if last else 2 * span
        up, down = call(
            functools.partial(fold_kernel, sizes, last),
            "fold_columns",
            [info, grad, pair_in, next_in],
            1,
            [shape(rows_sent, jnp.bfloat16), shape(rows_sent, jnp.bfloat16)],
        )
        above, below = along_narrow(up, down)
        if last:
            updated = call(
                functools.partial(final_kernel, sizes),
                "final_update",
                [info, x, grad, pair_in, next_in, above, below],
                1,
                shape(own, jnp.float32),
            )
        else:
            ending = iteration == ITERS - 2
            x, grad, pair_out, next_out, *rest = call(
                functools.partial(step_kernel, sizes, ending),
                "one_step",
                [info, row_ids, col_ids, x, grad, pair_in, next_in, above, below, seen, matrices, turned],
                3,
                step_outputs(ending),
                [low_scratch, rlow_scratch] + ([] if ending else [residual_scratch]),
                work,
            )
    residual = rest[0]
    return (
        updated.reshape(coefficients.shape),
        residual[:own].reshape(coefficients.shape),
    )


def solution(mesh):
    placed = (
        P("narrow", "wide", None, None),
        P("narrow", "wide", None, None),
        P("narrow", "wide", None, None, None),
        P("narrow", "wide", None),
        P("narrow", "wide", None),
        P("narrow", "wide"),
    )
    return jax.shard_map(
        local,
        mesh=mesh,
        in_specs=placed,
        out_specs=(P("narrow", "wide", None, None), P("narrow", "wide", None, None)),
        check_vma=False,
    )
```

```python
import functools

import jax
import jax.numpy as jnp
from jax import lax
from jax.experimental import pallas as pl
from jax.experimental.pallas import tpu as pltpu
from jax.sharding import PartitionSpec as P

ITERS = 5
descent = 0.1

ROW_FIRST, ROW_LAST, COL_FIRST, COL_LAST, EVEN, LIVE = range(6)


def cast_low(value):
    return value.astype(jnp.bfloat16)


def wide_value(value):
    return value.astype(jnp.float32)


def kept(value, drop):
    return jnp.where(drop, jnp.zeros_like(value), value)


def half_step(source_ref, blocks_ref, total_ref, source_ids, target_ids, live, slots):
    part = slots // 2

    def add(first):
        for slot in range(first, first + part):
            product = jnp.dot(
                source_ref[source_ids[slot]], blocks_ref[slot], preferred_element_type=jnp.float32
            )
            target = target_ids[slot]
            total_ref[target] = total_ref[target] + product

    add(0)

    @pl.when(live > part)
    def _():
        add(part)


def products(sizes, info_ref, rows_ref, cols_ref, observed_ref, blocks_ref, turned_ref, grad_ref, residual_ref, low_ref, rlow_ref):
    tile_x, tile_y, slots = sizes
    own = tile_x * tile_y
    extended = (tile_x + 2) * (tile_y + 2)
    low_ref[extended] = jnp.zeros_like(low_ref[extended])
    for block in range(own):
        residual_ref[block] = -observed_ref[block]
    residual_ref[own] = jnp.zeros_like(residual_ref[own])
    half_step(low_ref, blocks_ref, residual_ref, cols_ref, rows_ref, info_ref[LIVE], slots)
    for block in range(own + 1):
        rlow_ref[block] = cast_low(residual_ref[block])
    for block in range(extended + 1):
        grad_ref[block] = jnp.zeros_like(grad_ref[block])
    half_step(rlow_ref, turned_ref, grad_ref, rows_ref, cols_ref, info_ref[LIVE], slots)


def send_columns(sizes, last, info_ref, grad_ref, pair_ref, next_ref):
    tile_x, tile_y, _ = sizes
    span = tile_y + 2
    even = info_ref[EVEN] == 1
    for out_ref, right in ((pair_ref, even), (next_ref, jnp.logical_not(even))):
        if last:
            col = jnp.where(right, span - 1, 0)
            for row in range(tile_x + 2):
                out_ref[row] = cast_low(grad_ref[row * span + col])
        else:
            col = jnp.where(right, span - 2, 0)
            for row in range(tile_x + 2):
                for step in range(2):
                    out_ref[row * 2 + step] = cast_low(grad_ref[row * span + col + step])


def outside(sizes, info_ref, row, col):
    tile_x, tile_y, _ = sizes
    flag = None
    for hit, place in (
        (row == 0, ROW_FIRST),
        (row == tile_x + 1, ROW_LAST),
        (col == 0, COL_FIRST),
        (col == tile_y + 1, COL_LAST),
    ):
        if hit:
            here = info_ref[place] == 1
            flag = here if flag is None else jnp.logical_or(flag, here)
    return flag


def came_along_wide(sizes, last, info_ref, pair_in, next_in, row, col):
    tile_x, tile_y, _ = sizes
    even = info_ref[EVEN] == 1
    width = 1 if last else 2
    lefts = {1: 0} if last else {0: 0, 1: 1}
    rights = {tile_y: 0} if last else {tile_y: 0, tile_y + 1: 1}
    for places, from_pair, place in (
        (lefts, jnp.logical_not(even), COL_FIRST),
        (rights, even, COL_LAST),
    ):
        if col in places:
            at = row * width + places[col]
            came = jnp.where(from_pair, pair_in[at], next_in[at])
            return kept(wide_value(came), info_ref[place] == 1)
    return None


def plan_kernel(sizes, flags_ref, live_ref, rows_in, cols_in, info_ref, rows_ref, cols_ref):
    tile_x, tile_y, slots = sizes
    live = live_ref[0]
    for place in range(LIVE):
        info_ref[place] = flags_ref[place]
    info_ref[LIVE] = live
    group = 8

    def copy(step, carry):
        for place in range(group):
            slot = step * group + place
            used = slot < live
            rows_ref[slot] = jnp.where(used, rows_in[slot], tile_x * tile_y)
            cols_ref[slot] = jnp.where(used, cols_in[slot], (tile_x + 2) * (tile_y + 2))
        return carry

    lax.fori_loop(0, slots // group, copy, 0)


def turn_kernel(chunks, blocks_in, blocks_ref, turned_ref, arrived):
    size = blocks_in.shape[0] // chunks

    def bring(chunk):
        part = pl.ds(chunk * size, size)
        return pltpu.make_async_copy(blocks_in.at[part], blocks_ref.at[part], arrived.at[chunk])

    for chunk in range(chunks):
        bring(chunk).start()
    for chunk in range(chunks):
        bring(chunk).wait()
        for place in range(size):
            slot = chunk * size + place
            turned_ref[slot] = blocks_ref[slot].T


def first_kernel(sizes, info_ref, rows_ref, cols_ref, coef_ref, above_ref, below_ref, pair_in, next_in, observed_ref, blocks_ref, turned_ref, x_ref, grad_ref, pair_ref, next_ref, low_ref, rlow_ref, residual_ref):
    tile_x, tile_y, _ = sizes
    span = tile_y + 2
    even = info_ref[EVEN] == 1
    for row in range(tile_x + 2):
        for col in range(span):
            if col == 0:
                value = wide_value(jnp.where(even, next_in[row], pair_in[row]))
            elif col == tile_y + 1:
                value = wide_value(jnp.where(even, pair_in[row], next_in[row]))
            elif row == 0:
                value = wide_value(above_ref[col - 1])
            elif row == tile_x + 1:
                value = wide_value(below_ref[col - 1])
            else:
                value = coef_ref[(row - 1) * tile_y + col - 1]
            drop = outside(sizes, info_ref, row, col)
            if drop is not None:
                value = kept(value, drop)
            x_ref[row * span + col] = value
            low_ref[row * span + col] = cast_low(value)
    products(sizes, info_ref, rows_ref, cols_ref, observed_ref, blocks_ref, turned_ref, grad_ref, residual_ref, low_ref, rlow_ref)
    send_columns(sizes, False, info_ref, grad_ref, pair_ref, next_ref)


def step_kernel(sizes, last, info_ref, rows_ref, cols_ref, x_in, grad_in, pair_in, next_in, above_ref, below_ref, observed_ref, blocks_ref, turned_ref, x_ref, grad_ref, pair_ref, next_ref, *rest):
    tile_x, tile_y, _ = sizes
    span = tile_y + 2
    if last:
        residual_ref, low_ref, rlow_ref = rest
    else:
        low_ref, rlow_ref, residual_ref = rest
    first = info_ref[ROW_FIRST] == 1
    final = info_ref[ROW_LAST] == 1
    for row in range(tile_x + 2):
        for col in range(span):
            at = row * span + col
            gradient = grad_in[at]
            came = came_along_wide(sizes, False, info_ref, pair_in, next_in, row, col)
            if came is not None:
                gradient = gradient + came
            if row < 2:
                gradient = gradient + wide_value(kept(above_ref[row * span + col], first))
            elif row >= tile_x:
                gradient = gradient + wide_value(kept(below_ref[(row - tile_x) * span + col], final))
            value = x_in[at] - descent * gradient
            drop = outside(sizes, info_ref, row, col)
            if drop is not None:
                value = kept(value, drop)
            x_ref[at] = value
            low_ref[at] = cast_low(value)
    products(sizes, info_ref, rows_ref, cols_ref, observed_ref, blocks_ref, turned_ref, grad_ref, residual_ref, low_ref, rlow_ref)
    send_columns(sizes, last, info_ref, grad_ref, pair_ref, next_ref)


def fold_kernel(sizes, last, info_ref, grad_in, pair_in, next_in, up_ref, down_ref):
    tile_x, tile_y, _ = sizes
    span = tile_y + 2

    def folded(row, col):
        value = grad_in[row * span + col]
        came = came_along_wide(sizes, last, info_ref, pair_in, next_in, row, col)
        return cast_low(value if came is None else value + came)

    if last:
        for col in range(1, tile_y + 1):
            up_ref[col - 1] = folded(0, col)
            down_ref[col - 1] = folded(tile_x + 1, col)
    else:
        for row in range(2):
            for col in range(span):
                up_ref[row * span + col] = folded(row, col)
                down_ref[row * span + col] = folded(tile_x + row, col)


def final_kernel(sizes, info_ref, x_in, grad_in, pair_in, next_in, above_ref, below_ref, out_ref):
    tile_x, tile_y, _ = sizes
    span = tile_y + 2
    first = info_ref[ROW_FIRST] == 1
    final = info_ref[ROW_LAST] == 1
    for row in range(1, tile_x + 1):
        for col in range(1, tile_y + 1):
            at = row * span + col
            gradient = grad_in[at]
            came = came_along_wide(sizes, True, info_ref, pair_in, next_in, row, col)
            if came is not None:
                gradient = gradient + came
            if row == 1:
                gradient = gradient + wide_value(kept(above_ref[col - 1], first))
            if row == tile_x:
                gradient = gradient + wide_value(kept(below_ref[col - 1], final))
            out_ref[(row - 1) * tile_y + col - 1] = x_in[at] - descent * gradient


def local(coefficients, observed, blocks, block_rows, block_cols, live_count):
    tile_x, tile_y, frames, width = coefficients.shape
    slots = blocks.shape[2]
    own = tile_x * tile_y
    span = tile_y + 2
    extended = (tile_x + 2) * span
    sizes = (tile_x, tile_y, slots)
    narrow = lax.axis_size("narrow")
    wide = lax.axis_size("wide")
    a = lax.axis_index("narrow")
    b = lax.axis_index("wide")
    flags = jnp.stack([a == 0, a == narrow - 1, b == 0, b == wide - 1, b % 2 == 0]).astype(jnp.int32)
    even = b % 2 == 0

    def everywhere(move):
        return [
            (i * narrow + j, to_i * narrow + to_j)
            for i in range(wide)
            for j in range(narrow)
            for to_i, to_j in [move(i, j)]
        ]

    def other(i, j):
        return (i, j ^ 1) if i in (0, wide - 1) else (((i - 1) ^ 1) + 1, j)

    up_ring = everywhere(lambda i, j: (i, (j - 1) % narrow))
    down_ring = everywhere(lambda i, j: (i, (j + 1) % narrow))
    pairs = everywhere(lambda i, j: (i ^ 1, j))
    others = everywhere(other)

    def send(value, ring):
        return lax.ppermute(value, ("wide", "narrow"), ring)

    def along_narrow(up, down):
        return send(down, down_ring), send(up, up_ring)

    def along_wide(pair, other):
        return send(pair, pairs), send(other, others)

    seen = observed.reshape(own, frames, width)

    smem = pl.BlockSpec(memory_space=pltpu.SMEM)
    vmem = pl.BlockSpec(memory_space=pltpu.VMEM)

    def shape(count, kind):
        return jax.ShapeDtypeStruct((count, frames, width), kind)

    def place(output):
        return vmem if len(output.shape) > 1 else smem

    def call(kernel, name, inputs, scalars, outputs, scratch=(), flops=0):
        return pl.pallas_call(
            kernel,
            out_shape=outputs,
            in_specs=[smem] * scalars + [vmem] * (len(inputs) - scalars),
            out_specs=jax.tree.map(place, outputs),
            scratch_shapes=list(scratch),
            compiler_params=pltpu.CompilerParams(vmem_limit_bytes=24 << 20),
            cost_estimate=pl.CostEstimate(flops=flops, bytes_accessed=1 << 20, transcendentals=0),
            name=name,
        )(*inputs)

    low_scratch = pltpu.VMEM((extended + 1, frames, width), jnp.bfloat16)
    rlow_scratch = pltpu.VMEM((own + 1, frames, width), jnp.bfloat16)
    residual_scratch = pltpu.VMEM((own + 1, frames, width), jnp.float32)
    work = 4 * slots * frames * width * width

    def step_outputs(last):
        sent = tile_x + 2 if last else 2 * (tile_x + 2)
        outputs = [
            shape(extended, jnp.float32),
            shape(extended + 1, jnp.float32),
            shape(sent, jnp.bfloat16),
            shape(sent, jnp.bfloat16),
        ]
        return outputs + [shape(own + 1, jnp.float32)] if last else outputs

    top, bottom = lax.optimization_barrier((coefficients[0], coefficients[tile_x - 1]))
    above, below = along_narrow(cast_low(top), cast_low(bottom))
    in_hbm = pltpu.with_memory_space_constraint
    info, row_ids, col_ids = call(
        functools.partial(plan_kernel, sizes),
        "plan_slots",
        [
            flags,
            live_count.reshape(1),
            in_hbm(block_rows.reshape(slots), pltpu.HBM),
            in_hbm(block_cols.reshape(slots), pltpu.HBM),
        ],
        4,
        [
            pltpu.SMEM((LIVE + 1,), jnp.int32),
            pltpu.SMEM((slots,), jnp.int32),
            pltpu.SMEM((slots,), jnp.int32),
        ],
        flops=work,
    )
    chunks = 8
    matrices, turned = pl.pallas_call(
        functools.partial(turn_kernel, chunks),
        out_shape=[pltpu.VMEM((slots, width, width), jnp.bfloat16)] * 2,
        in_specs=[pl.BlockSpec(memory_space=pltpu.HBM)],
        out_specs=[vmem] * 2,
        scratch_shapes=[pltpu.SemaphoreType.DMA((chunks,))],
        compiler_params=pltpu.CompilerParams(vmem_limit_bytes=24 << 20),
        cost_estimate=pl.CostEstimate(flops=work, bytes_accessed=12 << 20, transcendentals=0),
        name="turn_blocks",
    )(in_hbm(blocks.reshape(slots, width, width), pltpu.HBM))
    above, below, info = lax.optimization_barrier((above, below, info))
    left, right = lax.optimization_barrier((coefficients[:, 0], coefficients[:, tile_y - 1]))
    left, right = cast_low(left), cast_low(right)
    sides = []
    for col, edge in ((0, left), (tile_y - 1, right)):
        sides.append(jnp.concatenate([above[col : col + 1], edge, below[col : col + 1]], axis=0))
    pair_in, next_in = along_wide(
        jnp.where(even, sides[1], sides[0]), jnp.where(even, sides[0], sides[1])
    )
    x, grad, pair_out, next_out = call(
        functools.partial(first_kernel, sizes),
        "first_step",
        [info, row_ids, col_ids, coefficients.reshape(own, frames, width), above, below, pair_in, next_in, seen, matrices, turned],
        3,
        step_outputs(False),
        [low_scratch, rlow_scratch, residual_scratch],
        work,
    )
    for iteration in range(ITERS):
        last = iteration == ITERS - 1
        pair_in, next_in = along_wide(pair_out, next_out)
        rows_sent = tile_y if last else 2 * span
        up, down = call(
            functools.partial(fold_kernel, sizes, last),
            "fold_columns",
            [info, grad, pair_in, next_in],
            1,
            [shape(rows_sent, jnp.bfloat16), shape(rows_sent, jnp.bfloat16)],
        )
        above, below = along_narrow(up, down)
        if last:
            updated = call(
                functools.partial(final_kernel, sizes),
                "final_update",
                [info, x, grad, pair_in, next_in, above, below],
                1,
                shape(own, jnp.float32),
            )
        else:
            ending = iteration == ITERS - 2
            x, grad, pair_out, next_out, *rest = call(
                functools.partial(step_kernel, sizes, ending),
                "one_step",
                [info, row_ids, col_ids, x, grad, pair_in, next_in, above, below, seen, matrices, turned],
                3,
                step_outputs(ending),
                [low_scratch, rlow_scratch] + ([] if ending else [residual_scratch]),
                work,
            )
    residual = rest[0]
    return (
        updated.reshape(coefficients.shape),
        residual[:own].reshape(coefficients.shape),
    )


def solution(mesh):
    placed = (
        P("narrow", "wide", None, None),
        P("narrow", "wide", None, None),
        P("narrow", "wide", None, None, None),
        P("narrow", "wide", None),
        P("narrow", "wide", None),
        P("narrow", "wide"),
    )
    return jax.shard_map(
        local,
        mesh=mesh,
        in_specs=placed,
        out_specs=(P("narrow", "wide", None, None), P("narrow", "wide", None, None)),
        check_vma=False,
    )
```

```python
import functools

import jax
import jax.numpy as jnp
from jax import lax
from jax.experimental import pallas as pl
from jax.experimental.pallas import tpu as pltpu
from jax.sharding import PartitionSpec as P

ITERS = 5
descent = 0.1

ROW_FIRST, ROW_LAST, COL_FIRST, COL_LAST, EVEN, ROW_EVEN, LIVE = range(7)


def cast_low(value):
    return value.astype(jnp.bfloat16)


def wide_value(value):
    return value.astype(jnp.float32)


def kept(value, drop):
    return jnp.where(drop, jnp.zeros_like(value), value)


def half_step(source_ref, blocks_ref, total_ref, source_ids, target_ids, live, slots):
    part = slots // 2

    def add(first):
        for slot in range(first, first + part):
            product = jnp.dot(
                source_ref[source_ids[slot]], blocks_ref[slot], preferred_element_type=jnp.float32
            )
            target = target_ids[slot]
            total_ref[target] = total_ref[target] + product

    add(0)

    @pl.when(live > part)
    def _():
        add(part)


def products(sizes, info_ref, rows_ref, cols_ref, observed_ref, blocks_ref, turned_ref, grad_ref, residual_ref, low_ref, rlow_ref):
    tile_x, tile_y, slots = sizes
    own = tile_x * tile_y
    extended = (tile_x + 2) * (tile_y + 2)
    low_ref[extended] = jnp.zeros_like(low_ref[extended])
    for block in range(own):
        residual_ref[block] = -observed_ref[block]
    residual_ref[own] = jnp.zeros_like(residual_ref[own])
    half_step(low_ref, blocks_ref, residual_ref, cols_ref, rows_ref, info_ref[LIVE], slots)
    for block in range(own + 1):
        rlow_ref[block] = cast_low(residual_ref[block])
    for block in range(extended + 1):
        grad_ref[block] = jnp.zeros_like(grad_ref[block])
    half_step(rlow_ref, turned_ref, grad_ref, rows_ref, cols_ref, info_ref[LIVE], slots)


def send_columns(sizes, last, info_ref, grad_ref, pair_ref, next_ref):
    tile_x, tile_y, _ = sizes
    span = tile_y + 2
    even = info_ref[EVEN] == 1
    for out_ref, right in ((pair_ref, even), (next_ref, jnp.logical_not(even))):
        if last:
            col = jnp.where(right, span - 1, 0)
            for row in range(tile_x + 2):
                out_ref[row] = cast_low(grad_ref[row * span + col])
        else:
            col = jnp.where(right, span - 2, 0)
            for row in range(tile_x + 2):
                for step in range(2):
                    out_ref[row * 2 + step] = cast_low(grad_ref[row * span + col + step])


def outside(sizes, info_ref, row, col):
    tile_x, tile_y, _ = sizes
    flag = None
    for hit, place in (
        (row == 0, ROW_FIRST),
        (row == tile_x + 1, ROW_LAST),
        (col == 0, COL_FIRST),
        (col == tile_y + 1, COL_LAST),
    ):
        if hit:
            here = info_ref[place] == 1
            flag = here if flag is None else jnp.logical_or(flag, here)
    return flag


def came_along_wide(sizes, last, info_ref, pair_in, next_in, row, col):
    tile_x, tile_y, _ = sizes
    even = info_ref[EVEN] == 1
    width = 1 if last else 2
    lefts = {1: 0} if last else {0: 0, 1: 1}
    rights = {tile_y: 0} if last else {tile_y: 0, tile_y + 1: 1}
    for places, from_pair, place in (
        (lefts, jnp.logical_not(even), COL_FIRST),
        (rights, even, COL_LAST),
    ):
        if col in places:
            at = row * width + places[col]
            came = jnp.where(from_pair, pair_in[at], next_in[at])
            return kept(wide_value(came), info_ref[place] == 1)
    return None


def plan_kernel(sizes, flags_ref, live_ref, rows_in, cols_in, info_ref, rows_ref, cols_ref):
    tile_x, tile_y, slots = sizes
    live = live_ref[0]
    for place in range(LIVE):
        info_ref[place] = flags_ref[place]
    info_ref[LIVE] = live
    group = 8

    def copy(step, carry):
        for place in range(group):
            slot = step * group + place
            used = slot < live
            rows_ref[slot] = jnp.where(used, rows_in[slot], tile_x * tile_y)
            cols_ref[slot] = jnp.where(used, cols_in[slot], (tile_x + 2) * (tile_y + 2))
        return carry

    lax.fori_loop(0, slots // group, copy, 0)


def turn_kernel(chunks, blocks_in, blocks_ref, turned_ref, arrived):
    size = blocks_in.shape[0] // chunks

    def bring(chunk):
        part = pl.ds(chunk * size, size)
        return pltpu.make_async_copy(blocks_in.at[part], blocks_ref.at[part], arrived.at[chunk])

    for chunk in range(chunks):
        bring(chunk).start()
    for chunk in range(chunks):
        bring(chunk).wait()
        for place in range(size):
            slot = chunk * size + place
            turned_ref[slot] = blocks_ref[slot].T


def first_kernel(sizes, info_ref, rows_ref, cols_ref, coef_ref, far_in, near_in, pair_in, next_in, observed_ref, blocks_ref, turned_ref, x_ref, grad_ref, pair_ref, next_ref, low_ref, rlow_ref, residual_ref):
    tile_x, tile_y, _ = sizes
    span = tile_y + 2
    even = info_ref[EVEN] == 1
    for row in range(tile_x + 2):
        for col in range(span):
            if col == 0:
                value = wide_value(jnp.where(even, next_in[row], pair_in[row]))
            elif col == tile_y + 1:
                value = wide_value(jnp.where(even, pair_in[row], next_in[row]))
            elif row == 0:
                value = came_along_narrow(info_ref, near_in, far_in, True, col - 1)
            elif row == tile_x + 1:
                value = came_along_narrow(info_ref, near_in, far_in, False, col - 1)
            else:
                value = coef_ref[(row - 1) * tile_y + col - 1]
            drop = outside(sizes, info_ref, row, col)
            if drop is not None:
                value = kept(value, drop)
            x_ref[row * span + col] = value
            low_ref[row * span + col] = cast_low(value)
    products(sizes, info_ref, rows_ref, cols_ref, observed_ref, blocks_ref, turned_ref, grad_ref, residual_ref, low_ref, rlow_ref)
    send_columns(sizes, False, info_ref, grad_ref, pair_ref, next_ref)


def step_kernel(sizes, last, info_ref, rows_ref, cols_ref, x_in, grad_in, pair_in, next_in, far_in, near_in, observed_ref, blocks_ref, turned_ref, x_ref, grad_ref, pair_ref, next_ref, *rest):
    tile_x, tile_y, _ = sizes
    span = tile_y + 2
    if last:
        residual_ref, low_ref, rlow_ref = rest
    else:
        low_ref, rlow_ref, residual_ref = rest
    for row in range(tile_x + 2):
        for col in range(span):
            at = row * span + col
            gradient = grad_in[at]
            came = came_along_wide(sizes, False, info_ref, pair_in, next_in, row, col)
            if came is not None:
                gradient = gradient + came
            if row < 2:
                gradient = gradient + came_along_narrow(info_ref, near_in, far_in, True, at)
            elif row >= tile_x:
                gradient = gradient + came_along_narrow(info_ref, near_in, far_in, False, at - tile_x * span)
            value = x_in[at] - descent * gradient
            drop = outside(sizes, info_ref, row, col)
            if drop is not None:
                value = kept(value, drop)
            x_ref[at] = value
            low_ref[at] = cast_low(value)
    products(sizes, info_ref, rows_ref, cols_ref, observed_ref, blocks_ref, turned_ref, grad_ref, residual_ref, low_ref, rlow_ref)
    send_columns(sizes, last, info_ref, grad_ref, pair_ref, next_ref)


def came_along_narrow(info_ref, near_in, far_in, upper, at):
    even = info_ref[ROW_EVEN] == 1
    from_near = jnp.logical_not(even) if upper else even
    came = jnp.where(from_near, near_in[at], far_in[at])
    return wide_value(kept(came, info_ref[ROW_FIRST if upper else ROW_LAST] == 1))


def fold_kernel(sizes, last, info_ref, grad_in, pair_in, next_in, far_ref, near_ref):
    tile_x, tile_y, _ = sizes
    span = tile_y + 2
    even = info_ref[ROW_EVEN] == 1

    def folded(row, col):
        value = grad_in[row * span + col]
        came = came_along_wide(sizes, last, info_ref, pair_in, next_in, row, col)
        return cast_low(value if came is None else value + came)

    for out_ref, lower in ((near_ref, even), (far_ref, jnp.logical_not(even))):
        if last:
            row = jnp.where(lower, tile_x + 1, 0)
            for col in range(1, tile_y + 1):
                out_ref[col - 1] = folded(row, col)
        else:
            row = jnp.where(lower, tile_x, 0)
            for step in range(2):
                for col in range(span):
                    out_ref[step * span + col] = folded(row + step, col)


def final_kernel(sizes, info_ref, x_in, grad_in, pair_in, next_in, far_in, near_in, out_ref):
    tile_x, tile_y, _ = sizes
    span = tile_y + 2
    for row in range(1, tile_x + 1):
        for col in range(1, tile_y + 1):
            at = row * span + col
            gradient = grad_in[at]
            came = came_along_wide(sizes, True, info_ref, pair_in, next_in, row, col)
            if came is not None:
                gradient = gradient + came
            if row == 1:
                gradient = gradient + came_along_narrow(info_ref, near_in, far_in, True, col - 1)
            if row == tile_x:
                gradient = gradient + came_along_narrow(info_ref, near_in, far_in, False, col - 1)
            out_ref[(row - 1) * tile_y + col - 1] = x_in[at] - descent * gradient


def local(coefficients, observed, blocks, block_rows, block_cols, live_count):
    tile_x, tile_y, frames, width = coefficients.shape
    slots = blocks.shape[2]
    own = tile_x * tile_y
    span = tile_y + 2
    extended = (tile_x + 2) * span
    sizes = (tile_x, tile_y, slots)
    narrow = lax.axis_size("narrow")
    wide = lax.axis_size("wide")
    a = lax.axis_index("narrow")
    b = lax.axis_index("wide")
    flags = jnp.stack([a == 0, a == narrow - 1, b == 0, b == wide - 1, b % 2 == 0, a % 2 == 0]).astype(jnp.int32)
    even = b % 2 == 0
    row_even = a % 2 == 0

    def everywhere(move):
        return [
            (i * narrow + j, to_i * narrow + to_j)
            for i in range(wide)
            for j in range(narrow)
            for to_i, to_j in [move(i, j)]
        ]

    def other(i, j):
        return (i, j ^ 1) if i in (0, wide - 1) else (((i - 1) ^ 1) + 1, j)

    def far(i, j):
        return (i ^ 1, j) if j in (0, narrow - 1) else (i, ((j - 1) ^ 1) + 1)

    near_pairs = everywhere(lambda i, j: (i, j ^ 1))
    far_pairs = everywhere(far)
    pairs = everywhere(lambda i, j: (i ^ 1, j))
    others = everywhere(other)

    def send(value, ring):
        return lax.ppermute(value, ("wide", "narrow"), ring)

    def along_narrow(far, near):
        return send(far, far_pairs), send(near, near_pairs)

    def along_wide(pair, other):
        return send(pair, pairs), send(other, others)

    seen = observed.reshape(own, frames, width)

    smem = pl.BlockSpec(memory_space=pltpu.SMEM)
    vmem = pl.BlockSpec(memory_space=pltpu.VMEM)

    def shape(count, kind):
        return jax.ShapeDtypeStruct((count, frames, width), kind)

    def place(output):
        return vmem if len(output.shape) > 1 else smem

    def call(kernel, name, inputs, scalars, outputs, scratch=(), flops=0):
        return pl.pallas_call(
            kernel,
            out_shape=outputs,
            in_specs=[smem] * scalars + [vmem] * (len(inputs) - scalars),
            out_specs=jax.tree.map(place, outputs),
            scratch_shapes=list(scratch),
            compiler_params=pltpu.CompilerParams(vmem_limit_bytes=24 << 20),
            cost_estimate=pl.CostEstimate(flops=flops, bytes_accessed=1 << 20, transcendentals=0),
            name=name,
        )(*inputs)

    low_scratch = pltpu.VMEM((extended + 1, frames, width), jnp.bfloat16)
    rlow_scratch = pltpu.VMEM((own + 1, frames, width), jnp.bfloat16)
    residual_scratch = pltpu.VMEM((own + 1, frames, width), jnp.float32)
    work = 4 * slots * frames * width * width

    def step_outputs(last):
        sent = tile_x + 2 if last else 2 * (tile_x + 2)
        outputs = [
            shape(extended, jnp.float32),
            shape(extended + 1, jnp.float32),
            shape(sent, jnp.bfloat16),
            shape(sent, jnp.bfloat16),
        ]
        return outputs + [shape(own + 1, jnp.float32)] if last else outputs

    top, bottom = lax.optimization_barrier((coefficients[0], coefficients[tile_x - 1]))
    far_row, near = along_narrow(
        cast_low(jnp.where(row_even, top, bottom)), cast_low(jnp.where(row_even, bottom, top))
    )
    in_hbm = pltpu.with_memory_space_constraint
    info, row_ids, col_ids = call(
        functools.partial(plan_kernel, sizes),
        "plan_slots",
        [
            flags,
            live_count.reshape(1),
            in_hbm(block_rows.reshape(slots), pltpu.HBM),
            in_hbm(block_cols.reshape(slots), pltpu.HBM),
        ],
        4,
        [
            pltpu.SMEM((LIVE + 1,), jnp.int32),
            pltpu.SMEM((slots,), jnp.int32),
            pltpu.SMEM((slots,), jnp.int32),
        ],
        flops=work,
    )
    chunks = 8
    matrices, turned = pl.pallas_call(
        functools.partial(turn_kernel, chunks),
        out_shape=[pltpu.VMEM((slots, width, width), jnp.bfloat16)] * 2,
        in_specs=[pl.BlockSpec(memory_space=pltpu.HBM)],
        out_specs=[vmem] * 2,
        scratch_shapes=[pltpu.SemaphoreType.DMA((chunks,))],
        compiler_params=pltpu.CompilerParams(vmem_limit_bytes=24 << 20),
        cost_estimate=pl.CostEstimate(flops=work, bytes_accessed=12 << 20, transcendentals=0),
        name="turn_blocks",
    )(in_hbm(blocks.reshape(slots, width, width), pltpu.HBM))
    near, far_row, info = lax.optimization_barrier((near, far_row, info))
    above = jnp.where(row_even, far_row, near)
    below = jnp.where(row_even, near, far_row)
    left, right = lax.optimization_barrier((coefficients[:, 0], coefficients[:, tile_y - 1]))
    left, right = cast_low(left), cast_low(right)
    sides = []
    for col, edge in ((0, left), (tile_y - 1, right)):
        sides.append(jnp.concatenate([above[col : col + 1], edge, below[col : col + 1]], axis=0))
    pair_in, next_in = along_wide(
        jnp.where(even, sides[1], sides[0]), jnp.where(even, sides[0], sides[1])
    )
    x, grad, pair_out, next_out = call(
        functools.partial(first_kernel, sizes),
        "first_step",
        [info, row_ids, col_ids, coefficients.reshape(own, frames, width), far_row, near, pair_in, next_in, seen, matrices, turned],
        3,
        step_outputs(False),
        [low_scratch, rlow_scratch, residual_scratch],
        work,
    )
    for iteration in range(ITERS):
        last = iteration == ITERS - 1
        pair_in, next_in = along_wide(pair_out, next_out)
        rows_sent = tile_y if last else 2 * span
        far_row, near = call(
            functools.partial(fold_kernel, sizes, last),
            "fold_columns",
            [info, grad, pair_in, next_in],
            1,
            [shape(rows_sent, jnp.bfloat16), shape(rows_sent, jnp.bfloat16)],
        )
        far_row, near = along_narrow(far_row, near)
        if last:
            updated = call(
                functools.partial(final_kernel, sizes),
                "final_update",
                [info, x, grad, pair_in, next_in, far_row, near],
                1,
                shape(own, jnp.float32),
            )
        else:
            ending = iteration == ITERS - 2
            x, grad, pair_out, next_out, *rest = call(
                functools.partial(step_kernel, sizes, ending),
                "one_step",
                [info, row_ids, col_ids, x, grad, pair_in, next_in, far_row, near, seen, matrices, turned],
                3,
                step_outputs(ending),
                [low_scratch, rlow_scratch] + ([] if ending else [residual_scratch]),
                work,
            )
    residual = rest[0]
    return (
        updated.reshape(coefficients.shape),
        residual[:own].reshape(coefficients.shape),
    )


def solution(mesh):
    placed = (
        P("narrow", "wide", None, None),
        P("narrow", "wide", None, None),
        P("narrow", "wide", None, None, None),
        P("narrow", "wide", None),
        P("narrow", "wide", None),
        P("narrow", "wide"),
    )
    return jax.shard_map(
        local,
        mesh=mesh,
        in_specs=placed,
        out_specs=(P("narrow", "wide", None, None), P("narrow", "wide", None, None)),
        check_vma=False,
    )
```

```python
import functools

import jax
import jax.numpy as jnp
from jax import lax
from jax.experimental import pallas as pl
from jax.experimental.pallas import tpu as pltpu
from jax.sharding import PartitionSpec as P

ITERS = 5
descent = 0.1

ROW_FIRST, ROW_LAST, COL_FIRST, COL_LAST, EVEN, ROW_EVEN, LIVE = range(7)


def cast_low(value):
    return value.astype(jnp.bfloat16)


def wide_value(value):
    return value.astype(jnp.float32)


def kept(value, drop):
    return jnp.where(drop, jnp.zeros_like(value), value)


def half_step(source_ref, blocks, total_ref, source_ids, target_ids, live):
    def add(first, blocks_ref):
        for at in range(0, blocks_ref.shape[0], 2):
            slot = first + at
            upper = source_ref[source_ids[slot]]
            lower = source_ref[source_ids[slot + 1]]
            frames, width = upper.shape
            zeros = jnp.zeros_like(upper)
            taken = jnp.concatenate(
                [jnp.concatenate([upper, zeros], axis=1), jnp.concatenate([zeros, lower], axis=1)],
                axis=0,
            )
            matrices = blocks_ref[pl.ds(at, 2)].reshape(2 * width, width)
            product = jnp.dot(taken, matrices, preferred_element_type=jnp.float32)
            target = target_ids[slot]
            total_ref[target] = total_ref[target] + product[:frames]
            target = target_ids[slot + 1]
            total_ref[target] = total_ref[target] + product[frames:]

    first_ref, second_ref = blocks
    half = first_ref.shape[0]
    add(0, first_ref)

    @pl.when(live > half)
    def _():
        add(half, second_ref)


def products(sizes, info_ref, rows_ref, cols_ref, observed_ref, blocks, turned, grad_ref, residual_ref, low_ref, rlow_ref):
    tile_x, tile_y, _ = sizes
    own = tile_x * tile_y
    extended = (tile_x + 2) * (tile_y + 2)
    low_ref[extended] = jnp.zeros_like(low_ref[extended])
    for block in range(own):
        residual_ref[block] = -observed_ref[block]
    residual_ref[own] = jnp.zeros_like(residual_ref[own])
    half_step(low_ref, blocks, residual_ref, cols_ref, rows_ref, info_ref[LIVE])
    for block in range(own + 1):
        rlow_ref[block] = cast_low(residual_ref[block])
    for block in range(extended + 1):
        grad_ref[block] = jnp.zeros_like(grad_ref[block])
    half_step(rlow_ref, turned, grad_ref, rows_ref, cols_ref, info_ref[LIVE])


def send_columns(sizes, last, info_ref, grad_ref, pair_ref, next_ref):
    tile_x, tile_y, _ = sizes
    span = tile_y + 2
    even = info_ref[EVEN] == 1
    for out_ref, right in ((pair_ref, even), (next_ref, jnp.logical_not(even))):
        if last:
            col = jnp.where(right, span - 1, 0)
            for row in range(tile_x + 2):
                out_ref[row] = cast_low(grad_ref[row * span + col])
        else:
            col = jnp.where(right, span - 2, 0)
            for row in range(tile_x + 2):
                for step in range(2):
                    out_ref[row * 2 + step] = cast_low(grad_ref[row * span + col + step])


def outside(sizes, info_ref, row, col):
    tile_x, tile_y, _ = sizes
    flag = None
    for hit, place in (
        (row == 0, ROW_FIRST),
        (row == tile_x + 1, ROW_LAST),
        (col == 0, COL_FIRST),
        (col == tile_y + 1, COL_LAST),
    ):
        if hit:
            here = info_ref[place] == 1
            flag = here if flag is None else jnp.logical_or(flag, here)
    return flag


def came_along_wide(sizes, last, info_ref, pair_in, next_in, row, col):
    tile_x, tile_y, _ = sizes
    even = info_ref[EVEN] == 1
    width = 1 if last else 2
    lefts = {1: 0} if last else {0: 0, 1: 1}
    rights = {tile_y: 0} if last else {tile_y: 0, tile_y + 1: 1}
    for places, from_pair, place in (
        (lefts, jnp.logical_not(even), COL_FIRST),
        (rights, even, COL_LAST),
    ):
        if col in places:
            at = row * width + places[col]
            came = jnp.where(from_pair, pair_in[at], next_in[at])
            return kept(wide_value(came), info_ref[place] == 1)
    return None


def bring(blocks_in, blocks_ref, arrived, chunk, first):
    size = blocks_ref.shape[0] // arrived.shape[0]
    return pltpu.make_async_copy(
        blocks_in.at[pl.ds(first + chunk * size, size)],
        blocks_ref.at[pl.ds(chunk * size, size)],
        arrived.at[chunk],
    )


def plan_kernel(sizes, flags_ref, live_ref, rows_in, cols_in, blocks_in, info_ref, rows_ref, cols_ref, first_blocks, arrived):
    tile_x, tile_y, slots = sizes
    for chunk in range(arrived.shape[0]):
        bring(blocks_in, first_blocks, arrived, chunk, 0).start()
    live = live_ref[0]
    for place in range(LIVE):
        info_ref[place] = flags_ref[place]
    info_ref[LIVE] = live
    group = 8

    def copy(step, carry):
        for place in range(group):
            slot = step * group + place
            used = slot < live
            rows_ref[slot] = jnp.where(used, rows_in[slot], tile_x * tile_y)
            cols_ref[slot] = jnp.where(used, cols_in[slot], (tile_x + 2) * (tile_y + 2))
        return carry

    lax.fori_loop(0, slots // group, copy, 0)
    for chunk in range(arrived.shape[0]):
        bring(blocks_in, first_blocks, arrived, chunk, 0).wait()


def turn_kernel(info_ref, first_blocks, blocks_in, first_turned, second_blocks, second_turned, arrived):
    half = first_blocks.shape[0]
    more = info_ref[LIVE] > half

    @pl.when(more)
    def _():
        for chunk in range(arrived.shape[0]):
            bring(blocks_in, second_blocks, arrived, chunk, half).start()

    for slot in range(half):
        first_turned[slot] = first_blocks[slot].T

    @pl.when(more)
    def _():
        size = half // arrived.shape[0]
        for chunk in range(arrived.shape[0]):
            bring(blocks_in, second_blocks, arrived, chunk, half).wait()
            for slot in range(chunk * size, (chunk + 1) * size):
                second_turned[slot] = second_blocks[slot].T


def first_kernel(sizes, info_ref, rows_ref, cols_ref, coef_ref, far_in, near_in, pair_in, next_in, observed_ref, first_blocks, second_blocks, first_turned, second_turned, x_ref, grad_ref, pair_ref, next_ref, low_ref, rlow_ref, residual_ref):
    tile_x, tile_y, _ = sizes
    span = tile_y + 2
    even = info_ref[EVEN] == 1
    for row in range(tile_x + 2):
        for col in range(span):
            if col == 0:
                value = wide_value(jnp.where(even, next_in[row], pair_in[row]))
            elif col == tile_y + 1:
                value = wide_value(jnp.where(even, pair_in[row], next_in[row]))
            elif row == 0:
                value = came_along_narrow(info_ref, near_in, far_in, True, col - 1)
            elif row == tile_x + 1:
                value = came_along_narrow(info_ref, near_in, far_in, False, col - 1)
            else:
                value = coef_ref[(row - 1) * tile_y + col - 1]
            drop = outside(sizes, info_ref, row, col)
            if drop is not None:
                value = kept(value, drop)
            x_ref[row * span + col] = value
            low_ref[row * span + col] = cast_low(value)
    products(sizes, info_ref, rows_ref, cols_ref, observed_ref, (first_blocks, second_blocks), (first_turned, second_turned), grad_ref, residual_ref, low_ref, rlow_ref)
    send_columns(sizes, False, info_ref, grad_ref, pair_ref, next_ref)


def step_kernel(sizes, last, info_ref, rows_ref, cols_ref, x_in, grad_in, pair_in, next_in, far_in, near_in, observed_ref, first_blocks, second_blocks, first_turned, second_turned, x_ref, grad_ref, pair_ref, next_ref, *rest):
    tile_x, tile_y, _ = sizes
    span = tile_y + 2
    if last:
        residual_ref, low_ref, rlow_ref = rest
    else:
        low_ref, rlow_ref, residual_ref = rest
    for row in range(tile_x + 2):
        for col in range(span):
            at = row * span + col
            gradient = grad_in[at]
            came = came_along_wide(sizes, False, info_ref, pair_in, next_in, row, col)
            if came is not None:
                gradient = gradient + came
            if row < 2:
                gradient = gradient + came_along_narrow(info_ref, near_in, far_in, True, at)
            elif row >= tile_x:
                gradient = gradient + came_along_narrow(info_ref, near_in, far_in, False, at - tile_x * span)
            value = x_in[at] - descent * gradient
            drop = outside(sizes, info_ref, row, col)
            if drop is not None:
                value = kept(value, drop)
            x_ref[at] = value
            low_ref[at] = cast_low(value)
    products(sizes, info_ref, rows_ref, cols_ref, observed_ref, (first_blocks, second_blocks), (first_turned, second_turned), grad_ref, residual_ref, low_ref, rlow_ref)
    send_columns(sizes, last, info_ref, grad_ref, pair_ref, next_ref)


def came_along_narrow(info_ref, near_in, far_in, upper, at):
    even = info_ref[ROW_EVEN] == 1
    from_near = jnp.logical_not(even) if upper else even
    came = jnp.where(from_near, near_in[at], far_in[at])
    return wide_value(kept(came, info_ref[ROW_FIRST if upper else ROW_LAST] == 1))


def fold_kernel(sizes, last, info_ref, grad_in, pair_in, next_in, far_ref, near_ref):
    tile_x, tile_y, _ = sizes
    span = tile_y + 2
    even = info_ref[ROW_EVEN] == 1

    def folded(row, col):
        value = grad_in[row * span + col]
        came = came_along_wide(sizes, last, info_ref, pair_in, next_in, row, col)
        return cast_low(value if came is None else value + came)

    for out_ref, lower in ((near_ref, even), (far_ref, jnp.logical_not(even))):
        if last:
            row = jnp.where(lower, tile_x + 1, 0)
            for col in range(1, tile_y + 1):
                out_ref[col - 1] = folded(row, col)
        else:
            row = jnp.where(lower, tile_x, 0)
            for step in range(2):
                for col in range(span):
                    out_ref[step * span + col] = folded(row + step, col)


def final_kernel(sizes, info_ref, x_in, grad_in, pair_in, next_in, far_in, near_in, out_ref):
    tile_x, tile_y, _ = sizes
    span = tile_y + 2
    for row in range(1, tile_x + 1):
        for col in range(1, tile_y + 1):
            at = row * span + col
            gradient = grad_in[at]
            came = came_along_wide(sizes, True, info_ref, pair_in, next_in, row, col)
            if came is not None:
                gradient = gradient + came
            if row == 1:
                gradient = gradient + came_along_narrow(info_ref, near_in, far_in, True, col - 1)
            if row == tile_x:
                gradient = gradient + came_along_narrow(info_ref, near_in, far_in, False, col - 1)
            out_ref[(row - 1) * tile_y + col - 1] = x_in[at] - descent * gradient


def local(coefficients, observed, blocks, block_rows, block_cols, live_count):
    tile_x, tile_y, frames, width = coefficients.shape
    slots = blocks.shape[2]
    own = tile_x * tile_y
    span = tile_y + 2
    extended = (tile_x + 2) * span
    sizes = (tile_x, tile_y, slots)
    narrow = lax.axis_size("narrow")
    wide = lax.axis_size("wide")
    a = lax.axis_index("narrow")
    b = lax.axis_index("wide")
    flags = jnp.stack([a == 0, a == narrow - 1, b == 0, b == wide - 1, b % 2 == 0, a % 2 == 0]).astype(jnp.int32)
    even = b % 2 == 0
    row_even = a % 2 == 0

    def everywhere(move):
        return [
            (i * narrow + j, to_i * narrow + to_j)
            for i in range(wide)
            for j in range(narrow)
            for to_i, to_j in [move(i, j)]
        ]

    def other(i, j):
        return (i, j ^ 1) if i in (0, wide - 1) else (((i - 1) ^ 1) + 1, j)

    def far(i, j):
        return (i ^ 1, j) if j in (0, narrow - 1) else (i, ((j - 1) ^ 1) + 1)

    near_pairs = everywhere(lambda i, j: (i, j ^ 1))
    far_pairs = everywhere(far)
    pairs = everywhere(lambda i, j: (i ^ 1, j))
    others = everywhere(other)

    def send(value, ring):
        return lax.ppermute(value, ("wide", "narrow"), ring)

    def along_narrow(far, near):
        return send(far, far_pairs), send(near, near_pairs)

    def along_wide(pair, other):
        return send(pair, pairs), send(other, others)

    seen = observed.reshape(own, frames, width)

    smem = pl.BlockSpec(memory_space=pltpu.SMEM)
    vmem = pl.BlockSpec(memory_space=pltpu.VMEM)

    def shape(count, kind):
        return jax.ShapeDtypeStruct((count, frames, width), kind)

    def place(output):
        return vmem if len(output.shape) > 1 else smem

    def call(kernel, name, inputs, scalars, outputs, scratch=(), flops=0):
        return pl.pallas_call(
            kernel,
            out_shape=outputs,
            in_specs=[smem] * scalars + [vmem] * (len(inputs) - scalars),
            out_specs=jax.tree.map(place, outputs),
            scratch_shapes=list(scratch),
            compiler_params=pltpu.CompilerParams(vmem_limit_bytes=24 << 20),
            cost_estimate=pl.CostEstimate(flops=flops, bytes_accessed=1 << 20, transcendentals=0),
            name=name,
        )(*inputs)

    low_scratch = pltpu.VMEM((extended + 1, frames, width), jnp.bfloat16)
    rlow_scratch = pltpu.VMEM((own + 1, frames, width), jnp.bfloat16)
    residual_scratch = pltpu.VMEM((own + 1, frames, width), jnp.float32)
    work = 4 * slots * frames * width * width

    def step_outputs(last):
        sent = tile_x + 2 if last else 2 * (tile_x + 2)
        outputs = [
            shape(extended, jnp.float32),
            shape(extended + 1, jnp.float32),
            shape(sent, jnp.bfloat16),
            shape(sent, jnp.bfloat16),
        ]
        return outputs + [shape(own + 1, jnp.float32)] if last else outputs

    top, bottom = lax.optimization_barrier((coefficients[0], coefficients[tile_x - 1]))
    far_row, near = along_narrow(
        cast_low(jnp.where(row_even, top, bottom)), cast_low(jnp.where(row_even, bottom, top))
    )
    in_hbm = pltpu.with_memory_space_constraint
    chunks = 4
    half = slots // 2
    stay = pl.BlockSpec(memory_space=pltpu.HBM)
    matrices = in_hbm(blocks.reshape(slots, width, width), pltpu.HBM)
    half_shape = pltpu.VMEM((half, width, width), jnp.bfloat16)
    options = dict(
        scratch_shapes=[pltpu.SemaphoreType.DMA((chunks,))],
        compiler_params=pltpu.CompilerParams(vmem_limit_bytes=24 << 20),
        cost_estimate=pl.CostEstimate(flops=work, bytes_accessed=4 << 20, transcendentals=0),
    )
    info, row_ids, col_ids, first_blocks = pl.pallas_call(
        functools.partial(plan_kernel, sizes),
        out_shape=[
            pltpu.SMEM((LIVE + 1,), jnp.int32),
            pltpu.SMEM((slots,), jnp.int32),
            pltpu.SMEM((slots,), jnp.int32),
            half_shape,
        ],
        in_specs=[smem] * 4 + [stay],
        out_specs=[smem] * 3 + [vmem],
        name="plan_slots",
        **options,
    )(
        flags,
        live_count.reshape(1),
        in_hbm(block_rows.reshape(slots), pltpu.HBM),
        in_hbm(block_cols.reshape(slots), pltpu.HBM),
        matrices,
    )
    first_turned, second_blocks, second_turned = pl.pallas_call(
        turn_kernel,
        out_shape=[half_shape] * 3,
        in_specs=[smem, vmem, stay],
        out_specs=[vmem] * 3,
        name="turn_blocks",
        **options,
    )(info, first_blocks, matrices)
    operator = [first_blocks, second_blocks, first_turned, second_turned]
    near, far_row, info = lax.optimization_barrier((near, far_row, info))
    above = jnp.where(row_even, far_row, near)
    below = jnp.where(row_even, near, far_row)
    left, right = lax.optimization_barrier((coefficients[:, 0], coefficients[:, tile_y - 1]))
    left, right = cast_low(left), cast_low(right)
    sides = []
    for col, edge in ((0, left), (tile_y - 1, right)):
        sides.append(jnp.concatenate([above[col : col + 1], edge, below[col : col + 1]], axis=0))
    pair_out, next_out = lax.optimization_barrier(
        (jnp.where(even, sides[1], sides[0]), jnp.where(even, sides[0], sides[1]))
    )
    pair_in, next_in = along_wide(pair_out, next_out)
    x, grad, pair_out, next_out = call(
        functools.partial(first_kernel, sizes),
        "first_step",
        [info, row_ids, col_ids, coefficients.reshape(own, frames, width), far_row, near, pair_in, next_in, seen, *operator],
        3,
        step_outputs(False),
        [low_scratch, rlow_scratch, residual_scratch],
        work,
    )
    for iteration in range(ITERS):
        last = iteration == ITERS - 1
        pair_in, next_in = along_wide(pair_out, next_out)
        rows_sent = tile_y if last else 2 * span
        far_row, near = call(
            functools.partial(fold_kernel, sizes, last),
            "fold_columns",
            [info, grad, pair_in, next_in],
            1,
            [shape(rows_sent, jnp.bfloat16), shape(rows_sent, jnp.bfloat16)],
        )
        far_row, near = along_narrow(far_row, near)
        if last:
            updated = call(
                functools.partial(final_kernel, sizes),
                "final_update",
                [info, x, grad, pair_in, next_in, far_row, near],
                1,
                shape(own, jnp.float32),
            )
        else:
            ending = iteration == ITERS - 2
            x, grad, pair_out, next_out, *rest = call(
                functools.partial(step_kernel, sizes, ending),
                "one_step",
                [info, row_ids, col_ids, x, grad, pair_in, next_in, far_row, near, seen, *operator],
                3,
                step_outputs(ending),
                [low_scratch, rlow_scratch] + ([] if ending else [residual_scratch]),
                work,
            )
    residual = rest[0]
    return (
        updated.reshape(coefficients.shape),
        residual[:own].reshape(coefficients.shape),
    )


def solution(mesh):
    placed = (
        P("narrow", "wide", None, None),
        P("narrow", "wide", None, None),
        P("narrow", "wide", None, None, None),
        P("narrow", "wide", None),
        P("narrow", "wide", None),
        P("narrow", "wide"),
    )
    return jax.shard_map(
        local,
        mesh=mesh,
        in_specs=placed,
        out_specs=(P("narrow", "wide", None, None), P("narrow", "wide", None, None)),
        check_vma=False,
    )
```

```python
import functools

import jax
import jax.numpy as jnp
from jax import lax
from jax.experimental import pallas as pl
from jax.experimental.pallas import tpu as pltpu
from jax.sharding import PartitionSpec as P

ITERS = 5
descent = 0.1

ROW_FIRST, ROW_LAST, COL_FIRST, COL_LAST, EVEN, ROW_EVEN, LIVE = range(7)


def cast_low(value):
    return value.astype(jnp.bfloat16)


def wide_value(value):
    return value.astype(jnp.float32)


def kept(value, drop):
    return jnp.where(drop, jnp.zeros_like(value), value)


def half_step(source_ref, blocks, total_ref, source_ids, target_ids, live):
    def add(first, blocks_ref):
        for at in range(0, blocks_ref.shape[0], 2):
            slot = first + at
            upper = source_ref[source_ids[slot]]
            lower = source_ref[source_ids[slot + 1]]
            frames, width = upper.shape
            zeros = jnp.zeros_like(upper)
            taken = jnp.concatenate(
                [jnp.concatenate([upper, zeros], axis=1), jnp.concatenate([zeros, lower], axis=1)],
                axis=0,
            )
            matrices = blocks_ref[pl.ds(at, 2)].reshape(2 * width, width)
            product = jnp.dot(taken, matrices, preferred_element_type=jnp.float32)
            target = target_ids[slot]
            total_ref[target] = total_ref[target] + product[:frames]
            target = target_ids[slot + 1]
            total_ref[target] = total_ref[target] + product[frames:]

    first_ref, second_ref = blocks
    half = first_ref.shape[0]
    add(0, first_ref)

    @pl.when(live > half)
    def _():
        add(half, second_ref)


def products(sizes, info_ref, rows_ref, cols_ref, observed_ref, blocks, turned, grad_ref, residual_ref, low_ref, rlow_ref):
    tile_x, tile_y, _ = sizes
    own = tile_x * tile_y
    extended = (tile_x + 2) * (tile_y + 2)
    low_ref[extended] = jnp.zeros_like(low_ref[extended])
    for block in range(own):
        residual_ref[block] = -observed_ref[block]
    residual_ref[own] = jnp.zeros_like(residual_ref[own])
    half_step(low_ref, blocks, residual_ref, cols_ref, rows_ref, info_ref[LIVE])
    for block in range(own + 1):
        rlow_ref[block] = cast_low(residual_ref[block])
    for block in range(extended + 1):
        grad_ref[block] = jnp.zeros_like(grad_ref[block])
    half_step(rlow_ref, turned, grad_ref, rows_ref, cols_ref, info_ref[LIVE])


def send_columns(sizes, last, info_ref, grad_ref, pair_ref, next_ref):
    tile_x, tile_y, _ = sizes
    span = tile_y + 2
    even = info_ref[EVEN] == 1
    for out_ref, right in ((pair_ref, even), (next_ref, jnp.logical_not(even))):
        if last:
            col = jnp.where(right, span - 1, 0)
            for row in range(tile_x + 2):
                out_ref[row] = cast_low(grad_ref[row * span + col])
        else:
            col = jnp.where(right, span - 2, 0)
            for row in range(tile_x + 2):
                for step in range(2):
                    out_ref[row * 2 + step] = cast_low(grad_ref[row * span + col + step])


def outside(sizes, info_ref, row, col):
    tile_x, tile_y, _ = sizes
    flag = None
    for hit, place in (
        (row == 0, ROW_FIRST),
        (row == tile_x + 1, ROW_LAST),
        (col == 0, COL_FIRST),
        (col == tile_y + 1, COL_LAST),
    ):
        if hit:
            here = info_ref[place] == 1
            flag = here if flag is None else jnp.logical_or(flag, here)
    return flag


def came_along_wide(sizes, last, info_ref, pair_in, next_in, row, col):
    tile_x, tile_y, _ = sizes
    even = info_ref[EVEN] == 1
    width = 1 if last else 2
    lefts = {1: 0} if last else {0: 0, 1: 1}
    rights = {tile_y: 0} if last else {tile_y: 0, tile_y + 1: 1}
    for places, from_pair, place in (
        (lefts, jnp.logical_not(even), COL_FIRST),
        (rights, even, COL_LAST),
    ):
        if col in places:
            at = row * width + places[col]
            came = jnp.where(from_pair, pair_in[at], next_in[at])
            return kept(wide_value(came), info_ref[place] == 1)
    return None


def bring(blocks_in, blocks_ref, arrived, chunk, first):
    size = blocks_ref.shape[0] // arrived.shape[0]
    return pltpu.make_async_copy(
        blocks_in.at[pl.ds(first + chunk * size, size)],
        blocks_ref.at[pl.ds(chunk * size, size)],
        arrived.at[chunk],
    )


def plan_kernel(sizes, flags_ref, live_ref, rows_in, cols_in, blocks_in, info_ref, rows_ref, cols_ref, first_blocks, arrived):
    tile_x, tile_y, slots = sizes
    for chunk in range(arrived.shape[0]):
        bring(blocks_in, first_blocks, arrived, chunk, 0).start()
    live = live_ref[0]
    for place in range(LIVE):
        info_ref[place] = flags_ref[place]
    info_ref[LIVE] = live
    group = 8

    def copy(step, carry):
        for place in range(group):
            slot = step * group + place
            used = slot < live
            rows_ref[slot] = jnp.where(used, rows_in[slot], tile_x * tile_y)
            cols_ref[slot] = jnp.where(used, cols_in[slot], (tile_x + 2) * (tile_y + 2))
        return carry

    lax.fori_loop(0, slots // group, copy, 0)
    for chunk in range(arrived.shape[0]):
        bring(blocks_in, first_blocks, arrived, chunk, 0).wait()


def turn_kernel(info_ref, first_blocks, blocks_in, first_turned, second_blocks, second_turned, arrived):
    half = first_blocks.shape[0]
    more = info_ref[LIVE] > half

    @pl.when(more)
    def _():
        for chunk in range(arrived.shape[0]):
            bring(blocks_in, second_blocks, arrived, chunk, half).start()

    for slot in range(half):
        first_turned[slot] = first_blocks[slot].T

    @pl.when(more)
    def _():
        size = half // arrived.shape[0]
        for chunk in range(arrived.shape[0]):
            bring(blocks_in, second_blocks, arrived, chunk, half).wait()
            for slot in range(chunk * size, (chunk + 1) * size):
                second_turned[slot] = second_blocks[slot].T


def first_kernel(sizes, info_ref, rows_ref, cols_ref, coef_ref, near_in, far_in, next_in, pair_in, observed_ref, first_blocks, second_blocks, first_turned, second_turned, x_ref, grad_ref, next_ref, pair_ref, low_ref, rlow_ref, residual_ref):
    tile_x, tile_y, _ = sizes
    span = tile_y + 2
    even = info_ref[EVEN] == 1
    for row in range(tile_x + 2):
        for col in range(span):
            if col == 0:
                value = wide_value(jnp.where(even, next_in[row], pair_in[row]))
            elif col == tile_y + 1:
                value = wide_value(jnp.where(even, pair_in[row], next_in[row]))
            elif row == 0:
                value = came_along_narrow(info_ref, near_in, far_in, True, col - 1)
            elif row == tile_x + 1:
                value = came_along_narrow(info_ref, near_in, far_in, False, col - 1)
            else:
                value = coef_ref[(row - 1) * tile_y + col - 1]
            drop = outside(sizes, info_ref, row, col)
            if drop is not None:
                value = kept(value, drop)
            x_ref[row * span + col] = value
            low_ref[row * span + col] = cast_low(value)
    products(sizes, info_ref, rows_ref, cols_ref, observed_ref, (first_blocks, second_blocks), (first_turned, second_turned), grad_ref, residual_ref, low_ref, rlow_ref)
    send_columns(sizes, False, info_ref, grad_ref, pair_ref, next_ref)


def step_kernel(sizes, last, info_ref, rows_ref, cols_ref, x_in, grad_in, next_in, pair_in, near_in, far_in, observed_ref, first_blocks, second_blocks, first_turned, second_turned, x_ref, grad_ref, next_ref, pair_ref, *rest):
    tile_x, tile_y, _ = sizes
    span = tile_y + 2
    if last:
        residual_ref, low_ref, rlow_ref = rest
    else:
        low_ref, rlow_ref, residual_ref = rest
    for row in range(tile_x + 2):
        for col in range(span):
            at = row * span + col
            gradient = grad_in[at]
            came = came_along_wide(sizes, False, info_ref, pair_in, next_in, row, col)
            if came is not None:
                gradient = gradient + came
            if row < 2:
                gradient = gradient + came_along_narrow(info_ref, near_in, far_in, True, at)
            elif row >= tile_x:
                gradient = gradient + came_along_narrow(info_ref, near_in, far_in, False, at - tile_x * span)
            value = x_in[at] - descent * gradient
            drop = outside(sizes, info_ref, row, col)
            if drop is not None:
                value = kept(value, drop)
            x_ref[at] = value
            low_ref[at] = cast_low(value)
    products(sizes, info_ref, rows_ref, cols_ref, observed_ref, (first_blocks, second_blocks), (first_turned, second_turned), grad_ref, residual_ref, low_ref, rlow_ref)
    send_columns(sizes, last, info_ref, grad_ref, pair_ref, next_ref)


def came_along_narrow(info_ref, near_in, far_in, upper, at):
    even = info_ref[ROW_EVEN] == 1
    from_near = jnp.logical_not(even) if upper else even
    came = jnp.where(from_near, near_in[at], far_in[at])
    return wide_value(kept(came, info_ref[ROW_FIRST if upper else ROW_LAST] == 1))


def fold_kernel(sizes, last, info_ref, grad_in, next_in, pair_in, near_ref, far_ref):
    tile_x, tile_y, _ = sizes
    span = tile_y + 2
    even = info_ref[ROW_EVEN] == 1

    def folded(row, col):
        value = grad_in[row * span + col]
        came = came_along_wide(sizes, last, info_ref, pair_in, next_in, row, col)
        return cast_low(value if came is None else value + came)

    for out_ref, lower in ((near_ref, even), (far_ref, jnp.logical_not(even))):
        if last:
            row = jnp.where(lower, tile_x + 1, 0)
            for col in range(1, tile_y + 1):
                out_ref[col - 1] = folded(row, col)
        else:
            row = jnp.where(lower, tile_x, 0)
            for step in range(2):
                for col in range(span):
                    out_ref[step * span + col] = folded(row + step, col)


def final_kernel(sizes, info_ref, x_in, grad_in, next_in, pair_in, near_in, far_in, out_ref):
    tile_x, tile_y, _ = sizes
    span = tile_y + 2
    for row in range(1, tile_x + 1):
        for col in range(1, tile_y + 1):
            at = row * span + col
            gradient = grad_in[at]
            came = came_along_wide(sizes, True, info_ref, pair_in, next_in, row, col)
            if came is not None:
                gradient = gradient + came
            if row == 1:
                gradient = gradient + came_along_narrow(info_ref, near_in, far_in, True, col - 1)
            if row == tile_x:
                gradient = gradient + came_along_narrow(info_ref, near_in, far_in, False, col - 1)
            out_ref[(row - 1) * tile_y + col - 1] = x_in[at] - descent * gradient


def local(coefficients, observed, blocks, block_rows, block_cols, live_count):
    tile_x, tile_y, frames, width = coefficients.shape
    slots = blocks.shape[2]
    own = tile_x * tile_y
    span = tile_y + 2
    extended = (tile_x + 2) * span
    sizes = (tile_x, tile_y, slots)
    narrow = lax.axis_size("narrow")
    wide = lax.axis_size("wide")
    a = lax.axis_index("narrow")
    b = lax.axis_index("wide")
    flags = jnp.stack([a == 0, a == narrow - 1, b == 0, b == wide - 1, b % 2 == 0, a % 2 == 0]).astype(jnp.int32)
    even = b % 2 == 0
    row_even = a % 2 == 0

    def everywhere(move):
        return [
            (i * narrow + j, to_i * narrow + to_j)
            for i in range(wide)
            for j in range(narrow)
            for to_i, to_j in [move(i, j)]
        ]

    def other(i, j):
        return (i, j ^ 1) if i in (0, wide - 1) else (((i - 1) ^ 1) + 1, j)

    def far(i, j):
        return (i ^ 1, j) if j in (0, narrow - 1) else (i, ((j - 1) ^ 1) + 1)

    near_pairs = everywhere(lambda i, j: (i, j ^ 1))
    far_pairs = everywhere(far)
    pairs = everywhere(lambda i, j: (i ^ 1, j))
    others = everywhere(other)

    def send(value, ring):
        return lax.ppermute(value, ("wide", "narrow"), ring)

    def along_narrow(near, far):
        return send(near, near_pairs), send(far, far_pairs)

    def along_wide(other, pair):
        return send(other, others), send(pair, pairs)

    seen = observed.reshape(own, frames, width)

    smem = pl.BlockSpec(memory_space=pltpu.SMEM)
    vmem = pl.BlockSpec(memory_space=pltpu.VMEM)

    def shape(count, kind):
        return jax.ShapeDtypeStruct((count, frames, width), kind)

    def place(output):
        return vmem if len(output.shape) > 1 else smem

    def call(kernel, name, inputs, scalars, outputs, scratch=(), flops=0):
        return pl.pallas_call(
            kernel,
            out_shape=outputs,
            in_specs=[smem] * scalars + [vmem] * (len(inputs) - scalars),
            out_specs=jax.tree.map(place, outputs),
            scratch_shapes=list(scratch),
            compiler_params=pltpu.CompilerParams(vmem_limit_bytes=24 << 20),
            cost_estimate=pl.CostEstimate(flops=flops, bytes_accessed=1 << 20, transcendentals=0),
            name=name,
        )(*inputs)

    low_scratch = pltpu.VMEM((extended + 1, frames, width), jnp.bfloat16)
    rlow_scratch = pltpu.VMEM((own + 1, frames, width), jnp.bfloat16)
    residual_scratch = pltpu.VMEM((own + 1, frames, width), jnp.float32)
    work = 4 * slots * frames * width * width

    def step_outputs(last):
        sent = tile_x + 2 if last else 2 * (tile_x + 2)
        outputs = [
            shape(extended, jnp.float32),
            shape(extended + 1, jnp.float32),
            shape(sent, jnp.bfloat16),
            shape(sent, jnp.bfloat16),
        ]
        return outputs + [shape(own + 1, jnp.float32)] if last else outputs

    top, bottom = lax.optimization_barrier((coefficients[0], coefficients[tile_x - 1]))
    near, far_row = lax.optimization_barrier(
        (cast_low(jnp.where(row_even, bottom, top)), cast_low(jnp.where(row_even, top, bottom)))
    )
    near, far_row = along_narrow(near, far_row)
    in_hbm = pltpu.with_memory_space_constraint
    chunks = 4
    half = slots // 2
    stay = pl.BlockSpec(memory_space=pltpu.HBM)
    matrices = in_hbm(blocks.reshape(slots, width, width), pltpu.HBM)
    half_shape = pltpu.VMEM((half, width, width), jnp.bfloat16)
    options = dict(
        scratch_shapes=[pltpu.SemaphoreType.DMA((chunks,))],
        compiler_params=pltpu.CompilerParams(vmem_limit_bytes=24 << 20),
        cost_estimate=pl.CostEstimate(flops=work, bytes_accessed=4 << 20, transcendentals=0),
    )
    info, row_ids, col_ids, first_blocks = pl.pallas_call(
        functools.partial(plan_kernel, sizes),
        out_shape=[
            pltpu.SMEM((LIVE + 1,), jnp.int32),
            pltpu.SMEM((slots,), jnp.int32),
            pltpu.SMEM((slots,), jnp.int32),
            half_shape,
        ],
        in_specs=[smem] * 4 + [stay],
        out_specs=[smem] * 3 + [vmem],
        name="plan_slots",
        **options,
    )(
        flags,
        live_count.reshape(1),
        in_hbm(block_rows.reshape(slots), pltpu.HBM),
        in_hbm(block_cols.reshape(slots), pltpu.HBM),
        matrices,
    )
    first_turned, second_blocks, second_turned = pl.pallas_call(
        turn_kernel,
        out_shape=[half_shape] * 3,
        in_specs=[smem, vmem, stay],
        out_specs=[vmem] * 3,
        name="turn_blocks",
        **options,
    )(info, first_blocks, matrices)
    operator = [first_blocks, second_blocks, first_turned, second_turned]
    near, far_row, info = lax.optimization_barrier((near, far_row, info))
    above = jnp.where(row_even, far_row, near)
    below = jnp.where(row_even, near, far_row)
    left, right = lax.optimization_barrier((coefficients[:, 0], coefficients[:, tile_y - 1]))
    left, right = cast_low(left), cast_low(right)
    sides = []
    for col, edge in ((0, left), (tile_y - 1, right)):
        sides.append(jnp.concatenate([above[col : col + 1], edge, below[col : col + 1]], axis=0))
    next_out, pair_out = lax.optimization_barrier(
        (jnp.where(even, sides[0], sides[1]), jnp.where(even, sides[1], sides[0]))
    )
    next_in, pair_in = along_wide(next_out, pair_out)
    x, grad, next_out, pair_out = call(
        functools.partial(first_kernel, sizes),
        "first_step",
        [info, row_ids, col_ids, coefficients.reshape(own, frames, width), near, far_row, next_in, pair_in, seen, *operator],
        3,
        step_outputs(False),
        [low_scratch, rlow_scratch, residual_scratch],
        work,
    )
    for iteration in range(ITERS):
        last = iteration == ITERS - 1
        next_in, pair_in = along_wide(next_out, pair_out)
        rows_sent = tile_y if last else 2 * span
        near, far_row = call(
            functools.partial(fold_kernel, sizes, last),
            "fold_columns",
            [info, grad, next_in, pair_in],
            1,
            [shape(rows_sent, jnp.bfloat16), shape(rows_sent, jnp.bfloat16)],
        )
        near, far_row = along_narrow(near, far_row)
        if last:
            updated = call(
                functools.partial(final_kernel, sizes),
                "final_update",
                [info, x, grad, next_in, pair_in, near, far_row],
                1,
                shape(own, jnp.float32),
            )
        else:
            ending = iteration == ITERS - 2
            x, grad, next_out, pair_out, *rest = call(
                functools.partial(step_kernel, sizes, ending),
                "one_step",
                [info, row_ids, col_ids, x, grad, next_in, pair_in, near, far_row, seen, *operator],
                3,
                step_outputs(ending),
                [low_scratch, rlow_scratch] + ([] if ending else [residual_scratch]),
                work,
            )
    residual = rest[0]
    return (
        updated.reshape(coefficients.shape),
        residual[:own].reshape(coefficients.shape),
    )


def solution(mesh):
    placed = (
        P("narrow", "wide", None, None),
        P("narrow", "wide", None, None),
        P("narrow", "wide", None, None, None),
        P("narrow", "wide", None),
        P("narrow", "wide", None),
        P("narrow", "wide"),
    )
    return jax.shard_map(
        local,
        mesh=mesh,
        in_specs=placed,
        out_specs=(P("narrow", "wide", None, None), P("narrow", "wide", None, None)),
        check_vma=False,
    )
```

```python
import functools

import jax
import jax.numpy as jnp
from jax import lax
from jax.experimental import pallas as pl
from jax.experimental.pallas import tpu as pltpu
from jax.sharding import PartitionSpec as P

ITERS = 5
descent = 0.1

ROW_FIRST, ROW_LAST, COL_FIRST, COL_LAST, EVEN, ROW_EVEN, LIVE = range(7)


def cast_low(value):
    return value.astype(jnp.bfloat16)


def wide_value(value):
    return value.astype(jnp.float32)


def kept(value, drop):
    return jnp.where(drop, jnp.zeros_like(value), value)


def half_step(source_ref, parts, total_ref, source_ids, target_ids, live, filler=()):
    filler = list(filler)

    def add(first, blocks_ref):
        for at in range(0, blocks_ref.shape[0], 2):
            slot = first + at
            upper = source_ref[source_ids[slot]]
            lower = source_ref[source_ids[slot + 1]]
            frames, width = upper.shape
            zeros = jnp.zeros_like(upper)
            taken = jnp.concatenate(
                [jnp.concatenate([upper, zeros], axis=1), jnp.concatenate([zeros, lower], axis=1)],
                axis=0,
            )
            matrices = blocks_ref[pl.ds(at, 2)].reshape(2 * width, width)
            product = jnp.dot(taken, matrices, preferred_element_type=jnp.float32)
            target = target_ids[slot]
            total_ref[target] = total_ref[target] + product[:frames]
            target = target_ids[slot + 1]
            total_ref[target] = total_ref[target] + product[frames:]
            for work in filler[:2]:
                work()
            del filler[:2]

    first = 0
    for part in parts[:-1]:
        add(first, part)
        first += part.shape[0]
    for work in filler:
        work()
    filler.clear()

    @pl.when(live > first)
    def _():
        add(first, parts[-1])


def products(sizes, info_ref, rows_ref, cols_ref, observed_ref, blocks, turned, grad_ref, residual_ref, low_ref, rlow_ref):
    tile_x, tile_y, _ = sizes
    own = tile_x * tile_y
    extended = (tile_x + 2) * (tile_y + 2)
    low_ref[extended] = jnp.zeros_like(low_ref[extended])
    for block in range(own):
        residual_ref[block] = -observed_ref[block]
    residual_ref[own] = jnp.zeros_like(residual_ref[own])

    def clear(block):
        grad_ref[block] = jnp.zeros_like(grad_ref[block])

    clears = [functools.partial(clear, block) for block in range(extended + 1)]
    half_step(low_ref, blocks, residual_ref, cols_ref, rows_ref, info_ref[LIVE], clears)
    for block in range(own + 1):
        rlow_ref[block] = cast_low(residual_ref[block])
    half_step(rlow_ref, turned, grad_ref, rows_ref, cols_ref, info_ref[LIVE])


def send_columns(sizes, last, info_ref, grad_ref, pair_ref, next_ref):
    tile_x, tile_y, _ = sizes
    span = tile_y + 2
    even = info_ref[EVEN] == 1
    for out_ref, right in ((pair_ref, even), (next_ref, jnp.logical_not(even))):
        if last:
            col = jnp.where(right, span - 1, 0)
            for row in range(tile_x + 2):
                out_ref[row] = cast_low(grad_ref[row * span + col])
        else:
            col = jnp.where(right, span - 2, 0)
            for row in range(tile_x + 2):
                for step in range(2):
                    out_ref[row * 2 + step] = cast_low(grad_ref[row * span + col + step])


def outside(sizes, info_ref, row, col):
    tile_x, tile_y, _ = sizes
    flag = None
    for hit, place in (
        (row == 0, ROW_FIRST),
        (row == tile_x + 1, ROW_LAST),
        (col == 0, COL_FIRST),
        (col == tile_y + 1, COL_LAST),
    ):
        if hit:
            here = info_ref[place] == 1
            flag = here if flag is None else jnp.logical_or(flag, here)
    return flag


def came_along_wide(sizes, last, info_ref, pair_in, next_in, row, col):
    tile_x, tile_y, _ = sizes
    even = info_ref[EVEN] == 1
    width = 1 if last else 2
    lefts = {1: 0} if last else {0: 0, 1: 1}
    rights = {tile_y: 0} if last else {tile_y: 0, tile_y + 1: 1}
    for places, from_pair, place in (
        (lefts, jnp.logical_not(even), COL_FIRST),
        (rights, even, COL_LAST),
    ):
        if col in places:
            at = row * width + places[col]
            came = jnp.where(from_pair, pair_in[at], next_in[at])
            return kept(wide_value(came), info_ref[place] == 1)
    return None


def bring(blocks_in, blocks_ref, arrived, chunk, first):
    size = blocks_ref.shape[0] // arrived.shape[0]
    return pltpu.make_async_copy(
        blocks_in.at[pl.ds(first + chunk * size, size)],
        blocks_ref.at[pl.ds(chunk * size, size)],
        arrived.at[chunk],
    )


def plan_kernel(sizes, flags_ref, live_ref, rows_in, cols_in, blocks_in, info_ref, rows_ref, cols_ref, blocks_0, arrived):
    tile_x, tile_y, slots = sizes
    chunks = arrived.shape[0]
    for chunk in range(chunks):
        bring(blocks_in, blocks_0, arrived, chunk, 0).start()
    live = live_ref[0]
    for place in range(LIVE):
        info_ref[place] = flags_ref[place]
    info_ref[LIVE] = live
    group = 8

    def copy(step, carry):
        for place in range(group):
            slot = step * group + place
            used = slot < live
            rows_ref[slot] = jnp.where(used, rows_in[slot], tile_x * tile_y)
            cols_ref[slot] = jnp.where(used, cols_in[slot], (tile_x + 2) * (tile_y + 2))
        return carry

    lax.fori_loop(0, slots // group, copy, 0)
    for chunk in range(chunks):
        bring(blocks_in, blocks_0, arrived, chunk, 0).wait()


def turn_kernel(info_ref, blocks_0, blocks_in, turned_0, blocks_1, blocks_2, turned_1, arrived_1, arrived_2):
    quarter = blocks_0.shape[0]
    half = turned_0.shape[0]
    more = info_ref[LIVE] > half
    chunks = arrived_1.shape[0]
    for chunk in range(chunks):
        bring(blocks_in, blocks_1, arrived_1, chunk, quarter).start()

    @pl.when(more)
    def _():
        for chunk in range(chunks):
            bring(blocks_in, blocks_2, arrived_2, chunk, half).start()

    for slot in range(quarter):
        turned_0[slot] = blocks_0[slot].T
    size = (half - quarter) // chunks
    for chunk in range(chunks):
        bring(blocks_in, blocks_1, arrived_1, chunk, quarter).wait()
        for slot in range(chunk * size, (chunk + 1) * size):
            turned_0[quarter + slot] = blocks_1[slot].T

    @pl.when(more)
    def _():
        size = half // chunks
        for chunk in range(chunks):
            bring(blocks_in, blocks_2, arrived_2, chunk, half).wait()
            for slot in range(chunk * size, (chunk + 1) * size):
                turned_1[slot] = blocks_2[slot].T


def first_kernel(sizes, info_ref, rows_ref, cols_ref, coef_ref, near_in, far_in, next_in, pair_in, observed_ref, blocks_0, blocks_1, blocks_2, turned_0, turned_1, x_ref, grad_ref, next_ref, pair_ref, low_ref, rlow_ref, residual_ref):
    tile_x, tile_y, _ = sizes
    span = tile_y + 2
    even = info_ref[EVEN] == 1
    for row in range(tile_x + 2):
        for col in range(span):
            if col == 0:
                value = wide_value(jnp.where(even, next_in[row], pair_in[row]))
            elif col == tile_y + 1:
                value = wide_value(jnp.where(even, pair_in[row], next_in[row]))
            elif row == 0:
                value = came_along_narrow(info_ref, near_in, far_in, True, col - 1)
            elif row == tile_x + 1:
                value = came_along_narrow(info_ref, near_in, far_in, False, col - 1)
            else:
                value = coef_ref[(row - 1) * tile_y + col - 1]
            drop = outside(sizes, info_ref, row, col)
            if drop is not None:
                value = kept(value, drop)
            x_ref[row * span + col] = value
            low_ref[row * span + col] = cast_low(value)
    products(sizes, info_ref, rows_ref, cols_ref, observed_ref, (blocks_0, blocks_1, blocks_2), (turned_0, turned_1), grad_ref, residual_ref, low_ref, rlow_ref)
    send_columns(sizes, False, info_ref, grad_ref, pair_ref, next_ref)


def step_kernel(sizes, last, info_ref, rows_ref, cols_ref, x_in, grad_in, next_in, pair_in, near_in, far_in, observed_ref, blocks_0, blocks_1, blocks_2, turned_0, turned_1, x_ref, grad_ref, next_ref, pair_ref, *rest):
    tile_x, tile_y, _ = sizes
    span = tile_y + 2
    if last:
        residual_ref, low_ref, rlow_ref = rest
    else:
        low_ref, rlow_ref, residual_ref = rest
    for row in range(tile_x + 2):
        for col in range(span):
            at = row * span + col
            gradient = grad_in[at]
            came = came_along_wide(sizes, False, info_ref, pair_in, next_in, row, col)
            if came is not None:
                gradient = gradient + came
            if row < 2:
                gradient = gradient + came_along_narrow(info_ref, near_in, far_in, True, at)
            elif row >= tile_x:
                gradient = gradient + came_along_narrow(info_ref, near_in, far_in, False, at - tile_x * span)
            value = x_in[at] - descent * gradient
            drop = outside(sizes, info_ref, row, col)
            if drop is not None:
                value = kept(value, drop)
            x_ref[at] = value
            low_ref[at] = cast_low(value)
    products(sizes, info_ref, rows_ref, cols_ref, observed_ref, (blocks_0, blocks_1, blocks_2), (turned_0, turned_1), grad_ref, residual_ref, low_ref, rlow_ref)
    send_columns(sizes, last, info_ref, grad_ref, pair_ref, next_ref)


def came_along_narrow(info_ref, near_in, far_in, upper, at):
    even = info_ref[ROW_EVEN] == 1
    from_near = jnp.logical_not(even) if upper else even
    came = jnp.where(from_near, near_in[at], far_in[at])
    return wide_value(kept(came, info_ref[ROW_FIRST if upper else ROW_LAST] == 1))


def fold_kernel(sizes, last, info_ref, grad_in, next_in, pair_in, near_ref, far_ref):
    tile_x, tile_y, _ = sizes
    span = tile_y + 2
    even = info_ref[ROW_EVEN] == 1

    def folded(row, col):
        value = grad_in[row * span + col]
        came = came_along_wide(sizes, last, info_ref, pair_in, next_in, row, col)
        return cast_low(value if came is None else value + came)

    for out_ref, lower in ((near_ref, even), (far_ref, jnp.logical_not(even))):
        if last:
            row = jnp.where(lower, tile_x + 1, 0)
            for col in range(1, tile_y + 1):
                out_ref[col - 1] = folded(row, col)
        else:
            row = jnp.where(lower, tile_x, 0)
            for step in range(2):
                for col in range(span):
                    out_ref[step * span + col] = folded(row + step, col)


def final_kernel(sizes, info_ref, x_in, grad_in, next_in, pair_in, near_in, far_in, out_ref):
    tile_x, tile_y, _ = sizes
    span = tile_y + 2
    for row in range(1, tile_x + 1):
        for col in range(1, tile_y + 1):
            at = row * span + col
            gradient = grad_in[at]
            came = came_along_wide(sizes, True, info_ref, pair_in, next_in, row, col)
            if came is not None:
                gradient = gradient + came
            if row == 1:
                gradient = gradient + came_along_narrow(info_ref, near_in, far_in, True, col - 1)
            if row == tile_x:
                gradient = gradient + came_along_narrow(info_ref, near_in, far_in, False, col - 1)
            out_ref[(row - 1) * tile_y + col - 1] = x_in[at] - descent * gradient


def local(coefficients, observed, blocks, block_rows, block_cols, live_count):
    tile_x, tile_y, frames, width = coefficients.shape
    slots = blocks.shape[2]
    own = tile_x * tile_y
    span = tile_y + 2
    extended = (tile_x + 2) * span
    sizes = (tile_x, tile_y, slots)
    narrow = lax.axis_size("narrow")
    wide = lax.axis_size("wide")
    a = lax.axis_index("narrow")
    b = lax.axis_index("wide")
    flags = jnp.stack([a == 0, a == narrow - 1, b == 0, b == wide - 1, b % 2 == 0, a % 2 == 0]).astype(jnp.int32)
    even = b % 2 == 0
    row_even = a % 2 == 0

    def everywhere(move):
        return [
            (i * narrow + j, to_i * narrow + to_j)
            for i in range(wide)
            for j in range(narrow)
            for to_i, to_j in [move(i, j)]
        ]

    def other(i, j):
        return (i, j ^ 1) if i in (0, wide - 1) else (((i - 1) ^ 1) + 1, j)

    def far(i, j):
        return (i ^ 1, j) if j in (0, narrow - 1) else (i, ((j - 1) ^ 1) + 1)

    near_pairs = everywhere(lambda i, j: (i, j ^ 1))
    far_pairs = everywhere(far)
    pairs = everywhere(lambda i, j: (i ^ 1, j))
    others = everywhere(other)

    def send(value, ring):
        return lax.ppermute(value, ("wide", "narrow"), ring)

    def along_narrow(near, far):
        return send(near, near_pairs), send(far, far_pairs)

    def along_wide(other, pair):
        return send(other, others), send(pair, pairs)

    seen = observed.reshape(own, frames, width)

    smem = pl.BlockSpec(memory_space=pltpu.SMEM)
    vmem = pl.BlockSpec(memory_space=pltpu.VMEM)

    def shape(count, kind):
        return jax.ShapeDtypeStruct((count, frames, width), kind)

    def place(output):
        return vmem if len(output.shape) > 1 else smem

    def call(kernel, name, inputs, scalars, outputs, scratch=(), flops=0):
        return pl.pallas_call(
            kernel,
            out_shape=outputs,
            in_specs=[smem] * scalars + [vmem] * (len(inputs) - scalars),
            out_specs=jax.tree.map(place, outputs),
            scratch_shapes=list(scratch),
            compiler_params=pltpu.CompilerParams(vmem_limit_bytes=24 << 20),
            cost_estimate=pl.CostEstimate(flops=flops, bytes_accessed=1 << 20, transcendentals=0),
            name=name,
        )(*inputs)

    low_scratch = pltpu.VMEM((extended + 1, frames, width), jnp.bfloat16)
    rlow_scratch = pltpu.VMEM((own + 1, frames, width), jnp.bfloat16)
    residual_scratch = pltpu.VMEM((own + 1, frames, width), jnp.float32)
    work = 4 * slots * frames * width * width

    def step_outputs(last):
        sent = tile_x + 2 if last else 2 * (tile_x + 2)
        outputs = [
            shape(extended, jnp.float32),
            shape(extended + 1, jnp.float32),
            shape(sent, jnp.bfloat16),
            shape(sent, jnp.bfloat16),
        ]
        return outputs + [shape(own + 1, jnp.float32)] if last else outputs

    top, bottom = lax.optimization_barrier((coefficients[0], coefficients[tile_x - 1]))
    near, far_row = lax.optimization_barrier(
        (cast_low(jnp.where(row_even, bottom, top)), cast_low(jnp.where(row_even, top, bottom)))
    )
    near, far_row = along_narrow(near, far_row)
    in_hbm = pltpu.with_memory_space_constraint
    chunks = 4
    half = slots // 2
    quarter = half // 2
    stay = pl.BlockSpec(memory_space=pltpu.HBM)
    matrices = in_hbm(blocks.reshape(slots, width, width), pltpu.HBM)

    def some(count):
        return pltpu.VMEM((count, width, width), jnp.bfloat16)

    def options(copies):
        return dict(
            scratch_shapes=[pltpu.SemaphoreType.DMA((chunks,))] * copies,
            compiler_params=pltpu.CompilerParams(vmem_limit_bytes=24 << 20),
            cost_estimate=pl.CostEstimate(flops=work, bytes_accessed=4 << 20, transcendentals=0),
        )

    info, row_ids, col_ids, blocks_0 = pl.pallas_call(
        functools.partial(plan_kernel, sizes),
        out_shape=[
            pltpu.SMEM((LIVE + 1,), jnp.int32),
            pltpu.SMEM((slots,), jnp.int32),
            pltpu.SMEM((slots,), jnp.int32),
            some(quarter),
        ],
        in_specs=[smem] * 4 + [stay],
        out_specs=[smem] * 3 + [vmem],
        name="plan_slots",
        **options(1),
    )(
        flags,
        live_count.reshape(1),
        in_hbm(block_rows.reshape(slots), pltpu.HBM),
        in_hbm(block_cols.reshape(slots), pltpu.HBM),
        matrices,
    )
    turned_0, blocks_1, blocks_2, turned_1 = pl.pallas_call(
        turn_kernel,
        out_shape=[some(half), some(half - quarter), some(slots - half), some(slots - half)],
        in_specs=[smem, vmem, stay],
        out_specs=[vmem] * 4,
        name="turn_blocks",
        **options(2),
    )(info, blocks_0, matrices)
    operator = [blocks_0, blocks_1, blocks_2, turned_0, turned_1]
    near, far_row, info = lax.optimization_barrier((near, far_row, info))
    above = jnp.where(row_even, far_row, near)
    below = jnp.where(row_even, near, far_row)
    left, right = lax.optimization_barrier((coefficients[:, 0], coefficients[:, tile_y - 1]))
    left, right = cast_low(left), cast_low(right)
    sides = []
    for col, edge in ((0, left), (tile_y - 1, right)):
        sides.append(jnp.concatenate([above[col : col + 1], edge, below[col : col + 1]], axis=0))
    next_out, pair_out = lax.optimization_barrier(
        (jnp.where(even, sides[0], sides[1]), jnp.where(even, sides[1], sides[0]))
    )
    next_in, pair_in = along_wide(next_out, pair_out)
    x, grad, next_out, pair_out = call(
        functools.partial(first_kernel, sizes),
        "first_step",
        [info, row_ids, col_ids, coefficients.reshape(own, frames, width), near, far_row, next_in, pair_in, seen, *operator],
        3,
        step_outputs(False),
        [low_scratch, rlow_scratch, residual_scratch],
        work,
    )
    for iteration in range(ITERS):
        last = iteration == ITERS - 1
        next_in, pair_in = along_wide(next_out, pair_out)
        rows_sent = tile_y if last else 2 * span
        near, far_row = call(
            functools.partial(fold_kernel, sizes, last),
            "fold_columns",
            [info, grad, next_in, pair_in],
            1,
            [shape(rows_sent, jnp.bfloat16), shape(rows_sent, jnp.bfloat16)],
        )
        near, far_row = along_narrow(near, far_row)
        if last:
            updated = call(
                functools.partial(final_kernel, sizes),
                "final_update",
                [info, x, grad, next_in, pair_in, near, far_row],
                1,
                shape(own, jnp.float32),
            )
        else:
            ending = iteration == ITERS - 2
            x, grad, next_out, pair_out, *rest = call(
                functools.partial(step_kernel, sizes, ending),
                "one_step",
                [info, row_ids, col_ids, x, grad, next_in, pair_in, near, far_row, seen, *operator],
                3,
                step_outputs(ending),
                [low_scratch, rlow_scratch] + ([] if ending else [residual_scratch]),
                work,
            )
    residual = rest[0]
    return (
        updated.reshape(coefficients.shape),
        residual[:own].reshape(coefficients.shape),
    )


def solution(mesh):
    placed = (
        P("narrow", "wide", None, None),
        P("narrow", "wide", None, None),
        P("narrow", "wide", None, None, None),
        P("narrow", "wide", None),
        P("narrow", "wide", None),
        P("narrow", "wide"),
    )
    return jax.shard_map(
        local,
        mesh=mesh,
        in_specs=placed,
        out_specs=(P("narrow", "wide", None, None), P("narrow", "wide", None, None)),
        check_vma=False,
    )
```

```python
import functools

import jax
import jax.numpy as jnp
from jax import lax
from jax.experimental import pallas as pl
from jax.experimental.pallas import tpu as pltpu
from jax.sharding import PartitionSpec as P

ITERS = 5
descent = 0.1

ROW_FIRST, ROW_LAST, COL_FIRST, COL_LAST, EVEN, ROW_EVEN, LIVE = range(7)


def cast_low(value):
    return value.astype(jnp.bfloat16)


def wide_value(value):
    return value.astype(jnp.float32)


def kept(value, drop):
    return jnp.where(drop, jnp.zeros_like(value), value)


def half_step(source_ref, parts, total_ref, source_ids, target_ids, live, filler=()):
    filler = list(filler)

    def add(first, blocks_ref):
        for at in range(0, blocks_ref.shape[0], 2):
            slot = first + at
            upper = source_ref[source_ids[slot]]
            lower = source_ref[source_ids[slot + 1]]
            frames, width = upper.shape
            zeros = jnp.zeros_like(upper)
            taken = jnp.concatenate(
                [jnp.concatenate([upper, zeros], axis=1), jnp.concatenate([zeros, lower], axis=1)],
                axis=0,
            )
            matrices = blocks_ref[pl.ds(at, 2)].reshape(2 * width, width)
            product = jnp.dot(taken, matrices, preferred_element_type=jnp.float32)
            target = target_ids[slot]
            total_ref[target] = total_ref[target] + product[:frames]
            target = target_ids[slot + 1]
            total_ref[target] = total_ref[target] + product[frames:]
            for work in filler[:2]:
                work()
            del filler[:2]

    first = 0
    for part in parts[:-1]:
        add(first, part)
        first += part.shape[0]
    for work in filler:
        work()
    filler.clear()

    @pl.when(live > first)
    def _():
        add(first, parts[-1])


def products(sizes, info_ref, rows_ref, cols_ref, observed_ref, blocks, turned, grad_ref, residual_ref, low_ref, rlow_ref):
    tile_x, tile_y, _ = sizes
    own = tile_x * tile_y
    extended = (tile_x + 2) * (tile_y + 2)
    low_ref[extended] = jnp.zeros_like(low_ref[extended])
    for block in range(own):
        residual_ref[block] = -observed_ref[block]
    residual_ref[own] = jnp.zeros_like(residual_ref[own])

    def clear(block):
        grad_ref[block] = jnp.zeros_like(grad_ref[block])

    clears = [functools.partial(clear, block) for block in range(extended + 1)]
    half_step(low_ref, blocks, residual_ref, cols_ref, rows_ref, info_ref[LIVE], clears)
    for block in range(own + 1):
        rlow_ref[block] = cast_low(residual_ref[block])
    half_step(rlow_ref, turned, grad_ref, rows_ref, cols_ref, info_ref[LIVE])


def send_columns(sizes, last, info_ref, grad_ref, pair_ref, next_ref):
    tile_x, tile_y, _ = sizes
    span = tile_y + 2
    even = info_ref[EVEN] == 1
    for out_ref, right in ((pair_ref, even), (next_ref, jnp.logical_not(even))):
        if last:
            col = jnp.where(right, span - 1, 0)
            for row in range(tile_x + 2):
                out_ref[row] = cast_low(grad_ref[row * span + col])
        else:
            col = jnp.where(right, span - 2, 0)
            for row in range(tile_x + 2):
                for step in range(2):
                    out_ref[row * 2 + step] = cast_low(grad_ref[row * span + col + step])


def outside(sizes, info_ref, row, col):
    tile_x, tile_y, _ = sizes
    flag = None
    for hit, place in (
        (row == 0, ROW_FIRST),
        (row == tile_x + 1, ROW_LAST),
        (col == 0, COL_FIRST),
        (col == tile_y + 1, COL_LAST),
    ):
        if hit:
            here = info_ref[place] == 1
            flag = here if flag is None else jnp.logical_or(flag, here)
    return flag


def came_along_wide(sizes, last, info_ref, pair_in, next_in, row, col):
    tile_x, tile_y, _ = sizes
    even = info_ref[EVEN] == 1
    width = 1 if last else 2
    lefts = {1: 0} if last else {0: 0, 1: 1}
    rights = {tile_y: 0} if last else {tile_y: 0, tile_y + 1: 1}
    for places, from_pair, place in (
        (lefts, jnp.logical_not(even), COL_FIRST),
        (rights, even, COL_LAST),
    ):
        if col in places:
            at = row * width + places[col]
            came = jnp.where(from_pair, pair_in[at], next_in[at])
            return kept(wide_value(came), info_ref[place] == 1)
    return None


def bring(blocks_in, blocks_ref, arrived, chunk, first):
    size = blocks_ref.shape[0] // arrived.shape[0]
    return pltpu.make_async_copy(
        blocks_in.at[pl.ds(first + chunk * size, size)],
        blocks_ref.at[pl.ds(chunk * size, size)],
        arrived.at[chunk],
    )


def plan_kernel(sizes, flags_ref, live_ref, rows_in, cols_in, info_ref, rows_ref, cols_ref):
    tile_x, tile_y, slots = sizes
    live = live_ref[0, 0]
    for place in range(LIVE):
        info_ref[place] = flags_ref[place]
    info_ref[LIVE] = live
    group = 8

    def copy(step, carry):
        for place in range(group):
            slot = step * group + place
            used = slot < live
            rows_ref[slot] = jnp.where(used, rows_in[slot], tile_x * tile_y)
            cols_ref[slot] = jnp.where(used, cols_in[slot], (tile_x + 2) * (tile_y + 2))
        return carry

    lax.fori_loop(0, slots // group, copy, 0)


def turn_kernel(info_ref, blocks_in, blocks_0, blocks_1, turned_0, turned_1, arrived_0, arrived_1):
    half = blocks_0.shape[0]
    chunks = arrived_0.shape[0]
    size = half // chunks
    more = info_ref[LIVE] > half
    for chunk in range(chunks):
        bring(blocks_in, blocks_0, arrived_0, chunk, 0).start()

    @pl.when(more)
    def _():
        for chunk in range(chunks):
            bring(blocks_in, blocks_1, arrived_1, chunk, half).start()

    for chunk in range(chunks):
        bring(blocks_in, blocks_0, arrived_0, chunk, 0).wait()
        for slot in range(chunk * size, (chunk + 1) * size):
            turned_0[slot] = blocks_0[slot].T

    @pl.when(more)
    def _():
        for chunk in range(chunks):
            bring(blocks_in, blocks_1, arrived_1, chunk, half).wait()
            for slot in range(chunk * size, (chunk + 1) * size):
                turned_1[slot] = blocks_1[slot].T


def first_kernel(sizes, info_ref, rows_ref, cols_ref, coef_ref, near_in, far_in, next_in, pair_in, observed_ref, blocks_0, blocks_1, turned_0, turned_1, x_ref, grad_ref, next_ref, pair_ref, low_ref, rlow_ref, residual_ref):
    tile_x, tile_y, _ = sizes
    span = tile_y + 2
    even = info_ref[EVEN] == 1
    for row in range(tile_x + 2):
        for col in range(span):
            if col == 0:
                value = wide_value(jnp.where(even, next_in[row], pair_in[row]))
            elif col == tile_y + 1:
                value = wide_value(jnp.where(even, pair_in[row], next_in[row]))
            elif row == 0:
                value = came_along_narrow(info_ref, near_in, far_in, True, col - 1)
            elif row == tile_x + 1:
                value = came_along_narrow(info_ref, near_in, far_in, False, col - 1)
            else:
                value = coef_ref[(row - 1) * tile_y + col - 1]
            drop = outside(sizes, info_ref, row, col)
            if drop is not None:
                value = kept(value, drop)
            x_ref[row * span + col] = value
            low_ref[row * span + col] = cast_low(value)
    products(sizes, info_ref, rows_ref, cols_ref, observed_ref, (blocks_0, blocks_1), (turned_0, turned_1), grad_ref, residual_ref, low_ref, rlow_ref)
    send_columns(sizes, False, info_ref, grad_ref, pair_ref, next_ref)


def step_kernel(sizes, last, info_ref, rows_ref, cols_ref, x_in, grad_in, next_in, pair_in, near_in, far_in, observed_ref, blocks_0, blocks_1, turned_0, turned_1, x_ref, grad_ref, next_ref, pair_ref, *rest):
    tile_x, tile_y, _ = sizes
    span = tile_y + 2
    if last:
        residual_ref, low_ref, rlow_ref = rest
    else:
        low_ref, rlow_ref, residual_ref = rest
    for row in range(tile_x + 2):
        for col in range(span):
            at = row * span + col
            gradient = grad_in[at]
            came = came_along_wide(sizes, False, info_ref, pair_in, next_in, row, col)
            if came is not None:
                gradient = gradient + came
            if row < 2:
                gradient = gradient + came_along_narrow(info_ref, near_in, far_in, True, at)
            elif row >= tile_x:
                gradient = gradient + came_along_narrow(info_ref, near_in, far_in, False, at - tile_x * span)
            value = x_in[at] - descent * gradient
            drop = outside(sizes, info_ref, row, col)
            if drop is not None:
                value = kept(value, drop)
            x_ref[at] = value
            low_ref[at] = cast_low(value)
    products(sizes, info_ref, rows_ref, cols_ref, observed_ref, (blocks_0, blocks_1), (turned_0, turned_1), grad_ref, residual_ref, low_ref, rlow_ref)
    send_columns(sizes, last, info_ref, grad_ref, pair_ref, next_ref)


def came_along_narrow(info_ref, near_in, far_in, upper, at):
    even = info_ref[ROW_EVEN] == 1
    from_near = jnp.logical_not(even) if upper else even
    came = jnp.where(from_near, near_in[at], far_in[at])
    return wide_value(kept(came, info_ref[ROW_FIRST if upper else ROW_LAST] == 1))


def fold_kernel(sizes, last, info_ref, grad_in, next_in, pair_in, near_ref, far_ref):
    tile_x, tile_y, _ = sizes
    span = tile_y + 2
    even = info_ref[ROW_EVEN] == 1

    def folded(row, col):
        value = grad_in[row * span + col]
        came = came_along_wide(sizes, last, info_ref, pair_in, next_in, row, col)
        return cast_low(value if came is None else value + came)

    for out_ref, lower in ((near_ref, even), (far_ref, jnp.logical_not(even))):
        if last:
            row = jnp.where(lower, tile_x + 1, 0)
            for col in range(1, tile_y + 1):
                out_ref[col - 1] = folded(row, col)
        else:
            row = jnp.where(lower, tile_x, 0)
            for step in range(2):
                for col in range(span):
                    out_ref[step * span + col] = folded(row + step, col)


def final_kernel(sizes, rows, info_ref, x_in, grad_in, next_in, pair_in, *rest):
    tile_x, tile_y, _ = sizes
    span = tile_y + 2
    if len(rest) > 3:
        near_in, far_in, _, out_ref, part_ref, sent = rest
    else:
        out_ref, part_ref, sent = rest
    copies = []
    for place, row in enumerate(rows):
        for col in range(1, tile_y + 1):
            at = row * span + col
            gradient = grad_in[at]
            came = came_along_wide(sizes, True, info_ref, pair_in, next_in, row, col)
            if came is not None:
                gradient = gradient + came
            if row == 1:
                gradient = gradient + came_along_narrow(info_ref, near_in, far_in, True, col - 1)
            if row == tile_x:
                gradient = gradient + came_along_narrow(info_ref, near_in, far_in, False, col - 1)
            part_ref[place, col - 1] = x_in[at] - descent * gradient
        copies.append(pltpu.make_async_copy(part_ref.at[place], out_ref.at[row - 1], sent.at[place]))
        copies[-1].start()
    for copy in copies:
        copy.wait()


def local(coefficients, observed, blocks, block_rows, block_cols, live_count):
    tile_x, tile_y, frames, width = coefficients.shape
    slots = blocks.shape[2]
    own = tile_x * tile_y
    span = tile_y + 2
    extended = (tile_x + 2) * span
    sizes = (tile_x, tile_y, slots)
    narrow = lax.axis_size("narrow")
    wide = lax.axis_size("wide")
    a = lax.axis_index("narrow")
    b = lax.axis_index("wide")
    flags = jnp.stack([a == 0, a == narrow - 1, b == 0, b == wide - 1, b % 2 == 0, a % 2 == 0]).astype(jnp.int32)
    even = b % 2 == 0
    row_even = a % 2 == 0

    def everywhere(move):
        return [
            (i * narrow + j, to_i * narrow + to_j)
            for i in range(wide)
            for j in range(narrow)
            for to_i, to_j in [move(i, j)]
        ]

    def other(i, j):
        return (i, j ^ 1) if i in (0, wide - 1) else (((i - 1) ^ 1) + 1, j)

    def far(i, j):
        return (i ^ 1, j) if j in (0, narrow - 1) else (i, ((j - 1) ^ 1) + 1)

    near_pairs = everywhere(lambda i, j: (i, j ^ 1))
    far_pairs = everywhere(far)
    pairs = everywhere(lambda i, j: (i ^ 1, j))
    others = everywhere(other)

    def send(value, ring):
        return lax.ppermute(value, ("wide", "narrow"), ring)

    def along_narrow(near, far):
        return send(near, near_pairs), send(far, far_pairs)

    def along_wide(other, pair):
        return send(other, others), send(pair, pairs)

    seen = observed.reshape(own, frames, width)

    smem = pl.BlockSpec(memory_space=pltpu.SMEM)
    vmem = pl.BlockSpec(memory_space=pltpu.VMEM)

    def shape(count, kind):
        return jax.ShapeDtypeStruct((count, frames, width), kind)

    def place(output):
        return vmem if len(output.shape) > 1 else smem

    def call(kernel, name, inputs, scalars, outputs, scratch=(), flops=0):
        return pl.pallas_call(
            kernel,
            out_shape=outputs,
            in_specs=[smem] * scalars + [vmem] * (len(inputs) - scalars),
            out_specs=jax.tree.map(place, outputs),
            scratch_shapes=list(scratch),
            compiler_params=pltpu.CompilerParams(vmem_limit_bytes=24 << 20),
            cost_estimate=pl.CostEstimate(flops=flops, bytes_accessed=1 << 20, transcendentals=0),
            name=name,
        )(*inputs)

    low_scratch = pltpu.VMEM((extended + 1, frames, width), jnp.bfloat16)
    rlow_scratch = pltpu.VMEM((own + 1, frames, width), jnp.bfloat16)
    residual_scratch = pltpu.VMEM((own + 1, frames, width), jnp.float32)
    work = 4 * slots * frames * width * width

    def step_outputs(last):
        sent = tile_x + 2 if last else 2 * (tile_x + 2)
        outputs = [
            shape(extended, jnp.float32),
            shape(extended + 1, jnp.float32),
            shape(sent, jnp.bfloat16),
            shape(sent, jnp.bfloat16),
        ]
        return outputs + [shape(own + 1, jnp.float32)] if last else outputs

    top, bottom = lax.optimization_barrier((coefficients[0], coefficients[tile_x - 1]))
    near, far_row = lax.optimization_barrier(
        (cast_low(jnp.where(row_even, bottom, top)), cast_low(jnp.where(row_even, top, bottom)))
    )
    near, far_row = along_narrow(near, far_row)
    in_hbm = pltpu.with_memory_space_constraint
    info, row_ids, col_ids = pl.pallas_call(
        functools.partial(plan_kernel, sizes),
        out_shape=[
            pltpu.SMEM((LIVE + 1,), jnp.int32),
            pltpu.SMEM((slots,), jnp.int32),
            pltpu.SMEM((slots,), jnp.int32),
        ],
        in_specs=[smem] * 4,
        out_specs=[smem] * 3,
        compiler_params=pltpu.CompilerParams(vmem_limit_bytes=24 << 20),
        cost_estimate=pl.CostEstimate(flops=work, bytes_accessed=1 << 20, transcendentals=0),
        name="plan_slots",
    )(
        flags,
        live_count,
        in_hbm(block_rows.reshape(slots), pltpu.HBM),
        in_hbm(block_cols.reshape(slots), pltpu.HBM),
    )
    chunks = 4
    half_shape = pltpu.VMEM((slots // 2, width, width), jnp.bfloat16)
    operator = pl.pallas_call(
        turn_kernel,
        out_shape=[half_shape] * 4,
        in_specs=[smem, pl.BlockSpec(memory_space=pltpu.HBM)],
        out_specs=[vmem] * 4,
        scratch_shapes=[pltpu.SemaphoreType.DMA((chunks,))] * 2,
        compiler_params=pltpu.CompilerParams(vmem_limit_bytes=24 << 20),
        cost_estimate=pl.CostEstimate(flops=work, bytes_accessed=4 << 20, transcendentals=0),
        name="turn_blocks",
    )(info, in_hbm(blocks.reshape(slots, width, width), pltpu.HBM))
    near, far_row, info = lax.optimization_barrier((near, far_row, info))
    above = jnp.where(row_even, far_row, near)
    below = jnp.where(row_even, near, far_row)
    left, right = lax.optimization_barrier((coefficients[:, 0], coefficients[:, tile_y - 1]))
    left, right = cast_low(left), cast_low(right)
    sides = []
    for col, edge in ((0, left), (tile_y - 1, right)):
        sides.append(jnp.concatenate([above[col : col + 1], edge, below[col : col + 1]], axis=0))
    next_out, pair_out = lax.optimization_barrier(
        (jnp.where(even, sides[0], sides[1]), jnp.where(even, sides[1], sides[0]))
    )
    next_in, pair_in = along_wide(next_out, pair_out)
    x, grad, next_out, pair_out = call(
        functools.partial(first_kernel, sizes),
        "first_step",
        [info, row_ids, col_ids, coefficients.reshape(own, frames, width), near, far_row, next_in, pair_in, seen, *operator],
        3,
        step_outputs(False),
        [low_scratch, rlow_scratch, residual_scratch],
        work,
    )
    for iteration in range(ITERS):
        last = iteration == ITERS - 1
        next_in, pair_in = along_wide(next_out, pair_out)
        rows_sent = tile_y if last else 2 * span
        near, far_row = call(
            functools.partial(fold_kernel, sizes, last),
            "fold_columns",
            [info, grad, next_in, pair_in],
            1,
            [shape(rows_sent, jnp.bfloat16), shape(rows_sent, jnp.bfloat16)],
        )
        near, far_row = along_narrow(near, far_row)
        if last:
            inner = list(range(2, tile_x))
            outer = [1, tile_x]
            stay = pl.BlockSpec(memory_space=pltpu.HBM)
            inputs = [info, x, grad, next_in, pair_in]

            def final_call(rows, operands, aliases, name):
                specs = [smem] + [vmem] * (len(operands) - 1)
                if aliases:
                    specs[-1] = stay
                return pl.pallas_call(
                    functools.partial(final_kernel, sizes, rows),
                    out_shape=jax.ShapeDtypeStruct(coefficients.shape, jnp.float32),
                    in_specs=specs,
                    out_specs=stay,
                    scratch_shapes=[
                        pltpu.VMEM((len(rows), tile_y, frames, width), jnp.float32),
                        pltpu.SemaphoreType.DMA((len(rows),)),
                    ],
                    input_output_aliases=aliases,
                    compiler_params=pltpu.CompilerParams(vmem_limit_bytes=24 << 20),
                    cost_estimate=pl.CostEstimate(flops=work, bytes_accessed=1 << 20, transcendentals=0),
                    name=name,
                )(*operands)

            started = final_call(inner, inputs, {}, "inner_rows")
            updated = final_call(outer, inputs + [near, far_row, started], {7: 0}, "outer_rows")
        else:
            ending = iteration == ITERS - 2
            x, grad, next_out, pair_out, *rest = call(
                functools.partial(step_kernel, sizes, ending),
                "one_step",
                [info, row_ids, col_ids, x, grad, next_in, pair_in, near, far_row, seen, *operator],
                3,
                step_outputs(ending),
                [low_scratch, rlow_scratch] + ([] if ending else [residual_scratch]),
                work,
            )
    residual = rest[0]
    return (
        updated,
        residual[:own].reshape(coefficients.shape),
    )


def solution(mesh):
    placed = (
        P("narrow", "wide", None, None),
        P("narrow", "wide", None, None),
        P("narrow", "wide", None, None, None),
        P("narrow", "wide", None),
        P("narrow", "wide", None),
        P("narrow", "wide"),
    )
    return jax.shard_map(
        local,
        mesh=mesh,
        in_specs=placed,
        out_specs=(P("narrow", "wide", None, None), P("narrow", "wide", None, None)),
        check_vma=False,
    )
```

```python
import functools

import jax
import jax.numpy as jnp
from jax import lax
from jax.experimental import pallas as pl
from jax.experimental.pallas import tpu as pltpu
from jax.sharding import PartitionSpec as P

ITERS = 5
descent = 0.1

ROW_FIRST, ROW_LAST, COL_FIRST, COL_LAST, EVEN, ROW_EVEN, LIVE = range(7)


def cast_low(value):
    return value.astype(jnp.bfloat16)


def wide_value(value):
    return value.astype(jnp.float32)


def kept(value, drop):
    return jnp.where(drop, jnp.zeros_like(value), value)


def half_step(source_ref, parts, total_ref, source_ids, target_ids, live, filler=()):
    filler = list(filler)

    def add(first, blocks_ref):
        for at in range(0, blocks_ref.shape[0], 2):
            slot = first + at
            upper = source_ref[source_ids[slot]]
            lower = source_ref[source_ids[slot + 1]]
            frames, width = upper.shape
            zeros = jnp.zeros_like(upper)
            taken = jnp.concatenate(
                [jnp.concatenate([upper, zeros], axis=1), jnp.concatenate([zeros, lower], axis=1)],
                axis=0,
            )
            matrices = blocks_ref[pl.ds(at, 2)].reshape(2 * width, width)
            product = jnp.dot(taken, matrices, preferred_element_type=jnp.float32)
            target = target_ids[slot]
            total_ref[target] = total_ref[target] + product[:frames]
            target = target_ids[slot + 1]
            total_ref[target] = total_ref[target] + product[frames:]
            for work in filler[:2]:
                work()
            del filler[:2]

    first = 0
    for part in parts[:-1]:
        add(first, part)
        first += part.shape[0]
    for work in filler:
        work()
    filler.clear()

    @pl.when(live > first)
    def _():
        add(first, parts[-1])


def products(sizes, info_ref, rows_ref, cols_ref, observed_ref, blocks, turned, grad_ref, residual_ref, low_ref, rlow_ref):
    tile_x, tile_y, _ = sizes
    own = tile_x * tile_y
    extended = (tile_x + 2) * (tile_y + 2)
    low_ref[extended] = jnp.zeros_like(low_ref[extended])
    for block in range(own):
        residual_ref[block] = -observed_ref[block]
    residual_ref[own] = jnp.zeros_like(residual_ref[own])

    def clear(block):
        grad_ref[block] = jnp.zeros_like(grad_ref[block])

    clears = [functools.partial(clear, block) for block in range(extended + 1)]
    half_step(low_ref, blocks, residual_ref, cols_ref, rows_ref, info_ref[LIVE], clears)
    for block in range(own + 1):
        rlow_ref[block] = cast_low(residual_ref[block])
    half_step(rlow_ref, turned, grad_ref, rows_ref, cols_ref, info_ref[LIVE])


def send_columns(sizes, last, info_ref, grad_ref, pair_ref, next_ref):
    tile_x, tile_y, _ = sizes
    span = tile_y + 2
    even = info_ref[EVEN] == 1
    for out_ref, right in ((pair_ref, even), (next_ref, jnp.logical_not(even))):
        if last:
            col = jnp.where(right, span - 1, 0)
            for row in range(tile_x + 2):
                out_ref[row] = cast_low(grad_ref[row * span + col])
        else:
            col = jnp.where(right, span - 2, 0)
            for row in range(tile_x + 2):
                for step in range(2):
                    out_ref[row * 2 + step] = cast_low(grad_ref[row * span + col + step])


def send_rows(sizes, info_ref, grad_ref, near_ref, far_ref):
    tile_x, tile_y, _ = sizes
    span = tile_y + 2
    even = info_ref[ROW_EVEN] == 1
    for out_ref, lower in ((near_ref, even), (far_ref, jnp.logical_not(even))):
        row = jnp.where(lower, tile_x, 0)
        for step in range(2):
            for col in range(2, span - 2):
                out_ref[step * (span - 4) + col - 2] = cast_low(grad_ref[(row + step) * span + col])


def outside(sizes, info_ref, row, col):
    tile_x, tile_y, _ = sizes
    flag = None
    for hit, place in (
        (row == 0, ROW_FIRST),
        (row == tile_x + 1, ROW_LAST),
        (col == 0, COL_FIRST),
        (col == tile_y + 1, COL_LAST),
    ):
        if hit:
            here = info_ref[place] == 1
            flag = here if flag is None else jnp.logical_or(flag, here)
    return flag


def came_along_wide(sizes, last, info_ref, pair_in, next_in, row, col):
    tile_x, tile_y, _ = sizes
    even = info_ref[EVEN] == 1
    width = 1 if last else 2
    lefts = {1: 0} if last else {0: 0, 1: 1}
    rights = {tile_y: 0} if last else {tile_y: 0, tile_y + 1: 1}
    for places, from_pair, place in (
        (lefts, jnp.logical_not(even), COL_FIRST),
        (rights, even, COL_LAST),
    ):
        if col in places:
            at = row * width + places[col]
            came = jnp.where(from_pair, pair_in[at], next_in[at])
            return kept(wide_value(came), info_ref[place] == 1)
    return None


def bring(blocks_in, blocks_ref, arrived, chunk, first):
    size = blocks_ref.shape[0] // arrived.shape[0]
    return pltpu.make_async_copy(
        blocks_in.at[pl.ds(first + chunk * size, size)],
        blocks_ref.at[pl.ds(chunk * size, size)],
        arrived.at[chunk],
    )


def plan_kernel(sizes, flags_ref, live_ref, rows_in, cols_in, info_ref, rows_ref, cols_ref):
    tile_x, tile_y, slots = sizes
    live = live_ref[0, 0]
    for place in range(LIVE):
        info_ref[place] = flags_ref[place]
    info_ref[LIVE] = live
    group = 8

    def copy(step, carry):
        for place in range(group):
            slot = step * group + place
            used = slot < live
            rows_ref[slot] = jnp.where(used, rows_in[slot], tile_x * tile_y)
            cols_ref[slot] = jnp.where(used, cols_in[slot], (tile_x + 2) * (tile_y + 2))
        return carry

    lax.fori_loop(0, slots // group, copy, 0)


def turn_kernel(info_ref, blocks_in, blocks_0, blocks_1, turned_0, turned_1, arrived_0, arrived_1):
    half = blocks_0.shape[0]
    chunks = arrived_0.shape[0]
    size = half // chunks
    more = info_ref[LIVE] > half
    for chunk in range(chunks):
        bring(blocks_in, blocks_0, arrived_0, chunk, 0).start()

    @pl.when(more)
    def _():
        for chunk in range(chunks):
            bring(blocks_in, blocks_1, arrived_1, chunk, half).start()

    for chunk in range(chunks):
        bring(blocks_in, blocks_0, arrived_0, chunk, 0).wait()
        for slot in range(chunk * size, (chunk + 1) * size):
            turned_0[slot] = blocks_0[slot].T

    @pl.when(more)
    def _():
        for chunk in range(chunks):
            bring(blocks_in, blocks_1, arrived_1, chunk, half).wait()
            for slot in range(chunk * size, (chunk + 1) * size):
                turned_1[slot] = blocks_1[slot].T


def first_kernel(sizes, info_ref, rows_ref, cols_ref, coef_ref, near_in, far_in, next_in, pair_in, observed_ref, blocks_0, blocks_1, turned_0, turned_1, x_ref, grad_ref, next_ref, pair_ref, near_ref, far_ref, low_ref, rlow_ref, residual_ref):
    tile_x, tile_y, _ = sizes
    span = tile_y + 2
    even = info_ref[EVEN] == 1
    for row in range(tile_x + 2):
        for col in range(span):
            if col == 0:
                value = wide_value(jnp.where(even, next_in[row], pair_in[row]))
            elif col == tile_y + 1:
                value = wide_value(jnp.where(even, pair_in[row], next_in[row]))
            elif row == 0:
                value = came_along_narrow(info_ref, near_in, far_in, True, col - 1)
            elif row == tile_x + 1:
                value = came_along_narrow(info_ref, near_in, far_in, False, col - 1)
            else:
                value = coef_ref[(row - 1) * tile_y + col - 1]
            drop = outside(sizes, info_ref, row, col)
            if drop is not None:
                value = kept(value, drop)
            x_ref[row * span + col] = value
            low_ref[row * span + col] = cast_low(value)
    products(sizes, info_ref, rows_ref, cols_ref, observed_ref, (blocks_0, blocks_1), (turned_0, turned_1), grad_ref, residual_ref, low_ref, rlow_ref)
    send_columns(sizes, False, info_ref, grad_ref, pair_ref, next_ref)
    send_rows(sizes, info_ref, grad_ref, near_ref, far_ref)


def step_kernel(sizes, last, info_ref, rows_ref, cols_ref, x_in, grad_in, next_in, pair_in, near_in, far_in, near_ends, far_ends, observed_ref, blocks_0, blocks_1, turned_0, turned_1, x_ref, grad_ref, next_ref, pair_ref, *rest):
    tile_x, tile_y, _ = sizes
    span = tile_y + 2
    if last:
        residual_ref, low_ref, rlow_ref = rest
    else:
        near_ref, far_ref, low_ref, rlow_ref, residual_ref = rest
    for row in range(tile_x + 2):
        for col in range(span):
            at = row * span + col
            gradient = grad_in[at]
            came = came_along_wide(sizes, False, info_ref, pair_in, next_in, row, col)
            if came is not None:
                gradient = gradient + came
            if row < 2 or row >= tile_x:
                step = row if row < 2 else row - tile_x
                if 2 <= col < span - 2:
                    came = came_along_narrow(info_ref, near_in, far_in, row < 2, step * (span - 4) + col - 2)
                else:
                    end = col if col < 2 else col - span + 4
                    came = came_along_narrow(info_ref, near_ends, far_ends, row < 2, step * 4 + end)
                gradient = gradient + came
            value = x_in[at] - descent * gradient
            drop = outside(sizes, info_ref, row, col)
            if drop is not None:
                value = kept(value, drop)
            x_ref[at] = value
            low_ref[at] = cast_low(value)
    products(sizes, info_ref, rows_ref, cols_ref, observed_ref, (blocks_0, blocks_1), (turned_0, turned_1), grad_ref, residual_ref, low_ref, rlow_ref)
    send_columns(sizes, last, info_ref, grad_ref, pair_ref, next_ref)
    if not last:
        send_rows(sizes, info_ref, grad_ref, near_ref, far_ref)


def came_along_narrow(info_ref, near_in, far_in, upper, at):
    even = info_ref[ROW_EVEN] == 1
    from_near = jnp.logical_not(even) if upper else even
    came = jnp.where(from_near, near_in[at], far_in[at])
    return wide_value(kept(came, info_ref[ROW_FIRST if upper else ROW_LAST] == 1))


def fold_kernel(sizes, last, info_ref, grad_in, next_in, pair_in, near_ref, far_ref):
    tile_x, tile_y, _ = sizes
    span = tile_y + 2
    even = info_ref[ROW_EVEN] == 1

    def folded(row, col):
        value = grad_in[row * span + col]
        came = came_along_wide(sizes, last, info_ref, pair_in, next_in, row, col)
        return cast_low(value if came is None else value + came)

    for out_ref, lower in ((near_ref, even), (far_ref, jnp.logical_not(even))):
        if last:
            row = jnp.where(lower, tile_x + 1, 0)
            for col in range(1, tile_y + 1):
                out_ref[col - 1] = folded(row, col)
        else:
            row = jnp.where(lower, tile_x, 0)
            for step in range(2):
                for end, col in enumerate((0, 1, span - 2, span - 1)):
                    out_ref[step * 4 + end] = folded(row + step, col)


def final_kernel(sizes, rows, info_ref, x_in, grad_in, next_in, pair_in, *rest):
    tile_x, tile_y, _ = sizes
    span = tile_y + 2
    if len(rest) > 3:
        near_in, far_in, _, out_ref, part_ref, sent = rest
    else:
        out_ref, part_ref, sent = rest
    copies = []
    for place, row in enumerate(rows):
        for col in range(1, tile_y + 1):
            at = row * span + col
            gradient = grad_in[at]
            came = came_along_wide(sizes, True, info_ref, pair_in, next_in, row, col)
            if came is not None:
                gradient = gradient + came
            if row == 1:
                gradient = gradient + came_along_narrow(info_ref, near_in, far_in, True, col - 1)
            if row == tile_x:
                gradient = gradient + came_along_narrow(info_ref, near_in, far_in, False, col - 1)
            part_ref[place, col - 1] = x_in[at] - descent * gradient
        copies.append(pltpu.make_async_copy(part_ref.at[place], out_ref.at[row - 1], sent.at[place]))
        copies[-1].start()
    for copy in copies:
        copy.wait()


def local(coefficients, observed, blocks, block_rows, block_cols, live_count):
    tile_x, tile_y, frames, width = coefficients.shape
    slots = blocks.shape[2]
    own = tile_x * tile_y
    span = tile_y + 2
    extended = (tile_x + 2) * span
    sizes = (tile_x, tile_y, slots)
    narrow = lax.axis_size("narrow")
    wide = lax.axis_size("wide")
    a = lax.axis_index("narrow")
    b = lax.axis_index("wide")
    flags = jnp.stack([a == 0, a == narrow - 1, b == 0, b == wide - 1, b % 2 == 0, a % 2 == 0]).astype(jnp.int32)
    even = b % 2 == 0
    row_even = a % 2 == 0

    def everywhere(move):
        return [
            (i * narrow + j, to_i * narrow + to_j)
            for i in range(wide)
            for j in range(narrow)
            for to_i, to_j in [move(i, j)]
        ]

    def other(i, j):
        return (i, j ^ 1) if i in (0, wide - 1) else (((i - 1) ^ 1) + 1, j)

    def far(i, j):
        return (i ^ 1, j) if j in (0, narrow - 1) else (i, ((j - 1) ^ 1) + 1)

    near_pairs = everywhere(lambda i, j: (i, j ^ 1))
    far_pairs = everywhere(far)
    pairs = everywhere(lambda i, j: (i ^ 1, j))
    others = everywhere(other)

    def send(value, ring):
        return lax.ppermute(value, ("wide", "narrow"), ring)

    def along_narrow(near, far):
        return send(near, near_pairs), send(far, far_pairs)

    def along_wide(other, pair):
        return send(other, others), send(pair, pairs)

    seen = observed.reshape(own, frames, width)

    smem = pl.BlockSpec(memory_space=pltpu.SMEM)
    vmem = pl.BlockSpec(memory_space=pltpu.VMEM)

    def shape(count, kind):
        return jax.ShapeDtypeStruct((count, frames, width), kind)

    def place(output):
        return vmem if len(output.shape) > 1 else smem

    def call(kernel, name, inputs, scalars, outputs, scratch=(), flops=0):
        return pl.pallas_call(
            kernel,
            out_shape=outputs,
            in_specs=[smem] * scalars + [vmem] * (len(inputs) - scalars),
            out_specs=jax.tree.map(place, outputs),
            scratch_shapes=list(scratch),
            compiler_params=pltpu.CompilerParams(vmem_limit_bytes=24 << 20),
            cost_estimate=pl.CostEstimate(flops=flops, bytes_accessed=1 << 20, transcendentals=0),
            name=name,
        )(*inputs)

    low_scratch = pltpu.VMEM((extended + 1, frames, width), jnp.bfloat16)
    rlow_scratch = pltpu.VMEM((own + 1, frames, width), jnp.bfloat16)
    residual_scratch = pltpu.VMEM((own + 1, frames, width), jnp.float32)
    work = 4 * slots * frames * width * width

    def step_outputs(last):
        sent = tile_x + 2 if last else 2 * (tile_x + 2)
        outputs = [
            shape(extended, jnp.float32),
            shape(extended + 1, jnp.float32),
            shape(sent, jnp.bfloat16),
            shape(sent, jnp.bfloat16),
        ]
        if last:
            return outputs + [shape(own + 1, jnp.float32)]
        return outputs + [shape(2 * (span - 4), jnp.bfloat16)] * 2

    top, bottom = lax.optimization_barrier((coefficients[0], coefficients[tile_x - 1]))
    near, far_row = lax.optimization_barrier(
        (cast_low(jnp.where(row_even, bottom, top)), cast_low(jnp.where(row_even, top, bottom)))
    )
    near, far_row = along_narrow(near, far_row)
    in_hbm = pltpu.with_memory_space_constraint
    info, row_ids, col_ids = pl.pallas_call(
        functools.partial(plan_kernel, sizes),
        out_shape=[
            pltpu.SMEM((LIVE + 1,), jnp.int32),
            pltpu.SMEM((slots,), jnp.int32),
            pltpu.SMEM((slots,), jnp.int32),
        ],
        in_specs=[smem] * 4,
        out_specs=[smem] * 3,
        compiler_params=pltpu.CompilerParams(vmem_limit_bytes=24 << 20),
        cost_estimate=pl.CostEstimate(flops=work, bytes_accessed=1 << 20, transcendentals=0),
        name="plan_slots",
    )(
        flags,
        live_count,
        in_hbm(block_rows.reshape(slots), pltpu.HBM),
        in_hbm(block_cols.reshape(slots), pltpu.HBM),
    )
    chunks = 4
    half_shape = pltpu.VMEM((slots // 2, width, width), jnp.bfloat16)
    operator = pl.pallas_call(
        turn_kernel,
        out_shape=[half_shape] * 4,
        in_specs=[smem, pl.BlockSpec(memory_space=pltpu.HBM)],
        out_specs=[vmem] * 4,
        scratch_shapes=[pltpu.SemaphoreType.DMA((chunks,))] * 2,
        compiler_params=pltpu.CompilerParams(vmem_limit_bytes=24 << 20),
        cost_estimate=pl.CostEstimate(flops=work, bytes_accessed=4 << 20, transcendentals=0),
        name="turn_blocks",
    )(info, in_hbm(blocks.reshape(slots, width, width), pltpu.HBM))
    near, far_row, info = lax.optimization_barrier((near, far_row, info))
    above = jnp.where(row_even, far_row, near)
    below = jnp.where(row_even, near, far_row)
    left, right = lax.optimization_barrier((coefficients[:, 0], coefficients[:, tile_y - 1]))
    left, right = cast_low(left), cast_low(right)
    sides = []
    for col, edge in ((0, left), (tile_y - 1, right)):
        sides.append(jnp.concatenate([above[col : col + 1], edge, below[col : col + 1]], axis=0))
    next_out, pair_out = lax.optimization_barrier(
        (jnp.where(even, sides[0], sides[1]), jnp.where(even, sides[1], sides[0]))
    )
    next_in, pair_in = along_wide(next_out, pair_out)
    x, grad, next_out, pair_out, *rest = call(
        functools.partial(first_kernel, sizes),
        "first_step",
        [info, row_ids, col_ids, coefficients.reshape(own, frames, width), near, far_row, next_in, pair_in, seen, *operator],
        3,
        step_outputs(False),
        [low_scratch, rlow_scratch, residual_scratch],
        work,
    )
    for iteration in range(ITERS):
        last = iteration == ITERS - 1
        next_in, pair_in = along_wide(next_out, pair_out)
        if not last:
            near_in, far_in = along_narrow(*rest)
        rows_sent = tile_y if last else 8
        near, far_row = call(
            functools.partial(fold_kernel, sizes, last),
            "fold_columns",
            [info, grad, next_in, pair_in],
            1,
            [shape(rows_sent, jnp.bfloat16), shape(rows_sent, jnp.bfloat16)],
        )
        near, far_row = along_narrow(near, far_row)
        if last:
            inner = list(range(2, tile_x))
            outer = [1, tile_x]
            stay = pl.BlockSpec(memory_space=pltpu.HBM)
            inputs = [info, x, grad, next_in, pair_in]

            def final_call(rows, operands, aliases, name):
                specs = [smem] + [vmem] * (len(operands) - 1)
                if aliases:
                    specs[-1] = stay
                return pl.pallas_call(
                    functools.partial(final_kernel, sizes, rows),
                    out_shape=jax.ShapeDtypeStruct(coefficients.shape, jnp.float32),
                    in_specs=specs,
                    out_specs=stay,
                    scratch_shapes=[
                        pltpu.VMEM((len(rows), tile_y, frames, width), jnp.float32),
                        pltpu.SemaphoreType.DMA((len(rows),)),
                    ],
                    input_output_aliases=aliases,
                    compiler_params=pltpu.CompilerParams(vmem_limit_bytes=24 << 20),
                    cost_estimate=pl.CostEstimate(flops=work, bytes_accessed=1 << 20, transcendentals=0),
                    name=name,
                )(*operands)

            started = final_call(inner, inputs, {}, "inner_rows")
            updated = final_call(outer, inputs + [near, far_row, started], {7: 0}, "outer_rows")
        else:
            ending = iteration == ITERS - 2
            x, grad, next_out, pair_out, *rest = call(
                functools.partial(step_kernel, sizes, ending),
                "one_step",
                [info, row_ids, col_ids, x, grad, next_in, pair_in, near_in, far_in, near, far_row, seen, *operator],
                3,
                step_outputs(ending),
                [low_scratch, rlow_scratch] + ([] if ending else [residual_scratch]),
                work,
            )
    residual = rest[0]
    return (
        updated,
        residual[:own].reshape(coefficients.shape),
    )


def solution(mesh):
    placed = (
        P("narrow", "wide", None, None),
        P("narrow", "wide", None, None),
        P("narrow", "wide", None, None, None),
        P("narrow", "wide", None),
        P("narrow", "wide", None),
        P("narrow", "wide"),
    )
    return jax.shard_map(
        local,
        mesh=mesh,
        in_specs=placed,
        out_specs=(P("narrow", "wide", None, None), P("narrow", "wide", None, None)),
        check_vma=False,
    )
```

```python
import functools

import jax
import jax.numpy as jnp
from jax import lax
from jax.experimental import pallas as pl
from jax.experimental.pallas import tpu as pltpu
from jax.sharding import PartitionSpec as P

ITERS = 5
descent = 0.1

ROW_FIRST, ROW_LAST, COL_FIRST, COL_LAST, EVEN, ROW_EVEN, LIVE = range(7)


def cast_low(value):
    return value.astype(jnp.bfloat16)


def wide_value(value):
    return value.astype(jnp.float32)


def kept(value, drop):
    return jnp.where(drop, jnp.zeros_like(value), value)


def half_step(source_ref, parts, total_ref, source_ids, target_ids, live, filler=()):
    filler = list(filler)

    def add(first, blocks_ref):
        for at in range(0, blocks_ref.shape[0], 2):
            slot = first + at
            upper = source_ref[source_ids[slot]]
            lower = source_ref[source_ids[slot + 1]]
            frames, width = upper.shape
            zeros = jnp.zeros_like(upper)
            taken = jnp.concatenate(
                [jnp.concatenate([upper, zeros], axis=1), jnp.concatenate([zeros, lower], axis=1)],
                axis=0,
            )
            matrices = blocks_ref[pl.ds(at, 2)].reshape(2 * width, width)
            product = jnp.dot(taken, matrices, preferred_element_type=jnp.float32)
            target = target_ids[slot]
            total_ref[target] = total_ref[target] + product[:frames]
            target = target_ids[slot + 1]
            total_ref[target] = total_ref[target] + product[frames:]
            for work in filler[:2]:
                work()
            del filler[:2]

    first = 0
    for part in parts[:-1]:
        add(first, part)
        first += part.shape[0]
    for work in filler:
        work()
    filler.clear()

    @pl.when(live > first)
    def _():
        add(first, parts[-1])


def products(sizes, info_ref, rows_ref, cols_ref, observed_ref, blocks, turned, grad_ref, residual_ref, low_ref, rlow_ref):
    tile_x, tile_y, _ = sizes
    own = tile_x * tile_y
    extended = (tile_x + 2) * (tile_y + 2)
    low_ref[extended] = jnp.zeros_like(low_ref[extended])
    for block in range(own):
        residual_ref[block] = -observed_ref[block]
    residual_ref[own] = jnp.zeros_like(residual_ref[own])

    def clear(block):
        grad_ref[block] = jnp.zeros_like(grad_ref[block])

    clears = [functools.partial(clear, block) for block in range(extended + 1)]
    half_step(low_ref, blocks, residual_ref, cols_ref, rows_ref, info_ref[LIVE], clears)
    for block in range(own + 1):
        rlow_ref[block] = cast_low(residual_ref[block])
    half_step(rlow_ref, turned, grad_ref, rows_ref, cols_ref, info_ref[LIVE])


def send_columns(sizes, last, info_ref, grad_ref, pair_ref, next_ref):
    tile_x, tile_y, _ = sizes
    span = tile_y + 2
    even = info_ref[EVEN] == 1
    for out_ref, right in ((pair_ref, even), (next_ref, jnp.logical_not(even))):
        if last:
            col = jnp.where(right, span - 1, 0)
            for row in range(tile_x + 2):
                out_ref[row] = cast_low(grad_ref[row * span + col])
        else:
            col = jnp.where(right, span - 2, 0)
            for row in range(tile_x + 2):
                for step in range(2):
                    out_ref[row * 2 + step] = cast_low(grad_ref[row * span + col + step])


def outside(sizes, info_ref, row, col):
    tile_x, tile_y, _ = sizes
    flag = None
    for hit, place in (
        (row == 0, ROW_FIRST),
        (row == tile_x + 1, ROW_LAST),
        (col == 0, COL_FIRST),
        (col == tile_y + 1, COL_LAST),
    ):
        if hit:
            here = info_ref[place] == 1
            flag = here if flag is None else jnp.logical_or(flag, here)
    return flag


def came_along_wide(sizes, last, info_ref, pair_in, next_in, row, col):
    tile_x, tile_y, _ = sizes
    even = info_ref[EVEN] == 1
    width = 1 if last else 2
    lefts = {1: 0} if last else {0: 0, 1: 1}
    rights = {tile_y: 0} if last else {tile_y: 0, tile_y + 1: 1}
    for places, from_pair, place in (
        (lefts, jnp.logical_not(even), COL_FIRST),
        (rights, even, COL_LAST),
    ):
        if col in places:
            at = row * width + places[col]
            came = jnp.where(from_pair, pair_in[at], next_in[at])
            return kept(wide_value(came), info_ref[place] == 1)
    return None


def bring(blocks_in, blocks_ref, arrived, chunk, first):
    size = blocks_ref.shape[0] // arrived.shape[0]
    return pltpu.make_async_copy(
        blocks_in.at[pl.ds(first + chunk * size, size)],
        blocks_ref.at[pl.ds(chunk * size, size)],
        arrived.at[chunk],
    )


def plan_kernel(sizes, flags_ref, live_ref, rows_in, cols_in, info_ref, rows_ref, cols_ref):
    tile_x, tile_y, slots = sizes
    live = live_ref[0, 0]
    for place in range(LIVE):
        info_ref[place] = flags_ref[place]
    info_ref[LIVE] = live
    group = 8

    def copy(step, carry):
        for place in range(group):
            slot = step * group + place
            used = slot < live
            rows_ref[slot] = jnp.where(used, rows_in[slot], tile_x * tile_y)
            cols_ref[slot] = jnp.where(used, cols_in[slot], (tile_x + 2) * (tile_y + 2))
        return carry

    lax.fori_loop(0, slots // group, copy, 0)


def turn_kernel(info_ref, blocks_in, blocks_0, blocks_1, turned_0, turned_1, arrived_0, arrived_1):
    half = blocks_0.shape[0]
    chunks = arrived_0.shape[0]
    size = half // chunks
    more = info_ref[LIVE] > half
    for chunk in range(chunks):
        bring(blocks_in, blocks_0, arrived_0, chunk, 0).start()

    @pl.when(more)
    def _():
        for chunk in range(chunks):
            bring(blocks_in, blocks_1, arrived_1, chunk, half).start()

    for chunk in range(chunks):
        bring(blocks_in, blocks_0, arrived_0, chunk, 0).wait()
        for slot in range(chunk * size, (chunk + 1) * size):
            turned_0[slot] = blocks_0[slot].T

    @pl.when(more)
    def _():
        for chunk in range(chunks):
            bring(blocks_in, blocks_1, arrived_1, chunk, half).wait()
            for slot in range(chunk * size, (chunk + 1) * size):
                turned_1[slot] = blocks_1[slot].T


def first_kernel(sizes, info_ref, rows_ref, cols_ref, coef_ref, near_in, far_in, next_in, pair_in, observed_ref, blocks_0, blocks_1, turned_0, turned_1, x_ref, grad_ref, next_ref, pair_ref, low_ref, rlow_ref, residual_ref):
    tile_x, tile_y, _ = sizes
    span = tile_y + 2
    even = info_ref[EVEN] == 1
    for row in range(tile_x + 2):
        for col in range(span):
            if col == 0:
                value = wide_value(jnp.where(even, next_in[row], pair_in[row]))
            elif col == tile_y + 1:
                value = wide_value(jnp.where(even, pair_in[row], next_in[row]))
            elif row == 0:
                value = came_along_narrow(info_ref, near_in, far_in, True, col - 1)
            elif row == tile_x + 1:
                value = came_along_narrow(info_ref, near_in, far_in, False, col - 1)
            else:
                value = coef_ref[(row - 1) * tile_y + col - 1]
            drop = outside(sizes, info_ref, row, col)
            if drop is not None:
                value = kept(value, drop)
            x_ref[row * span + col] = value
            low_ref[row * span + col] = cast_low(value)
    products(sizes, info_ref, rows_ref, cols_ref, observed_ref, (blocks_0, blocks_1), (turned_0, turned_1), grad_ref, residual_ref, low_ref, rlow_ref)
    send_columns(sizes, False, info_ref, grad_ref, pair_ref, next_ref)


def step_kernel(sizes, last, info_ref, rows_ref, cols_ref, x_in, grad_in, next_in, pair_in, near_in, far_in, near_ends, far_ends, observed_ref, blocks_0, blocks_1, turned_0, turned_1, x_ref, grad_ref, next_ref, pair_ref, *rest):
    tile_x, tile_y, _ = sizes
    span = tile_y + 2
    even = info_ref[EVEN] == 1
    if last:
        residual_ref, low_ref, rlow_ref = rest
    else:
        low_ref, rlow_ref, residual_ref = rest
    for row in range(tile_x + 2):
        for col in range(span):
            at = row * span + col
            gradient = grad_in[at]
            came = came_along_wide(sizes, False, info_ref, pair_in, next_in, row, col)
            if came is not None:
                gradient = gradient + came
            if row < 2 or row >= tile_x:
                step = row if row < 2 else row - tile_x
                inner = step * (span - 2) + col
                if col < 2:
                    came = jnp.where(
                        even,
                        came_along_narrow(info_ref, near_ends, far_ends, row < 2, step * 2 + col),
                        came_along_narrow(info_ref, near_in, far_in, row < 2, inner),
                    )
                elif col >= span - 2:
                    end = step * 2 + col - span + 2
                    came = jnp.where(
                        even,
                        came_along_narrow(info_ref, near_in, far_in, row < 2, inner - 2),
                        came_along_narrow(info_ref, near_ends, far_ends, row < 2, end),
                    )
                else:
                    inner = jnp.where(even, inner - 2, inner)
                    came = came_along_narrow(info_ref, near_in, far_in, row < 2, inner)
                gradient = gradient + came
            value = x_in[at] - descent * gradient
            drop = outside(sizes, info_ref, row, col)
            if drop is not None:
                value = kept(value, drop)
            x_ref[at] = value
            low_ref[at] = cast_low(value)
    products(sizes, info_ref, rows_ref, cols_ref, observed_ref, (blocks_0, blocks_1), (turned_0, turned_1), grad_ref, residual_ref, low_ref, rlow_ref)
    send_columns(sizes, last, info_ref, grad_ref, pair_ref, next_ref)


def came_along_narrow(info_ref, near_in, far_in, upper, at):
    even = info_ref[ROW_EVEN] == 1
    from_near = jnp.logical_not(even) if upper else even
    came = jnp.where(from_near, near_in[at], far_in[at])
    return wide_value(kept(came, info_ref[ROW_FIRST if upper else ROW_LAST] == 1))


def shared_rows(sizes, info_ref, near_ref, far_ref):
    even = info_ref[ROW_EVEN] == 1
    lower = sizes[0]
    return ((near_ref, jnp.where(even, lower, 0)), (far_ref, jnp.where(even, 0, lower)))


def inner_kernel(sizes, info_ref, grad_in, pair_in, near_ref, far_ref):
    span = sizes[1] + 2
    even = info_ref[EVEN] == 1
    first = jnp.where(even, 2, 0)
    for out_ref, start in shared_rows(sizes, info_ref, near_ref, far_ref):
        for step in range(2):
            row = start + step
            for place in range(span - 2):
                value = grad_in[row * span + first + place]
                if place < 2:
                    value = value + wide_value(kept(pair_in[row * 2 + place], even))
                elif place >= span - 4:
                    came = pair_in[row * 2 + place - span + 4]
                    value = value + wide_value(kept(came, jnp.logical_not(even)))
                out_ref[step * (span - 2) + place] = cast_low(value)


def ends_kernel(sizes, info_ref, grad_in, next_in, near_ref, far_ref):
    span = sizes[1] + 2
    even = info_ref[EVEN] == 1
    first = jnp.where(even, 0, span - 2)
    nobody = jnp.where(even, info_ref[COL_FIRST], info_ref[COL_LAST]) == 1
    for out_ref, start in shared_rows(sizes, info_ref, near_ref, far_ref):
        for step in range(2):
            row = start + step
            for place in range(2):
                value = grad_in[row * span + first + place]
                value = value + wide_value(kept(next_in[row * 2 + place], nobody))
                out_ref[step * 2 + place] = cast_low(value)


def last_kernel(sizes, info_ref, grad_in, next_in, pair_in, near_ref, far_ref):
    tile_x, tile_y, _ = sizes
    span = tile_y + 2
    even = info_ref[ROW_EVEN] == 1
    for out_ref, lower in ((near_ref, even), (far_ref, jnp.logical_not(even))):
        row = jnp.where(lower, tile_x + 1, 0)
        for col in range(1, tile_y + 1):
            value = grad_in[row * span + col]
            came = came_along_wide(sizes, True, info_ref, pair_in, next_in, row, col)
            out_ref[col - 1] = cast_low(value if came is None else value + came)


def final_kernel(sizes, rows, info_ref, x_in, grad_in, next_in, pair_in, *rest):
    tile_x, tile_y, _ = sizes
    span = tile_y + 2
    if len(rest) > 3:
        near_in, far_in, _, out_ref, part_ref, sent = rest
    else:
        out_ref, part_ref, sent = rest
    copies = []
    for place, row in enumerate(rows):
        for col in range(1, tile_y + 1):
            at = row * span + col
            gradient = grad_in[at]
            came = came_along_wide(sizes, True, info_ref, pair_in, next_in, row, col)
            if came is not None:
                gradient = gradient + came
            if row == 1:
                gradient = gradient + came_along_narrow(info_ref, near_in, far_in, True, col - 1)
            if row == tile_x:
                gradient = gradient + came_along_narrow(info_ref, near_in, far_in, False, col - 1)
            part_ref[place, col - 1] = x_in[at] - descent * gradient
        copies.append(pltpu.make_async_copy(part_ref.at[place], out_ref.at[row - 1], sent.at[place]))
        copies[-1].start()
    for copy in copies:
        copy.wait()


def local(coefficients, observed, blocks, block_rows, block_cols, live_count):
    tile_x, tile_y, frames, width = coefficients.shape
    slots = blocks.shape[2]
    own = tile_x * tile_y
    span = tile_y + 2
    extended = (tile_x + 2) * span
    sizes = (tile_x, tile_y, slots)
    narrow = lax.axis_size("narrow")
    wide = lax.axis_size("wide")
    a = lax.axis_index("narrow")
    b = lax.axis_index("wide")
    flags = jnp.stack([a == 0, a == narrow - 1, b == 0, b == wide - 1, b % 2 == 0, a % 2 == 0]).astype(jnp.int32)
    even = b % 2 == 0
    row_even = a % 2 == 0

    def everywhere(move):
        return [
            (i * narrow + j, to_i * narrow + to_j)
            for i in range(wide)
            for j in range(narrow)
            for to_i, to_j in [move(i, j)]
        ]

    def other(i, j):
        return (i, j ^ 1) if i in (0, wide - 1) else (((i - 1) ^ 1) + 1, j)

    def far(i, j):
        return (i ^ 1, j) if j in (0, narrow - 1) else (i, ((j - 1) ^ 1) + 1)

    near_pairs = everywhere(lambda i, j: (i, j ^ 1))
    far_pairs = everywhere(far)
    pairs = everywhere(lambda i, j: (i ^ 1, j))
    others = everywhere(other)

    def send(value, ring):
        return lax.ppermute(value, ("wide", "narrow"), ring)

    def along_narrow(near, far):
        return send(near, near_pairs), send(far, far_pairs)

    def along_wide(other, pair):
        return send(other, others), send(pair, pairs)

    seen = observed.reshape(own, frames, width)

    smem = pl.BlockSpec(memory_space=pltpu.SMEM)
    vmem = pl.BlockSpec(memory_space=pltpu.VMEM)

    def shape(count, kind):
        return jax.ShapeDtypeStruct((count, frames, width), kind)

    def place(output):
        return vmem if len(output.shape) > 1 else smem

    def call(kernel, name, inputs, scalars, outputs, scratch=(), flops=0):
        return pl.pallas_call(
            kernel,
            out_shape=outputs,
            in_specs=[smem] * scalars + [vmem] * (len(inputs) - scalars),
            out_specs=jax.tree.map(place, outputs),
            scratch_shapes=list(scratch),
            compiler_params=pltpu.CompilerParams(vmem_limit_bytes=24 << 20),
            cost_estimate=pl.CostEstimate(flops=flops, bytes_accessed=1 << 20, transcendentals=0),
            name=name,
        )(*inputs)

    low_scratch = pltpu.VMEM((extended + 1, frames, width), jnp.bfloat16)
    rlow_scratch = pltpu.VMEM((own + 1, frames, width), jnp.bfloat16)
    residual_scratch = pltpu.VMEM((own + 1, frames, width), jnp.float32)
    work = 4 * slots * frames * width * width

    def step_outputs(last):
        sent = tile_x + 2 if last else 2 * (tile_x + 2)
        outputs = [
            shape(extended, jnp.float32),
            shape(extended + 1, jnp.float32),
            shape(sent, jnp.bfloat16),
            shape(sent, jnp.bfloat16),
        ]
        if last:
            return outputs + [shape(own + 1, jnp.float32)]
        return outputs

    top, bottom = lax.optimization_barrier((coefficients[0], coefficients[tile_x - 1]))
    near, far_row = lax.optimization_barrier(
        (cast_low(jnp.where(row_even, bottom, top)), cast_low(jnp.where(row_even, top, bottom)))
    )
    near, far_row = along_narrow(near, far_row)
    in_hbm = pltpu.with_memory_space_constraint
    info, row_ids, col_ids = pl.pallas_call(
        functools.partial(plan_kernel, sizes),
        out_shape=[
            pltpu.SMEM((LIVE + 1,), jnp.int32),
            pltpu.SMEM((slots,), jnp.int32),
            pltpu.SMEM((slots,), jnp.int32),
        ],
        in_specs=[smem] * 4,
        out_specs=[smem] * 3,
        compiler_params=pltpu.CompilerParams(vmem_limit_bytes=24 << 20),
        cost_estimate=pl.CostEstimate(flops=work, bytes_accessed=1 << 20, transcendentals=0),
        name="plan_slots",
    )(
        flags,
        live_count,
        in_hbm(block_rows.reshape(slots), pltpu.HBM),
        in_hbm(block_cols.reshape(slots), pltpu.HBM),
    )
    chunks = 4
    half_shape = pltpu.VMEM((slots // 2, width, width), jnp.bfloat16)
    operator = pl.pallas_call(
        turn_kernel,
        out_shape=[half_shape] * 4,
        in_specs=[smem, pl.BlockSpec(memory_space=pltpu.HBM)],
        out_specs=[vmem] * 4,
        scratch_shapes=[pltpu.SemaphoreType.DMA((chunks,))] * 2,
        compiler_params=pltpu.CompilerParams(vmem_limit_bytes=24 << 20),
        cost_estimate=pl.CostEstimate(flops=work, bytes_accessed=4 << 20, transcendentals=0),
        name="turn_blocks",
    )(info, in_hbm(blocks.reshape(slots, width, width), pltpu.HBM))
    near, far_row, info = lax.optimization_barrier((near, far_row, info))
    above = jnp.where(row_even, far_row, near)
    below = jnp.where(row_even, near, far_row)
    left, right = lax.optimization_barrier((coefficients[:, 0], coefficients[:, tile_y - 1]))
    left, right = cast_low(left), cast_low(right)
    sides = []
    for col, edge in ((0, left), (tile_y - 1, right)):
        sides.append(jnp.concatenate([above[col : col + 1], edge, below[col : col + 1]], axis=0))
    next_out, pair_out = lax.optimization_barrier(
        (jnp.where(even, sides[0], sides[1]), jnp.where(even, sides[1], sides[0]))
    )
    next_in, pair_in = along_wide(next_out, pair_out)
    x, grad, next_out, pair_out = call(
        functools.partial(first_kernel, sizes),
        "first_step",
        [info, row_ids, col_ids, coefficients.reshape(own, frames, width), near, far_row, next_in, pair_in, seen, *operator],
        3,
        step_outputs(False),
        [low_scratch, rlow_scratch, residual_scratch],
        work,
    )
    for iteration in range(ITERS):
        last = iteration == ITERS - 1
        next_in, pair_in = along_wide(next_out, pair_out)
        if last:
            folds = [(last_kernel, "rows_beyond", [next_in, pair_in], tile_y)]
        else:
            folds = [
                (inner_kernel, "inner_columns", [pair_in], 2 * (span - 2)),
                (ends_kernel, "end_columns", [next_in], 4),
            ]
        came = []
        for kernel, name, wide_in, count in folds:
            near, far_row = call(
                functools.partial(kernel, sizes),
                name,
                [info, grad, *wide_in],
                1,
                [shape(count, jnp.bfloat16)] * 2,
            )
            came += along_narrow(near, far_row)
        if last:
            inner = list(range(2, tile_x))
            outer = [1, tile_x]
            stay = pl.BlockSpec(memory_space=pltpu.HBM)
            inputs = [info, x, grad, next_in, pair_in]

            def final_call(rows, operands, aliases, name):
                specs = [smem] + [vmem] * (len(operands) - 1)
                if aliases:
                    specs[-1] = stay
                return pl.pallas_call(
                    functools.partial(final_kernel, sizes, rows),
                    out_shape=jax.ShapeDtypeStruct(coefficients.shape, jnp.float32),
                    in_specs=specs,
                    out_specs=stay,
                    scratch_shapes=[
                        pltpu.VMEM((len(rows), tile_y, frames, width), jnp.float32),
                        pltpu.SemaphoreType.DMA((len(rows),)),
                    ],
                    input_output_aliases=aliases,
                    compiler_params=pltpu.CompilerParams(vmem_limit_bytes=24 << 20),
                    cost_estimate=pl.CostEstimate(flops=work, bytes_accessed=1 << 20, transcendentals=0),
                    name=name,
                )(*operands)

            started = final_call(inner, inputs, {}, "inner_rows")
            updated = final_call(outer, inputs + [*came, started], {7: 0}, "outer_rows")
        else:
            ending = iteration == ITERS - 2
            x, grad, next_out, pair_out, *rest = call(
                functools.partial(step_kernel, sizes, ending),
                "one_step",
                [info, row_ids, col_ids, x, grad, next_in, pair_in, *came, seen, *operator],
                3,
                step_outputs(ending),
                [low_scratch, rlow_scratch] + ([] if ending else [residual_scratch]),
                work,
            )
    residual = rest[0]
    return (
        updated,
        residual[:own].reshape(coefficients.shape),
    )


def solution(mesh):
    placed = (
        P("narrow", "wide", None, None),
        P("narrow", "wide", None, None),
        P("narrow", "wide", None, None, None),
        P("narrow", "wide", None),
        P("narrow", "wide", None),
        P("narrow", "wide"),
    )
    return jax.shard_map(
        local,
        mesh=mesh,
        in_specs=placed,
        out_specs=(P("narrow", "wide", None, None), P("narrow", "wide", None, None)),
        check_vma=False,
    )
```

```python
import functools

import jax
import jax.numpy as jnp
from jax import lax
from jax.experimental import pallas as pl
from jax.experimental.pallas import tpu as pltpu
from jax.sharding import PartitionSpec as P

ITERS = 5
descent = 0.1

ROW_FIRST, ROW_LAST, COL_FIRST, COL_LAST, EVEN, ROW_EVEN, LIVE = range(7)


def cast_low(value):
    return value.astype(jnp.bfloat16)


def wide_value(value):
    return value.astype(jnp.float32)


def kept(value, drop):
    return jnp.where(drop, jnp.zeros_like(value), value)


def half_step(source_ref, parts, total_ref, source_ids, target_ids, live, filler=()):
    filler = list(filler)

    def add(first, blocks_ref):
        for at in range(0, blocks_ref.shape[0], 2):
            slot = first + at
            upper = source_ref[source_ids[slot]]
            lower = source_ref[source_ids[slot + 1]]
            frames, width = upper.shape
            zeros = jnp.zeros_like(upper)
            taken = jnp.concatenate(
                [jnp.concatenate([upper, zeros], axis=1), jnp.concatenate([zeros, lower], axis=1)],
                axis=0,
            )
            matrices = blocks_ref[pl.ds(at, 2)].reshape(2 * width, width)
            product = jnp.dot(taken, matrices, preferred_element_type=jnp.float32)
            target = target_ids[slot]
            total_ref[target] = total_ref[target] + product[:frames]
            target = target_ids[slot + 1]
            total_ref[target] = total_ref[target] + product[frames:]
            for work in filler[:2]:
                work()
            del filler[:2]

    first = 0
    for part in parts[:-1]:
        add(first, part)
        first += part.shape[0]
    for work in filler:
        work()
    filler.clear()

    @pl.when(live > first)
    def _():
        add(first, parts[-1])


def products(sizes, info_ref, rows_ref, cols_ref, observed_ref, blocks, turned, grad_ref, residual_ref, low_ref, rlow_ref):
    tile_x, tile_y, _ = sizes
    own = tile_x * tile_y
    extended = (tile_x + 2) * (tile_y + 2)
    low_ref[extended] = jnp.zeros_like(low_ref[extended])
    for block in range(own):
        residual_ref[block] = -observed_ref[block]
    residual_ref[own] = jnp.zeros_like(residual_ref[own])

    def clear(block):
        grad_ref[block] = jnp.zeros_like(grad_ref[block])

    clears = [functools.partial(clear, block) for block in range(extended + 1)]
    half_step(low_ref, blocks, residual_ref, cols_ref, rows_ref, info_ref[LIVE], clears)
    for block in range(own + 1):
        rlow_ref[block] = cast_low(residual_ref[block])
    half_step(rlow_ref, turned, grad_ref, rows_ref, cols_ref, info_ref[LIVE])


def send_columns(sizes, last, info_ref, grad_ref, pair_ref, next_ref):
    tile_x, tile_y, _ = sizes
    span = tile_y + 2
    even = info_ref[EVEN] == 1
    for out_ref, right in ((pair_ref, even), (next_ref, jnp.logical_not(even))):
        if last:
            col = jnp.where(right, span - 1, 0)
            for row in range(tile_x + 2):
                out_ref[row] = cast_low(grad_ref[row * span + col])
        else:
            col = jnp.where(right, span - 2, 0)
            for row in range(tile_x + 2):
                for step in range(2):
                    out_ref[row * 2 + step] = cast_low(grad_ref[row * span + col + step])


def outside(sizes, info_ref, row, col):
    tile_x, tile_y, _ = sizes
    flag = None
    for hit, place in (
        (row == 0, ROW_FIRST),
        (row == tile_x + 1, ROW_LAST),
        (col == 0, COL_FIRST),
        (col == tile_y + 1, COL_LAST),
    ):
        if hit:
            here = info_ref[place] == 1
            flag = here if flag is None else jnp.logical_or(flag, here)
    return flag


def came_along_wide(sizes, last, info_ref, pair_in, next_in, row, col):
    tile_x, tile_y, _ = sizes
    even = info_ref[EVEN] == 1
    width = 1 if last else 2
    lefts = {1: 0} if last else {0: 0, 1: 1}
    rights = {tile_y: 0} if last else {tile_y: 0, tile_y + 1: 1}
    for places, from_pair, place in (
        (lefts, jnp.logical_not(even), COL_FIRST),
        (rights, even, COL_LAST),
    ):
        if col in places:
            at = row * width + places[col]
            came = jnp.where(from_pair, pair_in[at], next_in[at])
            return kept(wide_value(came), info_ref[place] == 1)
    return None


def bring(blocks_in, blocks_ref, arrived, chunk, first):
    size = blocks_ref.shape[0] // arrived.shape[0]
    return pltpu.make_async_copy(
        blocks_in.at[pl.ds(first + chunk * size, size)],
        blocks_ref.at[pl.ds(chunk * size, size)],
        arrived.at[chunk],
    )


def plan_kernel(sizes, flags_ref, live_ref, rows_in, cols_in, info_ref, rows_ref, cols_ref):
    tile_x, tile_y, slots = sizes
    live = live_ref[0, 0]
    for place in range(LIVE):
        info_ref[place] = flags_ref[place]
    info_ref[LIVE] = live
    group = 8

    def copy(step, carry):
        for place in range(group):
            slot = step * group + place
            used = slot < live
            rows_ref[slot] = jnp.where(used, rows_in[slot], tile_x * tile_y)
            cols_ref[slot] = jnp.where(used, cols_in[slot], (tile_x + 2) * (tile_y + 2))
        return carry

    lax.fori_loop(0, slots // group, copy, 0)


def turn_kernel(info_ref, blocks_in, blocks_0, blocks_1, turned_0, turned_1, arrived_0, arrived_1):
    half = blocks_0.shape[0]
    chunks = arrived_0.shape[0]
    size = half // chunks
    more = info_ref[LIVE] > half
    for chunk in range(chunks):
        bring(blocks_in, blocks_0, arrived_0, chunk, 0).start()

    @pl.when(more)
    def _():
        for chunk in range(chunks):
            bring(blocks_in, blocks_1, arrived_1, chunk, half).start()

    for chunk in range(chunks):
        bring(blocks_in, blocks_0, arrived_0, chunk, 0).wait()
        for slot in range(chunk * size, (chunk + 1) * size):
            turned_0[slot] = blocks_0[slot].T

    @pl.when(more)
    def _():
        for chunk in range(chunks):
            bring(blocks_in, blocks_1, arrived_1, chunk, half).wait()
            for slot in range(chunk * size, (chunk + 1) * size):
                turned_1[slot] = blocks_1[slot].T


def first_kernel(sizes, info_ref, rows_ref, cols_ref, coef_ref, near_in, far_in, next_in, pair_in, observed_ref, blocks_0, blocks_1, turned_0, turned_1, x_ref, grad_ref, next_ref, pair_ref, low_ref, rlow_ref, residual_ref):
    tile_x, tile_y, _ = sizes
    span = tile_y + 2
    even = info_ref[EVEN] == 1
    for row in range(tile_x + 2):
        for col in range(span):
            if col == 0:
                value = wide_value(jnp.where(even, next_in[row], pair_in[row]))
            elif col == tile_y + 1:
                value = wide_value(jnp.where(even, pair_in[row], next_in[row]))
            elif row == 0:
                value = came_along_narrow(info_ref, near_in, far_in, True, col - 1)
            elif row == tile_x + 1:
                value = came_along_narrow(info_ref, near_in, far_in, False, col - 1)
            else:
                value = coef_ref[(row - 1) * tile_y + col - 1]
            drop = outside(sizes, info_ref, row, col)
            if drop is not None:
                value = kept(value, drop)
            x_ref[row * span + col] = value
            low_ref[row * span + col] = cast_low(value)
    products(sizes, info_ref, rows_ref, cols_ref, observed_ref, (blocks_0, blocks_1), (turned_0, turned_1), grad_ref, residual_ref, low_ref, rlow_ref)
    send_columns(sizes, False, info_ref, grad_ref, pair_ref, next_ref)


def step_kernel(sizes, last, info_ref, rows_ref, cols_ref, x_in, grad_in, next_in, pair_in, near_in, far_in, near_ends, far_ends, observed_ref, blocks_0, blocks_1, turned_0, turned_1, x_ref, grad_ref, next_ref, pair_ref, *rest):
    tile_x, tile_y, _ = sizes
    span = tile_y + 2
    even = info_ref[EVEN] == 1
    if last:
        residual_ref, low_ref, rlow_ref = rest
    else:
        low_ref, rlow_ref, residual_ref = rest
    for row in range(tile_x + 2):
        for col in range(span):
            at = row * span + col
            gradient = grad_in[at]
            came = came_along_wide(sizes, False, info_ref, pair_in, next_in, row, col)
            if came is not None:
                gradient = gradient + came
            if row < 2 or row >= tile_x:
                step = row if row < 2 else row - tile_x
                inner = step * (span - 2) + col
                if col < 2:
                    came = jnp.where(
                        even,
                        came_along_narrow(info_ref, near_ends, far_ends, row < 2, step * 2 + col),
                        came_along_narrow(info_ref, near_in, far_in, row < 2, inner),
                    )
                elif col >= span - 2:
                    end = step * 2 + col - span + 2
                    came = jnp.where(
                        even,
                        came_along_narrow(info_ref, near_in, far_in, row < 2, inner - 2),
                        came_along_narrow(info_ref, near_ends, far_ends, row < 2, end),
                    )
                else:
                    inner = jnp.where(even, inner - 2, inner)
                    came = came_along_narrow(info_ref, near_in, far_in, row < 2, inner)
                gradient = gradient + came
            value = x_in[at] - descent * gradient
            drop = outside(sizes, info_ref, row, col)
            if drop is not None:
                value = kept(value, drop)
            x_ref[at] = value
            low_ref[at] = cast_low(value)
    products(sizes, info_ref, rows_ref, cols_ref, observed_ref, (blocks_0, blocks_1), (turned_0, turned_1), grad_ref, residual_ref, low_ref, rlow_ref)
    send_columns(sizes, last, info_ref, grad_ref, pair_ref, next_ref)


def came_along_narrow(info_ref, near_in, far_in, upper, at):
    even = info_ref[ROW_EVEN] == 1
    from_near = jnp.logical_not(even) if upper else even
    came = jnp.where(from_near, near_in[at], far_in[at])
    return wide_value(kept(came, info_ref[ROW_FIRST if upper else ROW_LAST] == 1))


def shared_rows(sizes, info_ref, near_ref, far_ref):
    even = info_ref[ROW_EVEN] == 1
    lower = sizes[0]
    return ((near_ref, jnp.where(even, lower, 0)), (far_ref, jnp.where(even, 0, lower)))


def inner_kernel(sizes, info_ref, grad_in, pair_in, near_ref, far_ref):
    span = sizes[1] + 2
    even = info_ref[EVEN] == 1
    first = jnp.where(even, 2, 0)
    for out_ref, start in shared_rows(sizes, info_ref, near_ref, far_ref):
        for step in range(2):
            row = start + step
            for place in range(span - 2):
                value = grad_in[row * span + first + place]
                if place < 2:
                    value = value + wide_value(kept(pair_in[row * 2 + place], even))
                elif place >= span - 4:
                    came = pair_in[row * 2 + place - span + 4]
                    value = value + wide_value(kept(came, jnp.logical_not(even)))
                out_ref[step * (span - 2) + place] = cast_low(value)


def ends_kernel(sizes, info_ref, grad_in, next_in, near_ref, far_ref):
    span = sizes[1] + 2
    even = info_ref[EVEN] == 1
    first = jnp.where(even, 0, span - 2)
    nobody = jnp.where(even, info_ref[COL_FIRST], info_ref[COL_LAST]) == 1
    for out_ref, start in shared_rows(sizes, info_ref, near_ref, far_ref):
        for step in range(2):
            row = start + step
            for place in range(2):
                value = grad_in[row * span + first + place]
                value = value + wide_value(kept(next_in[row * 2 + place], nobody))
                out_ref[step * 2 + place] = cast_low(value)


def last_inner_kernel(sizes, info_ref, grad_in, pair_in, near_ref, far_ref):
    tile_x, tile_y, _ = sizes
    span = tile_y + 2
    even = info_ref[EVEN] == 1
    row_even = info_ref[ROW_EVEN] == 1
    first = jnp.where(even, 2, 1)
    for out_ref, lower in ((near_ref, row_even), (far_ref, jnp.logical_not(row_even))):
        row = jnp.where(lower, tile_x + 1, 0)
        came = wide_value(pair_in[row])
        for place in range(tile_y - 1):
            value = grad_in[row * span + first + place]
            if place == 0:
                value = value + kept(came, even)
            if place == tile_y - 2:
                value = value + kept(came, jnp.logical_not(even))
            out_ref[place] = cast_low(value)


def last_ends_kernel(sizes, info_ref, grad_in, next_in, near_ref, far_ref):
    tile_x, tile_y, _ = sizes
    span = tile_y + 2
    even = info_ref[EVEN] == 1
    row_even = info_ref[ROW_EVEN] == 1
    col = jnp.where(even, 1, tile_y)
    nobody = jnp.where(even, info_ref[COL_FIRST], info_ref[COL_LAST]) == 1
    for out_ref, lower in ((near_ref, row_even), (far_ref, jnp.logical_not(row_even))):
        row = jnp.where(lower, tile_x + 1, 0)
        came = wide_value(kept(next_in[row], nobody))
        out_ref[0] = cast_low(grad_in[row * span + col] + came)


def final_kernel(sizes, rows, info_ref, x_in, grad_in, next_in, pair_in, *rest):
    tile_x, tile_y, _ = sizes
    span = tile_y + 2
    if len(rest) > 3:
        near_in, far_in, near_end, far_end, _, out_ref, part_ref, sent = rest
    else:
        out_ref, part_ref, sent = rest
    even = info_ref[EVEN] == 1
    copies = []
    for place, row in enumerate(rows):
        for col in range(1, tile_y + 1):
            at = row * span + col
            gradient = grad_in[at]
            came = came_along_wide(sizes, True, info_ref, pair_in, next_in, row, col)
            if came is not None:
                gradient = gradient + came
            for edge in (1, tile_x):
                if row != edge:
                    continue
                upper = edge == 1
                inner = jnp.where(even, jnp.maximum(col - 2, 0), jnp.minimum(col - 1, tile_y - 2))
                came = came_along_narrow(info_ref, near_in, far_in, upper, inner)
                if col in (1, tile_y):
                    end = came_along_narrow(info_ref, near_end, far_end, upper, 0)
                    came = jnp.where(even if col == 1 else jnp.logical_not(even), end, came)
                gradient = gradient + came
            part_ref[place, col - 1] = x_in[at] - descent * gradient
        copies.append(pltpu.make_async_copy(part_ref.at[place], out_ref.at[row - 1], sent.at[place]))
        copies[-1].start()
    for copy in copies:
        copy.wait()


def local(coefficients, observed, blocks, block_rows, block_cols, live_count):
    tile_x, tile_y, frames, width = coefficients.shape
    slots = blocks.shape[2]
    own = tile_x * tile_y
    span = tile_y + 2
    extended = (tile_x + 2) * span
    sizes = (tile_x, tile_y, slots)
    narrow = lax.axis_size("narrow")
    wide = lax.axis_size("wide")
    a = lax.axis_index("narrow")
    b = lax.axis_index("wide")
    flags = jnp.stack([a == 0, a == narrow - 1, b == 0, b == wide - 1, b % 2 == 0, a % 2 == 0]).astype(jnp.int32)
    even = b % 2 == 0
    row_even = a % 2 == 0

    def everywhere(move):
        return [
            (i * narrow + j, to_i * narrow + to_j)
            for i in range(wide)
            for j in range(narrow)
            for to_i, to_j in [move(i, j)]
        ]

    def other(i, j):
        return (i, j ^ 1) if i in (0, wide - 1) else (((i - 1) ^ 1) + 1, j)

    def far(i, j):
        return (i ^ 1, j) if j in (0, narrow - 1) else (i, ((j - 1) ^ 1) + 1)

    near_pairs = everywhere(lambda i, j: (i, j ^ 1))
    far_pairs = everywhere(far)
    pairs = everywhere(lambda i, j: (i ^ 1, j))
    others = everywhere(other)

    def send(value, ring):
        return lax.ppermute(value, ("wide", "narrow"), ring)

    def along_narrow(near, far):
        return send(near, near_pairs), send(far, far_pairs)

    def along_wide(other, pair):
        return send(other, others), send(pair, pairs)

    seen = observed.reshape(own, frames, width)

    smem = pl.BlockSpec(memory_space=pltpu.SMEM)
    vmem = pl.BlockSpec(memory_space=pltpu.VMEM)

    def shape(count, kind):
        return jax.ShapeDtypeStruct((count, frames, width), kind)

    def place(output):
        return vmem if len(output.shape) > 1 else smem

    def call(kernel, name, inputs, scalars, outputs, scratch=(), flops=0):
        return pl.pallas_call(
            kernel,
            out_shape=outputs,
            in_specs=[smem] * scalars + [vmem] * (len(inputs) - scalars),
            out_specs=jax.tree.map(place, outputs),
            scratch_shapes=list(scratch),
            compiler_params=pltpu.CompilerParams(vmem_limit_bytes=24 << 20),
            cost_estimate=pl.CostEstimate(flops=flops, bytes_accessed=1 << 20, transcendentals=0),
            name=name,
        )(*inputs)

    low_scratch = pltpu.VMEM((extended + 1, frames, width), jnp.bfloat16)
    rlow_scratch = pltpu.VMEM((own + 1, frames, width), jnp.bfloat16)
    residual_scratch = pltpu.VMEM((own + 1, frames, width), jnp.float32)
    work = 4 * slots * frames * width * width

    def step_outputs(last):
        sent = tile_x + 2 if last else 2 * (tile_x + 2)
        outputs = [
            shape(extended, jnp.float32),
            shape(extended + 1, jnp.float32),
            shape(sent, jnp.bfloat16),
            shape(sent, jnp.bfloat16),
        ]
        if last:
            return outputs + [shape(own + 1, jnp.float32)]
        return outputs

    top, bottom = lax.optimization_barrier((coefficients[0], coefficients[tile_x - 1]))
    near, far_row = lax.optimization_barrier(
        (cast_low(jnp.where(row_even, bottom, top)), cast_low(jnp.where(row_even, top, bottom)))
    )
    near, far_row = along_narrow(near, far_row)
    in_hbm = pltpu.with_memory_space_constraint
    info, row_ids, col_ids = pl.pallas_call(
        functools.partial(plan_kernel, sizes),
        out_shape=[
            pltpu.SMEM((LIVE + 1,), jnp.int32),
            pltpu.SMEM((slots,), jnp.int32),
            pltpu.SMEM((slots,), jnp.int32),
        ],
        in_specs=[smem] * 4,
        out_specs=[smem] * 3,
        compiler_params=pltpu.CompilerParams(vmem_limit_bytes=24 << 20),
        cost_estimate=pl.CostEstimate(flops=work, bytes_accessed=1 << 20, transcendentals=0),
        name="plan_slots",
    )(
        flags,
        live_count,
        in_hbm(block_rows.reshape(slots), pltpu.HBM),
        in_hbm(block_cols.reshape(slots), pltpu.HBM),
    )
    chunks = 4
    half_shape = pltpu.VMEM((slots // 2, width, width), jnp.bfloat16)
    operator = pl.pallas_call(
        turn_kernel,
        out_shape=[half_shape] * 4,
        in_specs=[smem, pl.BlockSpec(memory_space=pltpu.HBM)],
        out_specs=[vmem] * 4,
        scratch_shapes=[pltpu.SemaphoreType.DMA((chunks,))] * 2,
        compiler_params=pltpu.CompilerParams(vmem_limit_bytes=24 << 20),
        cost_estimate=pl.CostEstimate(flops=work, bytes_accessed=4 << 20, transcendentals=0),
        name="turn_blocks",
    )(info, in_hbm(blocks.reshape(slots, width, width), pltpu.HBM))
    near, far_row, info = lax.optimization_barrier((near, far_row, info))
    above = jnp.where(row_even, far_row, near)
    below = jnp.where(row_even, near, far_row)
    left, right = lax.optimization_barrier((coefficients[:, 0], coefficients[:, tile_y - 1]))
    left, right = cast_low(left), cast_low(right)
    sides = []
    for col, edge in ((0, left), (tile_y - 1, right)):
        sides.append(jnp.concatenate([above[col : col + 1], edge, below[col : col + 1]], axis=0))
    next_out, pair_out = lax.optimization_barrier(
        (jnp.where(even, sides[0], sides[1]), jnp.where(even, sides[1], sides[0]))
    )
    next_in, pair_in = along_wide(next_out, pair_out)
    x, grad, next_out, pair_out = call(
        functools.partial(first_kernel, sizes),
        "first_step",
        [info, row_ids, col_ids, coefficients.reshape(own, frames, width), near, far_row, next_in, pair_in, seen, *operator],
        3,
        step_outputs(False),
        [low_scratch, rlow_scratch, residual_scratch],
        work,
    )
    for iteration in range(ITERS):
        last = iteration == ITERS - 1
        next_in, pair_in = along_wide(next_out, pair_out)
        if last:
            folds = [
                (last_inner_kernel, "inner_beyond", [pair_in], tile_y - 1),
                (last_ends_kernel, "end_beyond", [next_in], 1),
            ]
        else:
            folds = [
                (inner_kernel, "inner_columns", [pair_in], 2 * (span - 2)),
                (ends_kernel, "end_columns", [next_in], 4),
            ]
        came = []
        for kernel, name, wide_in, count in folds:
            near, far_row = call(
                functools.partial(kernel, sizes),
                name,
                [info, grad, *wide_in],
                1,
                [shape(count, jnp.bfloat16)] * 2,
            )
            came += along_narrow(near, far_row)
        if last:
            inner = list(range(2, tile_x))
            outer = [1, tile_x]
            stay = pl.BlockSpec(memory_space=pltpu.HBM)
            inputs = [info, x, grad, next_in, pair_in]

            def final_call(rows, operands, aliases, name):
                specs = [smem] + [vmem] * (len(operands) - 1)
                if aliases:
                    specs[-1] = stay
                return pl.pallas_call(
                    functools.partial(final_kernel, sizes, rows),
                    out_shape=jax.ShapeDtypeStruct(coefficients.shape, jnp.float32),
                    in_specs=specs,
                    out_specs=stay,
                    scratch_shapes=[
                        pltpu.VMEM((len(rows), tile_y, frames, width), jnp.float32),
                        pltpu.SemaphoreType.DMA((len(rows),)),
                    ],
                    input_output_aliases=aliases,
                    compiler_params=pltpu.CompilerParams(vmem_limit_bytes=24 << 20),
                    cost_estimate=pl.CostEstimate(flops=work, bytes_accessed=1 << 20, transcendentals=0),
                    name=name,
                )(*operands)

            started = final_call(inner, inputs, {}, "inner_rows")
            updated = final_call(outer, inputs + [*came, started], {9: 0}, "outer_rows")
        else:
            ending = iteration == ITERS - 2
            x, grad, next_out, pair_out, *rest = call(
                functools.partial(step_kernel, sizes, ending),
                "one_step",
                [info, row_ids, col_ids, x, grad, next_in, pair_in, *came, seen, *operator],
                3,
                step_outputs(ending),
                [low_scratch, rlow_scratch] + ([] if ending else [residual_scratch]),
                work,
            )
    residual = rest[0]
    return (
        updated,
        residual[:own].reshape(coefficients.shape),
    )


def solution(mesh):
    placed = (
        P("narrow", "wide", None, None),
        P("narrow", "wide", None, None),
        P("narrow", "wide", None, None, None),
        P("narrow", "wide", None),
        P("narrow", "wide", None),
        P("narrow", "wide"),
    )
    return jax.shard_map(
        local,
        mesh=mesh,
        in_specs=placed,
        out_specs=(P("narrow", "wide", None, None), P("narrow", "wide", None, None)),
        check_vma=False,
    )
```

```python
import functools

import jax
import jax.numpy as jnp
from jax import lax
from jax.experimental import pallas as pl
from jax.experimental.pallas import tpu as pltpu
from jax.sharding import PartitionSpec as P

ITERS = 5
descent = 0.1

ROW_FIRST, ROW_LAST, COL_FIRST, COL_LAST, EVEN, ROW_EVEN, LIVE = range(7)


def cast_low(value):
    return value.astype(jnp.bfloat16)


def wide_value(value):
    return value.astype(jnp.float32)


def kept(value, drop):
    return jnp.where(drop, jnp.zeros_like(value), value)


def half_step(source_ref, parts, total_ref, source_ids, target_ids, live, filler=()):
    filler = list(filler)

    def add(first, blocks_ref):
        for at in range(0, blocks_ref.shape[0], 2):
            slot = first + at
            upper = source_ref[source_ids[slot]]
            lower = source_ref[source_ids[slot + 1]]
            frames, width = upper.shape
            zeros = jnp.zeros_like(upper)
            taken = jnp.concatenate(
                [jnp.concatenate([upper, zeros], axis=1), jnp.concatenate([zeros, lower], axis=1)],
                axis=0,
            )
            matrices = blocks_ref[pl.ds(at, 2)].reshape(2 * width, width)
            product = jnp.dot(taken, matrices, preferred_element_type=jnp.float32)
            target = target_ids[slot]
            total_ref[target] = total_ref[target] + product[:frames]
            target = target_ids[slot + 1]
            total_ref[target] = total_ref[target] + product[frames:]
            for work in filler[:2]:
                work()
            del filler[:2]

    first = 0
    for part in parts[:-1]:
        add(first, part)
        first += part.shape[0]
    for work in filler:
        work()
    filler.clear()

    @pl.when(live > first)
    def _():
        add(first, parts[-1])


def products(sizes, info_ref, rows_ref, cols_ref, observed_ref, blocks, turned, grad_ref, residual_ref, low_ref, rlow_ref):
    tile_x, tile_y, _ = sizes
    own = tile_x * tile_y
    extended = (tile_x + 2) * (tile_y + 2)
    low_ref[extended] = jnp.zeros_like(low_ref[extended])
    for block in range(own):
        residual_ref[block] = -observed_ref[block]
    residual_ref[own] = jnp.zeros_like(residual_ref[own])

    def clear(block):
        grad_ref[block] = jnp.zeros_like(grad_ref[block])

    clears = [functools.partial(clear, block) for block in range(extended + 1)]
    half_step(low_ref, blocks, residual_ref, cols_ref, rows_ref, info_ref[LIVE], clears)
    for block in range(own + 1):
        rlow_ref[block] = cast_low(residual_ref[block])
    half_step(rlow_ref, turned, grad_ref, rows_ref, cols_ref, info_ref[LIVE])


def send_columns(sizes, last, info_ref, grad_ref, pair_ref, next_ref):
    tile_x, tile_y, _ = sizes
    span = tile_y + 2
    even = info_ref[EVEN] == 1
    for out_ref, right in ((pair_ref, even), (next_ref, jnp.logical_not(even))):
        if last:
            col = jnp.where(right, span - 1, 0)
            for row in range(tile_x + 2):
                out_ref[row] = cast_low(grad_ref[row * span + col])
        else:
            col = jnp.where(right, span - 2, 0)
            for row in range(tile_x + 2):
                for step in range(2):
                    out_ref[row * 2 + step] = cast_low(grad_ref[row * span + col + step])


def outside(sizes, info_ref, row, col):
    tile_x, tile_y, _ = sizes
    flag = None
    for hit, place in (
        (row == 0, ROW_FIRST),
        (row == tile_x + 1, ROW_LAST),
        (col == 0, COL_FIRST),
        (col == tile_y + 1, COL_LAST),
    ):
        if hit:
            here = info_ref[place] == 1
            flag = here if flag is None else jnp.logical_or(flag, here)
    return flag


def came_along_wide(sizes, last, info_ref, pair_in, next_in, row, col):
    tile_x, tile_y, _ = sizes
    even = info_ref[EVEN] == 1
    width = 1 if last else 2
    lefts = {1: 0} if last else {0: 0, 1: 1}
    rights = {tile_y: 0} if last else {tile_y: 0, tile_y + 1: 1}
    for places, from_pair, place in (
        (lefts, jnp.logical_not(even), COL_FIRST),
        (rights, even, COL_LAST),
    ):
        if col in places:
            at = row * width + places[col]
            came = jnp.where(from_pair, pair_in[at], next_in[at])
            return kept(wide_value(came), info_ref[place] == 1)
    return None


def bring(blocks_in, blocks_ref, arrived, chunk, first):
    size = blocks_ref.shape[0] // arrived.shape[0]
    return pltpu.make_async_copy(
        blocks_in.at[pl.ds(first + chunk * size, size)],
        blocks_ref.at[pl.ds(chunk * size, size)],
        arrived.at[chunk],
    )


def plan_kernel(sizes, flags_ref, live_ref, rows_in, cols_in, info_ref, rows_ref, cols_ref):
    tile_x, tile_y, slots = sizes
    live = live_ref[0, 0]
    for place in range(LIVE):
        info_ref[place] = flags_ref[place]
    info_ref[LIVE] = live
    group = 8

    def copy(step, carry):
        for place in range(group):
            slot = step * group + place
            used = slot < live
            rows_ref[slot] = jnp.where(used, rows_in[slot], tile_x * tile_y)
            cols_ref[slot] = jnp.where(used, cols_in[slot], (tile_x + 2) * (tile_y + 2))
        return carry

    lax.fori_loop(0, slots // group, copy, 0)


def turn_kernel(info_ref, blocks_in, blocks_0, blocks_1, turned_0, turned_1, arrived_0, arrived_1):
    half = blocks_0.shape[0]
    chunks = arrived_0.shape[0]
    size = half // chunks
    more = info_ref[LIVE] > half
    for chunk in range(chunks):
        bring(blocks_in, blocks_0, arrived_0, chunk, 0).start()

    @pl.when(more)
    def _():
        for chunk in range(chunks):
            bring(blocks_in, blocks_1, arrived_1, chunk, half).start()

    for chunk in range(chunks):
        bring(blocks_in, blocks_0, arrived_0, chunk, 0).wait()
        for slot in range(chunk * size, (chunk + 1) * size):
            turned_0[slot] = blocks_0[slot].T

    @pl.when(more)
    def _():
        for chunk in range(chunks):
            bring(blocks_in, blocks_1, arrived_1, chunk, half).wait()
            for slot in range(chunk * size, (chunk + 1) * size):
                turned_1[slot] = blocks_1[slot].T


def first_kernel(sizes, info_ref, rows_ref, cols_ref, coef_ref, near_in, far_in, next_in, pair_in, near_ends, far_ends, observed_ref, blocks_0, blocks_1, turned_0, turned_1, x_ref, grad_ref, next_ref, pair_ref, low_ref, rlow_ref, residual_ref):
    tile_x, tile_y, _ = sizes
    span = tile_y + 2
    even = info_ref[EVEN] == 1
    for row in range(tile_x + 2):
        for col in range(span):
            if col in (0, tile_y + 1):
                left = col == 0
                if row in (0, tile_x + 1):
                    value = came_along_narrow(info_ref, near_ends, far_ends, row == 0, 0 if left else 1)
                else:
                    from_next = even if left else jnp.logical_not(even)
                    value = wide_value(jnp.where(from_next, next_in[row - 1], pair_in[row - 1]))
            elif row == 0:
                value = came_along_narrow(info_ref, near_in, far_in, True, col - 1)
            elif row == tile_x + 1:
                value = came_along_narrow(info_ref, near_in, far_in, False, col - 1)
            else:
                value = coef_ref[(row - 1) * tile_y + col - 1]
            drop = outside(sizes, info_ref, row, col)
            if drop is not None:
                value = kept(value, drop)
            x_ref[row * span + col] = value
            low_ref[row * span + col] = cast_low(value)
    products(sizes, info_ref, rows_ref, cols_ref, observed_ref, (blocks_0, blocks_1), (turned_0, turned_1), grad_ref, residual_ref, low_ref, rlow_ref)
    send_columns(sizes, False, info_ref, grad_ref, pair_ref, next_ref)


def step_kernel(sizes, last, info_ref, rows_ref, cols_ref, x_in, grad_in, next_in, pair_in, near_in, far_in, near_ends, far_ends, observed_ref, blocks_0, blocks_1, turned_0, turned_1, x_ref, grad_ref, next_ref, pair_ref, *rest):
    tile_x, tile_y, _ = sizes
    span = tile_y + 2
    even = info_ref[EVEN] == 1
    if last:
        residual_ref, low_ref, rlow_ref = rest
    else:
        low_ref, rlow_ref, residual_ref = rest
    for row in range(tile_x + 2):
        for col in range(span):
            at = row * span + col
            gradient = grad_in[at]
            came = came_along_wide(sizes, False, info_ref, pair_in, next_in, row, col)
            if came is not None:
                gradient = gradient + came
            if row < 2 or row >= tile_x:
                step = row if row < 2 else row - tile_x
                inner = step * (span - 2) + col
                if col < 2:
                    came = jnp.where(
                        even,
                        came_along_narrow(info_ref, near_ends, far_ends, row < 2, step * 2 + col),
                        came_along_narrow(info_ref, near_in, far_in, row < 2, inner),
                    )
                elif col >= span - 2:
                    end = step * 2 + col - span + 2
                    came = jnp.where(
                        even,
                        came_along_narrow(info_ref, near_in, far_in, row < 2, inner - 2),
                        came_along_narrow(info_ref, near_ends, far_ends, row < 2, end),
                    )
                else:
                    inner = jnp.where(even, inner - 2, inner)
                    came = came_along_narrow(info_ref, near_in, far_in, row < 2, inner)
                gradient = gradient + came
            value = x_in[at] - descent * gradient
            drop = outside(sizes, info_ref, row, col)
            if drop is not None:
                value = kept(value, drop)
            x_ref[at] = value
            low_ref[at] = cast_low(value)
    products(sizes, info_ref, rows_ref, cols_ref, observed_ref, (blocks_0, blocks_1), (turned_0, turned_1), grad_ref, residual_ref, low_ref, rlow_ref)
    send_columns(sizes, last, info_ref, grad_ref, pair_ref, next_ref)


def came_along_narrow(info_ref, near_in, far_in, upper, at):
    even = info_ref[ROW_EVEN] == 1
    from_near = jnp.logical_not(even) if upper else even
    came = jnp.where(from_near, near_in[at], far_in[at])
    return wide_value(kept(came, info_ref[ROW_FIRST if upper else ROW_LAST] == 1))


def shared_rows(sizes, info_ref, near_ref, far_ref):
    even = info_ref[ROW_EVEN] == 1
    lower = sizes[0]
    return ((near_ref, jnp.where(even, lower, 0)), (far_ref, jnp.where(even, 0, lower)))


def inner_kernel(sizes, info_ref, grad_in, pair_in, near_ref, far_ref):
    span = sizes[1] + 2
    even = info_ref[EVEN] == 1
    first = jnp.where(even, 2, 0)
    for out_ref, start in shared_rows(sizes, info_ref, near_ref, far_ref):
        for step in range(2):
            row = start + step
            for place in range(span - 2):
                value = grad_in[row * span + first + place]
                if place < 2:
                    value = value + wide_value(kept(pair_in[row * 2 + place], even))
                elif place >= span - 4:
                    came = pair_in[row * 2 + place - span + 4]
                    value = value + wide_value(kept(came, jnp.logical_not(even)))
                out_ref[step * (span - 2) + place] = cast_low(value)


def ends_kernel(sizes, info_ref, grad_in, next_in, near_ref, far_ref):
    span = sizes[1] + 2
    even = info_ref[EVEN] == 1
    first = jnp.where(even, 0, span - 2)
    nobody = jnp.where(even, info_ref[COL_FIRST], info_ref[COL_LAST]) == 1
    for out_ref, start in shared_rows(sizes, info_ref, near_ref, far_ref):
        for step in range(2):
            row = start + step
            for place in range(2):
                value = grad_in[row * span + first + place]
                value = value + wide_value(kept(next_in[row * 2 + place], nobody))
                out_ref[step * 2 + place] = cast_low(value)


def last_inner_kernel(sizes, info_ref, grad_in, pair_in, near_ref, far_ref):
    tile_x, tile_y, _ = sizes
    span = tile_y + 2
    even = info_ref[EVEN] == 1
    row_even = info_ref[ROW_EVEN] == 1
    first = jnp.where(even, 2, 1)
    for out_ref, lower in ((near_ref, row_even), (far_ref, jnp.logical_not(row_even))):
        row = jnp.where(lower, tile_x + 1, 0)
        came = wide_value(pair_in[row])
        for place in range(tile_y - 1):
            value = grad_in[row * span + first + place]
            if place == 0:
                value = value + kept(came, even)
            if place == tile_y - 2:
                value = value + kept(came, jnp.logical_not(even))
            out_ref[place] = cast_low(value)


def last_ends_kernel(sizes, info_ref, grad_in, next_in, near_ref, far_ref):
    tile_x, tile_y, _ = sizes
    span = tile_y + 2
    even = info_ref[EVEN] == 1
    row_even = info_ref[ROW_EVEN] == 1
    col = jnp.where(even, 1, tile_y)
    nobody = jnp.where(even, info_ref[COL_FIRST], info_ref[COL_LAST]) == 1
    for out_ref, lower in ((near_ref, row_even), (far_ref, jnp.logical_not(row_even))):
        row = jnp.where(lower, tile_x + 1, 0)
        came = wide_value(kept(next_in[row], nobody))
        out_ref[0] = cast_low(grad_in[row * span + col] + came)


def final_kernel(sizes, rows, info_ref, x_in, grad_in, next_in, pair_in, *rest):
    tile_x, tile_y, _ = sizes
    span = tile_y + 2
    if len(rest) > 3:
        near_in, far_in, near_end, far_end, _, out_ref, part_ref, sent = rest
    else:
        out_ref, part_ref, sent = rest
    even = info_ref[EVEN] == 1
    copies = []
    for place, row in enumerate(rows):
        for col in range(1, tile_y + 1):
            at = row * span + col
            gradient = grad_in[at]
            came = came_along_wide(sizes, True, info_ref, pair_in, next_in, row, col)
            if came is not None:
                gradient = gradient + came
            for edge in (1, tile_x):
                if row != edge:
                    continue
                upper = edge == 1
                inner = jnp.where(even, jnp.maximum(col - 2, 0), jnp.minimum(col - 1, tile_y - 2))
                came = came_along_narrow(info_ref, near_in, far_in, upper, inner)
                if col in (1, tile_y):
                    end = came_along_narrow(info_ref, near_end, far_end, upper, 0)
                    came = jnp.where(even if col == 1 else jnp.logical_not(even), end, came)
                gradient = gradient + came
            part_ref[place, col - 1] = x_in[at] - descent * gradient
        copies.append(pltpu.make_async_copy(part_ref.at[place], out_ref.at[row - 1], sent.at[place]))
        copies[-1].start()
    for copy in copies:
        copy.wait()


def local(coefficients, observed, blocks, block_rows, block_cols, live_count):
    tile_x, tile_y, frames, width = coefficients.shape
    slots = blocks.shape[2]
    own = tile_x * tile_y
    span = tile_y + 2
    extended = (tile_x + 2) * span
    sizes = (tile_x, tile_y, slots)
    narrow = lax.axis_size("narrow")
    wide = lax.axis_size("wide")
    a = lax.axis_index("narrow")
    b = lax.axis_index("wide")
    flags = jnp.stack([a == 0, a == narrow - 1, b == 0, b == wide - 1, b % 2 == 0, a % 2 == 0]).astype(jnp.int32)
    even = b % 2 == 0
    row_even = a % 2 == 0

    def everywhere(move):
        return [
            (i * narrow + j, to_i * narrow + to_j)
            for i in range(wide)
            for j in range(narrow)
            for to_i, to_j in [move(i, j)]
        ]

    def other(i, j):
        return (i, j ^ 1) if i in (0, wide - 1) else (((i - 1) ^ 1) + 1, j)

    def far(i, j):
        return (i ^ 1, j) if j in (0, narrow - 1) else (i, ((j - 1) ^ 1) + 1)

    near_pairs = everywhere(lambda i, j: (i, j ^ 1))
    far_pairs = everywhere(far)
    pairs = everywhere(lambda i, j: (i ^ 1, j))
    others = everywhere(other)

    def send(value, ring):
        return lax.ppermute(value, ("wide", "narrow"), ring)

    def along_narrow(near, far):
        return send(near, near_pairs), send(far, far_pairs)

    def along_wide(other, pair):
        return send(other, others), send(pair, pairs)

    seen = observed.reshape(own, frames, width)

    smem = pl.BlockSpec(memory_space=pltpu.SMEM)
    vmem = pl.BlockSpec(memory_space=pltpu.VMEM)

    def shape(count, kind):
        return jax.ShapeDtypeStruct((count, frames, width), kind)

    def place(output):
        return vmem if len(output.shape) > 1 else smem

    def call(kernel, name, inputs, scalars, outputs, scratch=(), flops=0):
        return pl.pallas_call(
            kernel,
            out_shape=outputs,
            in_specs=[smem] * scalars + [vmem] * (len(inputs) - scalars),
            out_specs=jax.tree.map(place, outputs),
            scratch_shapes=list(scratch),
            compiler_params=pltpu.CompilerParams(vmem_limit_bytes=24 << 20),
            cost_estimate=pl.CostEstimate(flops=flops, bytes_accessed=1 << 20, transcendentals=0),
            name=name,
        )(*inputs)

    low_scratch = pltpu.VMEM((extended + 1, frames, width), jnp.bfloat16)
    rlow_scratch = pltpu.VMEM((own + 1, frames, width), jnp.bfloat16)
    residual_scratch = pltpu.VMEM((own + 1, frames, width), jnp.float32)
    work = 4 * slots * frames * width * width

    def step_outputs(last):
        sent = tile_x + 2 if last else 2 * (tile_x + 2)
        outputs = [
            shape(extended, jnp.float32),
            shape(extended + 1, jnp.float32),
            shape(sent, jnp.bfloat16),
            shape(sent, jnp.bfloat16),
        ]
        if last:
            return outputs + [shape(own + 1, jnp.float32)]
        return outputs

    top, bottom = lax.optimization_barrier((coefficients[0], coefficients[tile_x - 1]))
    near, far_row = lax.optimization_barrier(
        (cast_low(jnp.where(row_even, bottom, top)), cast_low(jnp.where(row_even, top, bottom)))
    )
    near, far_row = along_narrow(near, far_row)
    in_hbm = pltpu.with_memory_space_constraint
    info, row_ids, col_ids = pl.pallas_call(
        functools.partial(plan_kernel, sizes),
        out_shape=[
            pltpu.SMEM((LIVE + 1,), jnp.int32),
            pltpu.SMEM((slots,), jnp.int32),
            pltpu.SMEM((slots,), jnp.int32),
        ],
        in_specs=[smem] * 4,
        out_specs=[smem] * 3,
        compiler_params=pltpu.CompilerParams(vmem_limit_bytes=24 << 20),
        cost_estimate=pl.CostEstimate(flops=work, bytes_accessed=1 << 20, transcendentals=0),
        name="plan_slots",
    )(
        flags,
        live_count,
        in_hbm(block_rows.reshape(slots), pltpu.HBM),
        in_hbm(block_cols.reshape(slots), pltpu.HBM),
    )
    chunks = 4
    half_shape = pltpu.VMEM((slots // 2, width, width), jnp.bfloat16)
    operator = pl.pallas_call(
        turn_kernel,
        out_shape=[half_shape] * 4,
        in_specs=[smem, pl.BlockSpec(memory_space=pltpu.HBM)],
        out_specs=[vmem] * 4,
        scratch_shapes=[pltpu.SemaphoreType.DMA((chunks,))] * 2,
        compiler_params=pltpu.CompilerParams(vmem_limit_bytes=24 << 20),
        cost_estimate=pl.CostEstimate(flops=work, bytes_accessed=4 << 20, transcendentals=0),
        name="turn_blocks",
    )(info, in_hbm(blocks.reshape(slots, width, width), pltpu.HBM))
    left, right = lax.optimization_barrier((coefficients[:, 0], coefficients[:, tile_y - 1]))
    left, right = cast_low(left), cast_low(right)
    next_out, pair_out = lax.optimization_barrier(
        (jnp.where(even, left, right), jnp.where(even, right, left))
    )
    next_in, pair_in = along_wide(next_out, pair_out)
    next_in, pair_in, info = lax.optimization_barrier((next_in, pair_in, info))
    beside = (jnp.where(even, next_in, pair_in), jnp.where(even, pair_in, next_in))
    upper = jnp.stack([side[0] for side in beside])
    lower = jnp.stack([side[tile_x - 1] for side in beside])
    near_out, far_out = lax.optimization_barrier(
        (jnp.where(row_even, lower, upper), jnp.where(row_even, upper, lower))
    )
    ends = along_narrow(near_out, far_out)
    x, grad, next_out, pair_out = call(
        functools.partial(first_kernel, sizes),
        "first_step",
        [info, row_ids, col_ids, coefficients.reshape(own, frames, width), near, far_row, next_in, pair_in, *ends, seen, *operator],
        3,
        step_outputs(False),
        [low_scratch, rlow_scratch, residual_scratch],
        work,
    )
    for iteration in range(ITERS):
        last = iteration == ITERS - 1
        next_in, pair_in = along_wide(next_out, pair_out)
        if last:
            folds = [
                (last_inner_kernel, "inner_beyond", [pair_in], tile_y - 1),
                (last_ends_kernel, "end_beyond", [next_in], 1),
            ]
        else:
            folds = [
                (inner_kernel, "inner_columns", [pair_in], 2 * (span - 2)),
                (ends_kernel, "end_columns", [next_in], 4),
            ]
        came = []
        for kernel, name, wide_in, count in folds:
            near, far_row = call(
                functools.partial(kernel, sizes),
                name,
                [info, grad, *wide_in],
                1,
                [shape(count, jnp.bfloat16)] * 2,
            )
            came += along_narrow(near, far_row)
        if last:
            inner = list(range(2, tile_x))
            outer = [1, tile_x]
            stay = pl.BlockSpec(memory_space=pltpu.HBM)
            inputs = [info, x, grad, next_in, pair_in]

            def final_call(rows, operands, aliases, name):
                specs = [smem] + [vmem] * (len(operands) - 1)
                if aliases:
                    specs[-1] = stay
                return pl.pallas_call(
                    functools.partial(final_kernel, sizes, rows),
                    out_shape=jax.ShapeDtypeStruct(coefficients.shape, jnp.float32),
                    in_specs=specs,
                    out_specs=stay,
                    scratch_shapes=[
                        pltpu.VMEM((len(rows), tile_y, frames, width), jnp.float32),
                        pltpu.SemaphoreType.DMA((len(rows),)),
                    ],
                    input_output_aliases=aliases,
                    compiler_params=pltpu.CompilerParams(vmem_limit_bytes=24 << 20),
                    cost_estimate=pl.CostEstimate(flops=work, bytes_accessed=1 << 20, transcendentals=0),
                    name=name,
                )(*operands)

            started = final_call(inner, inputs, {}, "inner_rows")
            updated = final_call(outer, inputs + [*came, started], {9: 0}, "outer_rows")
        else:
            ending = iteration == ITERS - 2
            x, grad, next_out, pair_out, *rest = call(
                functools.partial(step_kernel, sizes, ending),
                "one_step",
                [info, row_ids, col_ids, x, grad, next_in, pair_in, *came, seen, *operator],
                3,
                step_outputs(ending),
                [low_scratch, rlow_scratch] + ([] if ending else [residual_scratch]),
                work,
            )
    residual = rest[0]
    return (
        updated,
        residual[:own].reshape(coefficients.shape),
    )


def solution(mesh):
    placed = (
        P("narrow", "wide", None, None),
        P("narrow", "wide", None, None),
        P("narrow", "wide", None, None, None),
        P("narrow", "wide", None),
        P("narrow", "wide", None),
        P("narrow", "wide"),
    )
    return jax.shard_map(
        local,
        mesh=mesh,
        in_specs=placed,
        out_specs=(P("narrow", "wide", None, None), P("narrow", "wide", None, None)),
        check_vma=False,
    )
```
